256 devices in a mesh: dp: 8 (over x, core), ts: 32 (over z, y).
Axes of the slice: x: 4, y: 4, z: 8, core: 2. Of those that a mesh axis runs over, the one named last changes fastest.
Arguments:
- block_activity: bfloat16 [8, 2048, 3584], P('dp', 'ts'), may hold values from -6 to 6
- result_cotangent: bfloat16 [8, 2048, 3584], P('dp', 'ts'), may hold values from -6 to 6
- kept_locations: int32 [8, 256], P('dp'), may hold values from 0 to 2047, as said below
- prenormal_scaling: bfloat16 [3584], replicated, may hold values from 0.5 to 1.5
- scorer_matrix: bfloat16 [3584], replicated, may hold values from -0.09375 to 0.09375
- switch_matrix: bfloat16 [3584, 14336], P(None, 'ts'), may hold values from -0.09375 to 0.09375
- expand_matrix: bfloat16 [3584, 14336], P(None, 'ts'), may hold values from -0.09375 to 0.09375
- contract_matrix: bfloat16 [14336, 3584], P('ts'), may hold values from -0.046875 to 0.046875
Outputs:
- token_grad: bfloat16 [8, 2048, 3584], P('dp', 'ts')
- gate_grad: bfloat16 [3584, 14336], P('dp', 'ts')
- up_grad: bfloat16 [3584, 14336], P('dp', 'ts')
- down_grad: bfloat16 [14336, 3584], P('ts', 'dp')
The draws below stay inside these ranges and needn't reach their ends.
Inputs may be any that keep to these rules, and one draw needn't show every extreme that they name: `kept_locations`: for each sequence, 256 distinct positions in increasing order; each aligned block of 64 positions holds at most 32 of them, and in every sequence one block holds exactly 32.
All inputs are finite; a program needn't handle non-finite values.
Results may differ from the reference program's by a relative error of at most 0.023.
Values may be sent and summed in bfloat16 or wider, within the bound.
A program may use at most 128 MiB of HBM per device.

```python
import math
import jax
import jax.numpy as jnp
from jax import lax

D = 3584
FF = 14336
TOK_DEV = 64
SEQ = 2048
CAP = 256
N_DP = 8
N_TS = 32


def draw_kept_locations(key, part):
    key = jax.random.fold_in(key, 7)
    share_base = TOK_DEV // 8
    rest_half = (N_TS - 4) // 2

    def one_sequence(seq_index):
        seq_key = jax.random.fold_in(key, seq_index)
        order_key, amount_key, pick_key = jax.random.split(seq_key, 3)
        shard_order = jax.random.permutation(order_key, N_TS)
        shift_amount = jax.random.randint(amount_key, (rest_half,), 0, share_base + 1)
        counts = jnp.full((N_TS,), share_base, jnp.int32)
        counts = counts.at[shard_order[0]].set(4 * share_base)
        counts = counts.at[shard_order[1:4]].set(0)
        counts = counts.at[shard_order[4:4 + rest_half]].add(shift_amount)
        counts = counts.at[shard_order[4 + rest_half:]].add(-shift_amount)
        rank_table = jax.vmap(lambda sub_key: jax.random.permutation(sub_key, TOK_DEV))(jax.random.split(pick_key, N_TS))
        chosen = (rank_table < counts[:, None]).reshape(-1).astype(jnp.int32)
        return jnp.argsort(1 - chosen, stable=True)[:CAP].astype(jnp.int32)
    return jax.vmap(one_sequence)(jnp.arange(N_DP))


def levels(own_key, dims, shards, low, top_value):
    def one(axis_at, shards_of):
        steps = jax.random.uniform(jax.random.fold_in(jax.random.fold_in(own_key, 6), axis_at), (shards_of,), jnp.float32, low / len(shards), top_value / len(shards))
        return jnp.repeat(jnp.exp(steps), dims[axis_at] // shards_of).reshape((-1,) + (1,) * (len(dims) - axis_at - 1))

    level = one(*shards[0])
    for cut in shards[1:]:
        level = level * one(*cut)
    return level


def centred(stream_key, dims, width, most, pieces=(), dtype=jnp.bfloat16):
    level = levels(stream_key, dims, pieces, -0.22, 0.18) if pieces else 1.0
    entries = jax.random.normal(stream_key, dims, jnp.float32) * width * level
    return jnp.minimum(jnp.maximum(entries, -most), most).astype(dtype)


def setup_inputs(seed: int = 0) -> dict:
    key_list = jax.random.split(jax.random.key(seed), 9)
    return {
        "block_activity": centred(key_list[0], (N_DP, SEQ, D), 1.0, 6.0, ((0, 8), (1, 32))),
        "result_cotangent": centred(key_list[1], (N_DP, SEQ, D), 1.0, 6.0, ((0, 8), (1, 32))),
        "kept_locations": draw_kept_locations(jax.random.fold_in(key_list[8], 71), 0),
        "prenormal_scaling": jnp.clip(1.0 + 0.1 * jax.random.normal(key_list[3], (D,), jnp.float32), 0.5, 1.5).astype(jnp.bfloat16),
        "scorer_matrix": centred(key_list[4], (D,), D ** -0.5, 0.09375),
        "switch_matrix": centred(key_list[5], (D, FF), D ** -0.5, 0.09375, ((1, 32),)),
        "expand_matrix": centred(key_list[6], (D, FF), D ** -0.5, 0.09375, ((1, 32),)),
        "contract_matrix": centred(key_list[7], (FF, D), FF ** -0.5, 0.046875, ((0, 32),)),
    }


epsilon = 1e-06
gelu_scale = math.sqrt(2.0 / math.pi)

def gelu_pair(pre_act):
    cubic = pre_act + 0.044715 * pre_act * pre_act * pre_act
    tanh_part = jnp.tanh(gelu_scale * cubic)
    gelu_out = 0.5 * pre_act * (1.0 + tanh_part)
    slope_out = 0.5 * (1.0 + tanh_part) + 0.5 * pre_act * (1.0 - tanh_part * tanh_part) * gelu_scale * (1.0 + 3.0 * 0.044715 * pre_act * pre_act)
    return (gelu_out, slope_out)

def round_trip(values):
    return lax.optimization_barrier(values.astype(jnp.bfloat16)).astype(jnp.float32)

def reference(block_activity, result_cotangent, kept_locations, prenormal_scaling, scorer_matrix, switch_matrix, expand_matrix, contract_matrix):
    factor = (N_DP * CAP) ** (-0.5)
    slice_width = FF // N_TS
    gain_f = prenormal_scaling.astype(jnp.float32)
    router_f = scorer_matrix.astype(jnp.float32)
    token_parts = []
    gate_total = jnp.zeros((D, FF), jnp.float32)
    up_total = jnp.zeros((D, FF), jnp.float32)
    down_total = jnp.zeros((FF, D), jnp.float32)
    for batch_slot_number in range(N_DP):
        kept_entries = kept_locations[batch_slot_number]
        row_data = jnp.take(block_activity[batch_slot_number], kept_entries, axis=0)
        grad_data = jnp.take(result_cotangent[batch_slot_number], kept_entries, axis=0)
        row_f = row_data.astype(jnp.float32)
        inv_rms = lax.rsqrt(lax.optimization_barrier(jnp.mean(row_f * row_f, axis=1, keepdims=True)) + epsilon)
        unit_rows = row_f * inv_rms
        normed = (unit_rows * gain_f).astype(jnp.bfloat16)
        weight = jax.nn.sigmoid(jnp.dot(row_data, scorer_matrix, preferred_element_type=jnp.float32))
        pre_gate = jnp.dot(normed, switch_matrix, preferred_element_type=jnp.float32)
        pre_up = jnp.dot(normed, expand_matrix, preferred_element_type=jnp.float32)
        gelu_out, slope_out = gelu_pair(pre_gate)
        hidden = (gelu_out * pre_up).astype(jnp.bfloat16)
        scaled = (weight[:, None] * grad_data.astype(jnp.float32)).astype(jnp.bfloat16)
        hidden_grad = jnp.dot(scaled, contract_matrix.T, preferred_element_type=jnp.float32)
        gate_in = (hidden_grad * pre_up * slope_out).astype(jnp.bfloat16)
        up_in = (hidden_grad * gelu_out).astype(jnp.bfloat16)
        block_sums = lax.optimization_barrier(jnp.sum((hidden.astype(jnp.float32) * hidden_grad).reshape(CAP, N_TS, slice_width), axis=2))
        logit_grad = (1.0 - weight) * lax.optimization_barrier(jnp.sum(round_trip(block_sums), axis=1))

        def add_slice(block_index, running):
            offset = (block_index * slice_width).astype(jnp.int32)
            gate_part = lax.dynamic_slice_in_dim(gate_in, offset, slice_width, 1)
            up_part = lax.dynamic_slice_in_dim(up_in, offset, slice_width, 1)
            gate_cols = lax.dynamic_slice_in_dim(switch_matrix, offset, slice_width, 1)
            up_cols = lax.dynamic_slice_in_dim(expand_matrix, offset, slice_width, 1)
            slice_term = jnp.dot(gate_part, gate_cols.T, preferred_element_type=jnp.float32)
            slice_term = slice_term + jnp.dot(up_part, up_cols.T, preferred_element_type=jnp.float32)
            return running + round_trip(slice_term)
        normed_grad = lax.fori_loop(0, N_TS, add_slice, jnp.zeros((CAP, D), jnp.float32))
        gained = normed_grad * gain_f
        row_grad = inv_rms * (gained - unit_rows * lax.optimization_barrier(jnp.mean(gained * unit_rows, axis=1, keepdims=True))) + logit_grad[:, None] * router_f
        token_parts.append(jnp.zeros((SEQ, D), jnp.float32).at[kept_entries].set(row_grad).astype(jnp.bfloat16))
        gate_total = gate_total + round_trip(factor * jnp.dot(normed.T, gate_in, preferred_element_type=jnp.float32))
        up_total = up_total + round_trip(factor * jnp.dot(normed.T, up_in, preferred_element_type=jnp.float32))
        down_total = down_total + round_trip(factor * jnp.dot(hidden.T, scaled, preferred_element_type=jnp.float32))
    return (jnp.stack(token_parts), gate_total.astype(jnp.bfloat16), up_total.astype(jnp.bfloat16), down_total.astype(jnp.bfloat16))
```

```python
import functools
import math

import jax
import jax.numpy as jnp
from jax import lax
from jax.experimental import pallas as pl
from jax.experimental.pallas import tpu as pltpu
from jax.sharding import PartitionSpec as P

MESH = pl.DeviceIdType.MESH
NY = 4
Z_STEPS = (0, -1, 1, -2, 2, -3, 3, 4)


def gather_kernel(n_ts, block, kept_ref, slots_ref, full_ref, landed, wide, p1_send, p1_recv, send_sem, recv_sem):
    nz = n_ts // NY
    me = lax.axis_index("ts")
    z, y = me // NY, lax.rem(me, NY)
    rows, width = full_ref.shape[2], full_ref.shape[3]
    lanes = wide.shape[2]
    half = width // 2

    def node(dz, dy):
        return lax.rem(z + dz + nz, nz) * NY + lax.rem(y + dy + NY, NY)

    barrier = pltpu.get_barrier_semaphore()

    @pl.loop(1, n_ts)
    def _(step):
        pl.semaphore_signal(barrier, inc=1, device_id={"ts": lax.rem(me + step, n_ts)}, device_id_type=MESH)

    pl.semaphore_wait(barrier, n_ts - 1)

    @pl.loop(1, n_ts)
    def _(step):
        to = lax.rem(me + step, n_ts)
        pltpu.make_async_remote_copy(
            slots_ref.at[to], landed.at[me], p1_send.at[step], p1_recv.at[step],
            device_id={"ts": to}, device_id_type=MESH,
        ).start()

    landed[me] = slots_ref[me]

    @pl.loop(1, n_ts)
    def _(step):
        to = lax.rem(me + step, n_ts)
        source = lax.rem(me - step + n_ts, n_ts)
        pltpu.make_async_remote_copy(
            slots_ref.at[to], landed.at[source], p1_send.at[step], p1_recv.at[step],
            device_id={"ts": to}, device_id_type=MESH,
        ).wait()

    for k in range(rows):
        holder = kept_ref[0, n_ts * k + me] // block
        wide[k] = landed[holder].astype(jnp.float32)
    tiles = width // lanes
    for part in range(2):
        for t in range(tiles):
            full_ref[part, me, :, t * lanes:(t + 1) * lanes] = wide[:, part * tiles + t, :].astype(jnp.bfloat16)

    pending = []

    def send(index, ref, to):
        copy = pltpu.make_async_remote_copy(
            ref, ref, send_sem.at[index], recv_sem.at[index], device_id={"ts": to}, device_id_type=MESH)
        copy.start()
        pending.append(copy)

    def arrive(index, ref):
        pltpu.make_async_remote_copy(
            ref, ref, send_sem.at[index], recv_sem.at[index], device_id={"ts": me}, device_id_type=MESH).wait_recv()

    def piece(part, n):
        return full_ref.at[part, n]

    def piece_half(part, n, which):
        return full_ref.at[part, n, :, pl.ds(which * half, half)]

    def group(dz):
        return full_ref.at[1, pl.ds(lax.rem(z + dz + nz, nz) * NY, NY)]

    def group_half(dz, which):
        return full_ref.at[1, pl.ds(lax.rem(z + dz + nz, nz) * NY + which * (NY // 2), NY // 2)]

    up, down, left, right = node(1, 0), node(-1, 0), node(0, -1), node(0, 1)
    B1, A1, B2, A2, A3 = 0, 4, 12, 20, 36

    send(B1 + 0, piece(1, me), right)
    send(B1 + 1, piece(1, me), left)
    send(A1 + 0, piece(0, me), up)
    send(A1 + 1, piece(0, me), down)

    def spread(j):
        dz = Z_STEPS[j]
        send(A2 + 2 * j, piece(0, node(dz, 0)), right)
        send(A2 + 2 * j + 1, piece(0, node(dz, 0)), left)

    def relay(j):
        dz = Z_STEPS[j]
        arrive(A2 + 2 * j, piece(0, node(dz, -1)))
        send(A3 + 2 * j, piece_half(0, node(dz, -1), 0), right)
        arrive(A2 + 2 * j + 1, piece(0, node(dz, 1)))
        send(A3 + 2 * j + 1, piece_half(0, node(dz, 1), 1), left)

    def along(s):
        if s < 4:
            arrive(A1 + 2 * (s - 1), piece(0, node(-s, 0)))
            if s < 3:
                send(A1 + 2 * s, piece(0, node(-s, 0)), up)
            else:
                send(A1 + 6, piece_half(0, node(-3, 0), 0), up)
            arrive(A1 + 2 * (s - 1) + 1, piece(0, node(s, 0)))
            if s < 3:
                send(A1 + 2 * s + 1, piece(0, node(s, 0)), down)
            else:
                send(A1 + 7, piece_half(0, node(3, 0), 1), down)
            spread(2 * s - 1)
            spread(2 * s)
        else:
            arrive(A1 + 6, piece_half(0, node(-4, 0), 0))
            arrive(A1 + 7, piece_half(0, node(4, 0), 1))
            spread(7)

    def groups(s):
        if s < 4:
            arrive(B2 + 2 * (s - 1), group(-s))
            if s < 3:
                send(B2 + 2 * s, group(-s), up)
            else:
                send(B2 + 6, group_half(-3, 0), up)
            arrive(B2 + 2 * (s - 1) + 1, group(s))
            if s < 3:
                send(B2 + 2 * s + 1, group(s), down)
            else:
                send(B2 + 7, group_half(3, 1), down)
        else:
            arrive(B2 + 6, group_half(-4, 0))
            arrive(B2 + 7, group_half(4, 1))

    spread(0)
    arrive(B1 + 0, piece(1, node(0, -1)))
    send(B1 + 2, piece_half(1, node(0, -1), 0), right)
    arrive(B1 + 1, piece(1, node(0, 1)))
    send(B1 + 3, piece_half(1, node(0, 1), 1), left)
    along(1)
    arrive(B1 + 2, piece_half(1, node(0, -2), 0))
    arrive(B1 + 3, piece_half(1, node(0, 2), 1))
    send(B2 + 0, group(0), up)
    send(B2 + 1, group(0), down)
    along(2)
    relay(0)
    along(3)
    relay(1)
    relay(2)
    groups(1)
    along(4)
    relay(3)
    relay(4)
    groups(2)
    relay(5)
    relay(6)
    relay(7)
    groups(3)
    for j in range(8):
        arrive(A3 + 2 * j, piece_half(0, node(Z_STEPS[j], -2), 0))
        arrive(A3 + 2 * j + 1, piece_half(0, node(Z_STEPS[j], 2), 1))
    groups(4)
    for copy in pending:
        copy.wait_send()


def gather_rows(kept, slots, n_ts, block):
    tiles = slots.shape[1] // 2
    width = tiles * slots.shape[2]
    rows = kept.shape[1] // n_ts
    return pl.pallas_call(
        functools.partial(gather_kernel, n_ts, block),
        out_shape=jax.ShapeDtypeStruct((2, n_ts, rows, width), jnp.bfloat16),
        in_specs=[pl.BlockSpec(memory_space=pltpu.SMEM), pl.BlockSpec(memory_space=pltpu.VMEM)],
        out_specs=pl.BlockSpec(memory_space=pltpu.VMEM),
        scratch_shapes=[
            pltpu.VMEM(slots.shape, jnp.bfloat16),
            pltpu.VMEM((rows,) + slots.shape[1:], jnp.float32),
            pltpu.SemaphoreType.DMA((n_ts,)),
            pltpu.SemaphoreType.DMA((n_ts,)),
            pltpu.SemaphoreType.DMA((52,)),
            pltpu.SemaphoreType.DMA((52,)),
        ],
        compiler_params=pltpu.CompilerParams(
            collective_id=0, has_side_effects=True, vmem_limit_bytes=24 * 1024 * 1024),
        name="gather_rows",
    )(kept, slots)


def reduce_weights(parts):
    return lax.psum_scatter(parts, "dp", scatter_dimension=0, tiled=True)


epsilon = 1e-06
gelu_scale = math.sqrt(2.0 / math.pi)


def gelu_pair(pre_act):
    cubic = pre_act + 0.044715 * pre_act * pre_act * pre_act
    tanh_part = jnp.tanh(gelu_scale * cubic)
    gelu_out = 0.5 * pre_act * (1.0 + tanh_part)
    slope_out = 0.5 * (1.0 + tanh_part) + 0.5 * pre_act * (
        1.0 - tanh_part * tanh_part
    ) * gelu_scale * (1.0 + 3.0 * 0.044715 * pre_act * pre_act)
    return (gelu_out, slope_out)


def norm_backward(row_data, summed_grad, summed_dot, prenormal_scaling, scorer_matrix):
    row_f = row_data.astype(jnp.float32)
    inv_rms = lax.rsqrt(jnp.mean(row_f * row_f, axis=1, keepdims=True) + epsilon)
    unit_rows = row_f * inv_rms
    weight = jax.nn.sigmoid(jnp.dot(row_data, scorer_matrix, preferred_element_type=jnp.float32))
    logit_grad = (1.0 - weight) * summed_dot
    gained = summed_grad * prenormal_scaling.astype(jnp.float32)
    row_grad = inv_rms * (gained - unit_rows * jnp.mean(gained * unit_rows, axis=1, keepdims=True))
    return row_grad + logit_grad[:, None] * scorer_matrix.astype(jnp.float32)


def local(
    block_activity, result_cotangent, kept_locations, prenormal_scaling, scorer_matrix,
    switch_matrix, expand_matrix, contract_matrix,
):
    n_ts = lax.axis_size("ts")
    me = lax.axis_index("ts")
    n_dp = lax.axis_size("dp")
    local_tokens = block_activity.shape[1]
    model_width = block_activity.shape[2]
    cap = kept_locations.shape[1]
    hidden_width = switch_matrix.shape[1]
    factor = (n_dp * cap) ** (-0.5)
    kept = kept_locations[0]
    first = jnp.sum((kept < me * local_tokens).astype(jnp.int32))
    count = jnp.sum((kept // local_tokens == me).astype(jnp.int32))
    classes = jnp.arange(n_ts, dtype=jnp.int32)
    ranks = first + lax.rem(classes - lax.rem(first, n_ts) + n_ts, n_ts)
    own_valid = ranks < first + count
    own_index = jnp.clip(jnp.take(kept, jnp.minimum(ranks, cap - 1)) - me * local_tokens, 0, local_tokens - 1)
    own_rows = jnp.take(block_activity[0], own_index, axis=0)
    own_grads = jnp.take(result_cotangent[0], own_index, axis=0)
    slots = jnp.concatenate([own_rows, own_grads], axis=1).reshape(n_ts, -1, 128)
    full = gather_rows(kept_locations, slots, n_ts, local_tokens)
    row_data = full[0].reshape(cap, model_width)
    grad_data = full[1].reshape(cap, model_width)

    row_f = row_data.astype(jnp.float32)
    inv_rms = lax.rsqrt(jnp.mean(row_f * row_f, axis=1, keepdims=True) + epsilon)
    normed = (row_f * inv_rms * prenormal_scaling.astype(jnp.float32)).astype(jnp.bfloat16)
    weight = jax.nn.sigmoid(jnp.dot(row_data, scorer_matrix, preferred_element_type=jnp.float32))
    pre_gate = jnp.dot(normed, switch_matrix, preferred_element_type=jnp.float32)
    pre_up = jnp.dot(normed, expand_matrix, preferred_element_type=jnp.float32)
    gelu_out, slope_out = gelu_pair(pre_gate)
    hidden = (gelu_out * pre_up).astype(jnp.bfloat16)
    scaled = (weight[:, None] * grad_data.astype(jnp.float32)).astype(jnp.bfloat16)
    hidden_grad = jnp.einsum("cd,fd->cf", scaled, contract_matrix, preferred_element_type=jnp.float32)
    gate_in = (hidden_grad * pre_up * slope_out).astype(jnp.bfloat16)
    up_in = (hidden_grad * gelu_out).astype(jnp.bfloat16)
    dot_part = jnp.sum(hidden.astype(jnp.float32) * hidden_grad, axis=1)
    normed_term = jnp.einsum("cf,df->cd", gate_in, switch_matrix, preferred_element_type=jnp.float32)
    normed_term = normed_term + jnp.einsum("cf,df->cd", up_in, expand_matrix, preferred_element_type=jnp.float32)
    term = jnp.concatenate(
        [normed_term, jnp.broadcast_to(dot_part[:, None], (cap, 128))], axis=1).astype(jnp.bfloat16)
    own_sum = lax.psum_scatter(term, "ts", scatter_dimension=0, tiled=True)
    gate_term = jnp.einsum("cd,cf->df", normed, gate_in, preferred_element_type=jnp.float32)
    up_term = jnp.einsum("cd,cf->df", normed, up_in, preferred_element_type=jnp.float32)
    down_term = jnp.einsum("cd,cf->df", scaled, hidden, preferred_element_type=jnp.float32)
    parts = (factor * jnp.concatenate([gate_term, up_term, down_term], axis=1)).astype(jnp.bfloat16)
    summed_weights = reduce_weights(parts)
    gate_grad = summed_weights[:, :hidden_width]
    up_grad = summed_weights[:, hidden_width : 2 * hidden_width]
    down_grad = summed_weights[:, 2 * hidden_width :].T

    class_holder = jnp.take(kept.reshape(-1, n_ts), me, axis=1) // local_tokens
    pick = jnp.argmax(class_holder[None, :] == classes[:, None], axis=1)
    back = lax.all_to_all(jnp.take(own_sum, pick, axis=0), "ts", split_axis=0, concat_axis=0, tiled=True)
    own_term = back[:, :model_width].astype(jnp.float32)
    own_dot = back[:, model_width].astype(jnp.float32)
    row_grad = norm_backward(own_rows, own_term, own_dot, prenormal_scaling, scorer_matrix)
    row_grad = jnp.where(own_valid[:, None], row_grad, 0.0).astype(jnp.bfloat16)
    place = (jnp.arange(local_tokens)[:, None] == own_index[None, :]) & own_valid[None, :]
    token_grad = jnp.dot(place.astype(jnp.bfloat16), row_grad, preferred_element_type=jnp.float32)
    return (token_grad.astype(jnp.bfloat16)[None], gate_grad, up_grad, down_grad)


def solution(mesh):
    in_specs = (
        P("dp", "ts", None), P("dp", "ts", None), P("dp", None), P(), P(),
        P(None, "ts"), P(None, "ts"), P("ts", None),
    )
    out_specs = (P("dp", "ts", None), P("dp", "ts"), P("dp", "ts"), P("ts", "dp"))
    return jax.shard_map(local, mesh=mesh, in_specs=in_specs, out_specs=out_specs, check_vma=False)
```

```python
import functools
import math

import jax
import jax.numpy as jnp
from jax import lax
from jax.experimental import pallas as pl
from jax.experimental.pallas import tpu as pltpu
from jax.sharding import PartitionSpec as P

MESH = pl.DeviceIdType.MESH
NY = 4
Z_STEPS = (0, -1, 1, -2, 2, -3, 3, 4)


def gather_kernel(n_ts, block, kept_ref, slots_ref, full_ref, landed, wide, p1_send, p1_recv, send_sem, recv_sem):
    nz = n_ts // NY
    me = lax.axis_index("ts")
    z, y = me // NY, lax.rem(me, NY)
    rows, width = full_ref.shape[2], full_ref.shape[3]
    lanes = wide.shape[2]
    half = width // 2

    def node(dz, dy):
        return lax.rem(z + dz + nz, nz) * NY + lax.rem(y + dy + NY, NY)

    barrier = pltpu.get_barrier_semaphore()

    @pl.loop(1, n_ts)
    def _(step):
        pl.semaphore_signal(barrier, inc=1, device_id={"ts": lax.rem(me + step, n_ts)}, device_id_type=MESH)

    pl.semaphore_wait(barrier, n_ts - 1)

    @pl.loop(1, n_ts)
    def _(step):
        to = lax.rem(me + step, n_ts)
        pltpu.make_async_remote_copy(
            slots_ref.at[to], landed.at[me], p1_send.at[step], p1_recv.at[step],
            device_id={"ts": to}, device_id_type=MESH,
        ).start()

    landed[me] = slots_ref[me]

    @pl.loop(1, n_ts)
    def _(step):
        to = lax.rem(me + step, n_ts)
        source = lax.rem(me - step + n_ts, n_ts)
        pltpu.make_async_remote_copy(
            slots_ref.at[to], landed.at[source], p1_send.at[step], p1_recv.at[step],
            device_id={"ts": to}, device_id_type=MESH,
        ).wait()

    for k in range(rows):
        holder = kept_ref[0, n_ts * k + me] // block
        wide[k] = landed[holder].astype(jnp.float32)
    tiles = width // lanes
    for part in range(2):
        for t in range(tiles):
            full_ref[part, me, :, t * lanes:(t + 1) * lanes] = wide[:, part * tiles + t, :].astype(jnp.bfloat16)

    pending = []

    def send(index, ref, to):
        copy = pltpu.make_async_remote_copy(
            ref, ref, send_sem.at[index], recv_sem.at[index], device_id={"ts": to}, device_id_type=MESH)
        copy.start()
        pending.append(copy)

    def arrive(index, ref):
        pltpu.make_async_remote_copy(
            ref, ref, send_sem.at[index], recv_sem.at[index], device_id={"ts": me}, device_id_type=MESH).wait_recv()

    def piece(part, n):
        return full_ref.at[part, n]

    def piece_half(part, n, which):
        return full_ref.at[part, n, :, pl.ds(which * half, half)]

    def group(dz):
        return full_ref.at[1, pl.ds(lax.rem(z + dz + nz, nz) * NY, NY)]

    def group_half(dz, which):
        return full_ref.at[1, pl.ds(lax.rem(z + dz + nz, nz) * NY + which * (NY // 2), NY // 2)]

    up, down, left, right = node(1, 0), node(-1, 0), node(0, -1), node(0, 1)
    B1, A1, B2, A2, A3 = 0, 4, 12, 20, 36

    send(B1 + 0, piece(1, me), right)
    send(B1 + 1, piece(1, me), left)
    send(A1 + 0, piece(0, me), up)
    send(A1 + 1, piece(0, me), down)

    def spread(j):
        dz = Z_STEPS[j]
        send(A2 + 2 * j, piece(0, node(dz, 0)), right)
        send(A2 + 2 * j + 1, piece(0, node(dz, 0)), left)

    def relay(j):
        dz = Z_STEPS[j]
        arrive(A2 + 2 * j, piece(0, node(dz, -1)))
        send(A3 + 2 * j, piece_half(0, node(dz, -1), 0), right)
        arrive(A2 + 2 * j + 1, piece(0, node(dz, 1)))
        send(A3 + 2 * j + 1, piece_half(0, node(dz, 1), 1), left)

    def along(s):
        if s < 4:
            arrive(A1 + 2 * (s - 1), piece(0, node(-s, 0)))
            if s < 3:
                send(A1 + 2 * s, piece(0, node(-s, 0)), up)
            else:
                send(A1 + 6, piece_half(0, node(-3, 0), 0), up)
            arrive(A1 + 2 * (s - 1) + 1, piece(0, node(s, 0)))
            if s < 3:
                send(A1 + 2 * s + 1, piece(0, node(s, 0)), down)
            else:
                send(A1 + 7, piece_half(0, node(3, 0), 1), down)
            spread(2 * s - 1)
            spread(2 * s)
        else:
            arrive(A1 + 6, piece_half(0, node(-4, 0), 0))
            arrive(A1 + 7, piece_half(0, node(4, 0), 1))
            spread(7)

    def groups(s):
        if s < 4:
            arrive(B2 + 2 * (s - 1), group(-s))
            if s < 3:
                send(B2 + 2 * s, group(-s), up)
            else:
                send(B2 + 6, group_half(-3, 0), up)
            arrive(B2 + 2 * (s - 1) + 1, group(s))
            if s < 3:
                send(B2 + 2 * s + 1, group(s), down)
            else:
                send(B2 + 7, group_half(3, 1), down)
        else:
            arrive(B2 + 6, group_half(-4, 0))
            arrive(B2 + 7, group_half(4, 1))

    spread(0)
    arrive(B1 + 0, piece(1, node(0, -1)))
    send(B1 + 2, piece_half(1, node(0, -1), 0), right)
    arrive(B1 + 1, piece(1, node(0, 1)))
    send(B1 + 3, piece_half(1, node(0, 1), 1), left)
    along(1)
    arrive(B1 + 2, piece_half(1, node(0, -2), 0))
    arrive(B1 + 3, piece_half(1, node(0, 2), 1))
    send(B2 + 0, group(0), up)
    send(B2 + 1, group(0), down)
    along(2)
    relay(0)
    along(3)
    relay(1)
    relay(2)
    groups(1)
    along(4)
    relay(3)
    relay(4)
    groups(2)
    relay(5)
    relay(6)
    relay(7)
    groups(3)
    for j in range(8):
        arrive(A3 + 2 * j, piece_half(0, node(Z_STEPS[j], -2), 0))
        arrive(A3 + 2 * j + 1, piece_half(0, node(Z_STEPS[j], 2), 1))
    groups(4)
    for copy in pending:
        copy.wait_send()


def gather_rows(kept, slots, n_ts, block):
    tiles = slots.shape[1] // 2
    width = tiles * slots.shape[2]
    rows = kept.shape[1] // n_ts
    return pl.pallas_call(
        functools.partial(gather_kernel, n_ts, block),
        out_shape=jax.ShapeDtypeStruct((2, n_ts, rows, width), jnp.bfloat16),
        in_specs=[pl.BlockSpec(memory_space=pltpu.SMEM), pl.BlockSpec(memory_space=pltpu.VMEM)],
        out_specs=pl.BlockSpec(memory_space=pltpu.VMEM),
        scratch_shapes=[
            pltpu.VMEM(slots.shape, jnp.bfloat16),
            pltpu.VMEM((rows,) + slots.shape[1:], jnp.float32),
            pltpu.SemaphoreType.DMA((n_ts,)),
            pltpu.SemaphoreType.DMA((n_ts,)),
            pltpu.SemaphoreType.DMA((52,)),
            pltpu.SemaphoreType.DMA((52,)),
        ],
        compiler_params=pltpu.CompilerParams(
            collective_id=0, has_side_effects=True, vmem_limit_bytes=24 * 1024 * 1024),
        name="gather_rows",
    )(kept, slots)


def reduce_kernel(
    n_ts, n_dp, factor,
    pick_ref, normed_ref, scaled_ref, acts_ref, term_ref, out_ref, back_ref,
    pair, sib, x_first, x_last, y_first, y_last, y_sum, z_in, z_out, spread, rows_out, slots_out,
    sib_send, sib_recv, x_send, x_recv, y_send, y_recv, z_send, z_recv, b_send, b_recv,
):
    nz = n_ts // NY
    nx = n_dp // 2
    me = lax.axis_index("ts")
    z, y = me // NY, lax.rem(me, NY)
    dp = lax.axis_index("dp")
    x, core = dp // 2, lax.rem(dp, 2)
    rows = sib.shape[1]
    quarter = rows // 4
    hidden = acts_ref.shape[1] // 3
    pending = []

    def node(dz, dy):
        return lax.rem(z + dz + nz, nz) * NY + lax.rem(y + dy + NY, NY)

    def chip(dx):
        return lax.rem(x + dx + nx, nx) * 2 + core

    barrier = pltpu.get_barrier_semaphore()

    @pl.loop(1, n_ts)
    def _(step):
        pl.semaphore_signal(barrier, inc=1, device_id={"ts": lax.rem(me + step, n_ts)}, device_id_type=MESH)

    for other in (x * 2 + 1 - core, chip(1), chip(-1)):
        pl.semaphore_signal(barrier, inc=1, device_id={"dp": other}, device_id_type=MESH)
    pl.semaphore_wait(barrier, n_ts - 1 + 3)

    def copy_to(sems, index, src, dst, where):
        return pltpu.make_async_remote_copy(
            src, dst, sems[0].at[index], sems[1].at[index], device_id=where, device_id_type=MESH)

    def send(sems, index, src, dst, where):
        copy = copy_to(sems, index, src, dst, where)
        copy.start()
        pending.append(copy)

    def arrive(sems, index, dst):
        copy_to(sems, index, dst, dst, {"ts": me}).wait_recv()

    sib_sems, x_sems, y_sems = (sib_send, sib_recv), (x_send, x_recv), (y_send, y_recv)
    z_sems = (z_send, z_recv)
    right, left = {"ts": node(0, 1)}, {"ts": node(0, -1)}
    up, down = {"ts": node(1, 0)}, {"ts": node(-1, 0)}
    ahead, behind = {"dp": chip(1)}, {"dp": chip(-1)}
    sibling = {"dp": x * 2 + 1 - core}
    zh = nz // 2

    def y_part(dy, which):
        return term_ref.at[pl.ds(which * zh, zh), lax.rem(y + dy + NY, NY)]

    def y_half(buffer, way, which):
        return buffer.at[way, pl.ds(which * zh, zh)]

    send(y_sems, 0, y_part(2, 0), y_first.at[0], right)
    send(y_sems, 1, y_part(2, 1), y_first.at[1], left)
    send(y_sems, 2, y_part(1, 1), y_half(y_last, 0, 1), right)
    send(y_sems, 3, y_part(-1, 0), y_half(y_last, 1, 0), left)

    def lhs(ref, chip_at, m):
        return ref[:, pl.ds(pl.multiple_of(chip_at * (2 * rows) + m * 128, 128), 128)]

    order = (2, 1, -1, 0)
    for j in range(4):
        chip_at = lax.rem(x + order[j] + nx, nx)

        @pl.loop(0, 2 * rows // 128)
        def _(m):
            at = pl.ds(pl.multiple_of(m * 128, 128), 128)
            turned = (((0,), (0,)), ((), ()))
            both = lax.dot_general(
                lhs(normed_ref, chip_at, m), acts_ref[:, : 2 * hidden], turned, preferred_element_type=jnp.float32)
            pair[j, at, : 2 * hidden] = (factor * both).astype(jnp.bfloat16)
            one = lax.dot_general(
                lhs(scaled_ref, chip_at, m), acts_ref[:, 2 * hidden :], turned, preferred_element_type=jnp.float32)
            pair[j, at, 2 * hidden :] = (factor * one).astype(jnp.bfloat16)

        for q in range(4):
            theirs = pl.ds(pl.multiple_of((1 - core) * rows + q * quarter, 16), quarter)
            send(sib_sems, 4 * j + q, pair.at[j, theirs], sib.at[j, pl.ds(q * quarter, quarter)], sibling)

    def add(j, q, others, target):
        arrive(sib_sems, 4 * j + q, sib.at[j, pl.ds(q * quarter, quarter)])

        @pl.loop(0, quarter // 16)
        def _(i):
            mine = pl.ds(pl.multiple_of(core * rows + q * quarter + i * 16, 16), 16)
            here = pl.ds(pl.multiple_of(q * quarter + i * 16, 16), 16)
            total = pair[j, mine, :].astype(jnp.float32) + sib[j, here, :].astype(jnp.float32)
            for ref, start in others:
                total += ref[pl.ds(pl.multiple_of(start + i * 16, 16), 16), :].astype(jnp.float32)
            target[pl.ds(pl.multiple_of(q * quarter + i * 16, 16), 16), :] = total.astype(jnp.bfloat16)

    def chunk(ref, q):
        return ref.at[pl.ds(q * quarter, quarter)]

    for q in range(4):
        add(0, q, (), sib.at[0])
        way = q // 2
        send(x_sems, q, chunk(sib.at[0], q), x_first.at[way, pl.ds((q % 2) * quarter, quarter)], (ahead, behind)[way])
    for q in range(2):
        add(1, 2 + q, (), sib.at[1])
        send(x_sems, 4 + q, chunk(sib.at[1], 2 + q), chunk(x_last.at[0], 2 + q), ahead)
        add(2, q, (), sib.at[2])
        send(x_sems, 6 + q, chunk(sib.at[2], q), chunk(x_last.at[1], q), behind)

    for way, dy, to in ((0, 1, right), (1, -1, left)):
        arrive(y_sems, way, y_first.at[way])
        for k in range(zh):
            own = term_ref[way * zh + k, lax.rem(y + dy + NY, NY)].astype(jnp.float32)
            y_first[way, k] = (own + y_first[way, k].astype(jnp.float32)).astype(jnp.bfloat16)
        send(y_sems, 4 + way, y_first.at[way], y_half(y_last, way, way), to)
    for way in range(2):
        arrive(y_sems, 2 + way, y_half(y_last, way, 1 - way))
        arrive(y_sems, 4 + way, y_half(y_last, way, way))

    @pl.loop(0, nz)
    def _(i):
        at = lax.rem(z + i, nz)
        total = term_ref[at, y].astype(jnp.float32) + y_last[0, at].astype(jnp.float32)
        y_sum[i] = (total + y_last[1, at].astype(jnp.float32)).astype(jnp.bfloat16)

    width = y_sum.shape[2]
    cut = width // 256 * 128
    halves = (pl.ds(0, cut), pl.ds(cut, width - cut))
    send(z_sems, 0, y_sum.at[4, :, halves[0]], z_in.at[0, 0, :, halves[0]], up)
    send(z_sems, 1, y_sum.at[4, :, halves[1]], z_in.at[1, 0, :, halves[1]], down)

    for q in range(2):
        arrive(x_sems, q, x_first.at[0, pl.ds(q * quarter, quarter)])
        add(1, q, ((x_first.at[0], q * quarter),), sib.at[1])
        send(x_sems, 8 + q, chunk(sib.at[1], q), chunk(x_last.at[0], q), ahead)
        arrive(x_sems, 2 + q, x_first.at[1, pl.ds(q * quarter, quarter)])
        add(2, 2 + q, ((x_first.at[1], q * quarter),), sib.at[2])
        send(x_sems, 10 + q, chunk(sib.at[2], 2 + q), chunk(x_last.at[1], 2 + q), behind)

    for s in range(1, 4):
        for way, to in ((0, up), (1, down)):
            own = y_sum[4 - s if way == 0 else 4 + s].astype(jnp.float32)
            if s == 1:
                arrive(z_sems, way, z_in.at[way, 0, :, halves[way]])
                z_out[way, s] = own.astype(jnp.bfloat16)
                landed = z_in[way, 0, :, halves[way]].astype(jnp.float32)
                z_out[way, s, :, halves[way]] = (
                    y_sum[4 - s if way == 0 else 4 + s, :, halves[way]].astype(jnp.float32) + landed
                ).astype(jnp.bfloat16)
            else:
                arrive(z_sems, 2 * (s - 1) + way, z_in.at[way, s - 1])
                z_out[way, s] = (own + z_in[way, s - 1].astype(jnp.float32)).astype(jnp.bfloat16)
            send(z_sems, 2 * s + way, z_out.at[way, s], z_in.at[way, s], to)
    for way in range(2):
        arrive(z_sems, 6 + way, z_in.at[way, 3])

    for t in range(width // 128):
        at = pl.ds(t * 128, 128)
        total = y_sum[0, :, at].astype(jnp.float32) + z_in[0, 3, :, at].astype(jnp.float32)
        spread[:, t, :] = total + z_in[1, 3, :, at].astype(jnp.float32)
    for k in range(rows_out.shape[0]):
        rows_out[k] = spread[k].astype(jnp.bfloat16)

    @pl.loop(0, n_ts)
    def _(h):
        slots_out[h] = rows_out[pick_ref[0, h]]

    def back_copy(step):
        to = lax.rem(me + step, n_ts)
        return pltpu.make_async_remote_copy(
            slots_out.at[to], back_ref.at[me], b_send.at[step], b_recv.at[step],
            device_id={"ts": to}, device_id_type=MESH)

    @pl.loop(1, n_ts)
    def _(step):
        back_copy(step).start()

    back_ref[me] = slots_out[me]

    for q in range(4):
        for way in range(2):
            index = (8 + q, 6 + q)[way] if q < 2 else (2 + q, 8 + q)[way]
            arrive(x_sems, index, chunk(x_last.at[way], q))
        add(3, q, ((x_last.at[0], q * quarter), (x_last.at[1], q * quarter)), out_ref)

    @pl.loop(1, n_ts)
    def _(step):
        back_copy(step).wait_send()
        source = lax.rem(me - step + n_ts, n_ts)
        pltpu.make_async_remote_copy(
            slots_out.at[source], back_ref.at[source], b_send.at[step], b_recv.at[step],
            device_id={"ts": source}, device_id_type=MESH).wait_recv()

    for copy in pending:
        copy.wait_send()


def reduce_all(pick, normed, scaled, acts, term, n_ts, n_dp, factor):
    nz = n_ts // NY
    rows = normed.shape[1] // n_dp
    wide = acts.shape[1]
    piece = term.shape[2:]
    tiles = piece[1] // 128
    pad = -(-tiles // 16) * 16
    bf16, dma = jnp.bfloat16, pltpu.SemaphoreType.DMA
    vmem = pl.BlockSpec(memory_space=pltpu.VMEM)
    return pl.pallas_call(
        functools.partial(reduce_kernel, n_ts, n_dp, factor),
        out_shape=(
            jax.ShapeDtypeStruct((rows, wide), bf16),
            jax.ShapeDtypeStruct((n_ts, pad, 128), bf16),
        ),
        in_specs=[pl.BlockSpec(memory_space=pltpu.SMEM)] + [vmem] * 4,
        out_specs=(vmem, vmem),
        scratch_shapes=[
            pltpu.VMEM((4, 2 * rows, wide), bf16),
            pltpu.VMEM((4, rows, wide), bf16),
            pltpu.VMEM((2, rows // 2, wide), bf16),
            pltpu.VMEM((2, rows, wide), bf16),
            pltpu.VMEM((2, nz // 2) + piece, bf16),
            pltpu.VMEM((2, nz) + piece, bf16),
            pltpu.VMEM((nz,) + piece, bf16),
            pltpu.VMEM((2, 4) + piece, bf16),
            pltpu.VMEM((2, 4) + piece, bf16),
            pltpu.VMEM((piece[0], pad, 128), jnp.float32),
            pltpu.VMEM((piece[0], pad, 128), bf16),
            pltpu.VMEM((n_ts, pad, 128), bf16),
            dma((16,)), dma((16,)), dma((12,)), dma((12,)), dma((6,)), dma((6,)),
            dma((8,)), dma((8,)), dma((n_ts,)), dma((n_ts,)),
        ],
        compiler_params=pltpu.CompilerParams(
            collective_id=1, has_side_effects=True, vmem_limit_bytes=44 * 1024 * 1024),
        name="reduce_all",
    )(pick, normed, scaled, acts, term)


epsilon = 1e-06
gelu_scale = math.sqrt(2.0 / math.pi)


def gelu_pair(pre_act):
    cubic = pre_act + 0.044715 * pre_act * pre_act * pre_act
    tanh_part = jnp.tanh(gelu_scale * cubic)
    gelu_out = 0.5 * pre_act * (1.0 + tanh_part)
    slope_out = 0.5 * (1.0 + tanh_part) + 0.5 * pre_act * (
        1.0 - tanh_part * tanh_part
    ) * gelu_scale * (1.0 + 3.0 * 0.044715 * pre_act * pre_act)
    return (gelu_out, slope_out)


def norm_backward(row_data, summed_grad, summed_dot, prenormal_scaling, scorer_matrix):
    row_f = row_data.astype(jnp.float32)
    inv_rms = lax.rsqrt(jnp.mean(row_f * row_f, axis=1, keepdims=True) + epsilon)
    unit_rows = row_f * inv_rms
    weight = jax.nn.sigmoid(jnp.dot(row_data, scorer_matrix, preferred_element_type=jnp.float32))
    logit_grad = (1.0 - weight) * summed_dot
    gained = summed_grad * prenormal_scaling.astype(jnp.float32)
    row_grad = inv_rms * (gained - unit_rows * jnp.mean(gained * unit_rows, axis=1, keepdims=True))
    return row_grad + logit_grad[:, None] * scorer_matrix.astype(jnp.float32)


def local(
    block_activity, result_cotangent, kept_locations, prenormal_scaling, scorer_matrix,
    switch_matrix, expand_matrix, contract_matrix,
):
    n_ts = lax.axis_size("ts")
    me = lax.axis_index("ts")
    n_dp = lax.axis_size("dp")
    local_tokens = block_activity.shape[1]
    model_width = block_activity.shape[2]
    cap = kept_locations.shape[1]
    hidden_width = switch_matrix.shape[1]
    factor = (n_dp * cap) ** (-0.5)
    kept = kept_locations[0]
    first = jnp.sum((kept < me * local_tokens).astype(jnp.int32))
    count = jnp.sum((kept // local_tokens == me).astype(jnp.int32))
    classes = jnp.arange(n_ts, dtype=jnp.int32)
    ranks = first + lax.rem(classes - lax.rem(first, n_ts) + n_ts, n_ts)
    own_valid = ranks < first + count
    own_index = jnp.clip(jnp.take(kept, jnp.minimum(ranks, cap - 1)) - me * local_tokens, 0, local_tokens - 1)
    own_rows = jnp.take(block_activity[0], own_index, axis=0)
    own_grads = jnp.take(result_cotangent[0], own_index, axis=0)
    slots = jnp.concatenate([own_rows, own_grads], axis=1).reshape(n_ts, -1, 128)
    full = gather_rows(kept_locations, slots, n_ts, local_tokens)
    row_data = full[0].reshape(cap, model_width)
    grad_data = full[1].reshape(cap, model_width)

    row_f = row_data.astype(jnp.float32)
    inv_rms = lax.rsqrt(jnp.mean(row_f * row_f, axis=1, keepdims=True) + epsilon)
    normed = (row_f * inv_rms * prenormal_scaling.astype(jnp.float32)).astype(jnp.bfloat16)
    weight = jax.nn.sigmoid(jnp.dot(row_data, scorer_matrix, preferred_element_type=jnp.float32))
    pre_gate = jnp.dot(normed, switch_matrix, preferred_element_type=jnp.float32)
    pre_up = jnp.dot(normed, expand_matrix, preferred_element_type=jnp.float32)
    gelu_out, slope_out = gelu_pair(pre_gate)
    hidden = (gelu_out * pre_up).astype(jnp.bfloat16)
    scaled = (weight[:, None] * grad_data.astype(jnp.float32)).astype(jnp.bfloat16)
    hidden_grad = jnp.einsum("cd,fd->cf", scaled, contract_matrix, preferred_element_type=jnp.float32)
    gate_in = (hidden_grad * pre_up * slope_out).astype(jnp.bfloat16)
    up_in = (hidden_grad * gelu_out).astype(jnp.bfloat16)
    dot_part = jnp.sum(hidden.astype(jnp.float32) * hidden_grad, axis=1)
    normed_term = jnp.einsum("cf,df->cd", gate_in, switch_matrix, preferred_element_type=jnp.float32)
    normed_term = normed_term + jnp.einsum("cf,df->cd", up_in, expand_matrix, preferred_element_type=jnp.float32)
    term = jnp.concatenate(
        [normed_term, jnp.broadcast_to(dot_part[:, None], (cap, 128))], axis=1).astype(jnp.bfloat16)
    acts = jnp.concatenate([gate_in, up_in, hidden], axis=1)
    class_holder = jnp.take(kept.reshape(-1, n_ts), me, axis=1) // local_tokens
    pick = jnp.argmax(class_holder[None, :] == classes[:, None], axis=1).astype(jnp.int32)[None]
    summed_weights, back = reduce_all(
        pick, normed, scaled, acts, term.reshape(n_ts // NY, NY, cap // n_ts, -1), n_ts, n_dp, factor)
    gate_grad = summed_weights[:, :hidden_width]
    up_grad = summed_weights[:, hidden_width : 2 * hidden_width]
    down_grad = summed_weights[:, 2 * hidden_width :].T
    back = back.reshape(n_ts, -1)
    own_term = back[:, :model_width].astype(jnp.float32)
    own_dot = back[:, model_width].astype(jnp.float32)
    row_grad = norm_backward(own_rows, own_term, own_dot, prenormal_scaling, scorer_matrix)
    row_grad = jnp.where(own_valid[:, None], row_grad, 0.0).astype(jnp.bfloat16)
    place = (jnp.arange(local_tokens)[:, None] == own_index[None, :]) & own_valid[None, :]
    token_grad = jnp.dot(place.astype(jnp.bfloat16), row_grad, preferred_element_type=jnp.float32)
    return (token_grad.astype(jnp.bfloat16)[None], gate_grad, up_grad, down_grad)


def solution(mesh):
    in_specs = (
        P("dp", "ts", None), P("dp", "ts", None), P("dp", None), P(), P(),
        P(None, "ts"), P(None, "ts"), P("ts", None),
    )
    out_specs = (P("dp", "ts", None), P("dp", "ts"), P("dp", "ts"), P("ts", "dp"))
    return jax.shard_map(local, mesh=mesh, in_specs=in_specs, out_specs=out_specs, check_vma=False)
```

```python
import functools
import math

import jax
import jax.numpy as jnp
from jax import lax
from jax.experimental import pallas as pl
from jax.experimental.pallas import tpu as pltpu
from jax.sharding import PartitionSpec as P

MESH = pl.DeviceIdType.MESH
NY = 4
Z_STEPS = (0, -1, 1, -2, 2, -3, 3, 4)
LANES = 128
K_TILE = 512
epsilon = 1e-06
gelu_scale = math.sqrt(2.0 / math.pi)
ROWS_BY_ROWS = (((0,), (0,)), ((), ()))
COLS_BY_COLS = (((1,), (1,)), ((), ()))


def gelu_pair(pre_act):
    cubic = pre_act + 0.044715 * pre_act * pre_act * pre_act
    tanh_part = jnp.tanh(gelu_scale * cubic)
    gelu_out = 0.5 * pre_act * (1.0 + tanh_part)
    slope_out = 0.5 * (1.0 + tanh_part) + 0.5 * pre_act * (
        1.0 - tanh_part * tanh_part
    ) * gelu_scale * (1.0 + 3.0 * 0.044715 * pre_act * pre_act)
    return (gelu_out, slope_out)


def dot(a, b, dims=(((1,), (0,)), ((), ()))):
    return lax.dot_general(a, b, dims, preferred_element_type=jnp.float32)


def block_kernel(
    n_ts, n_dp, factor,
    kept_ref, kept_row, act_ref, cot_ref, gain_ref, scorer_ref, switch_hbm, expand_hbm, contract_hbm,
    token_ref, gate_ref, up_ref, down_ref,
    switch, expand, contract, w_sem,
    own, slots_f, slots, landed, wide, piece_f, full, p1_send, p1_recv, g_send, g_recv,
    pre_gate, pre_up, hidden_grad, gate_in, up_in, acts, hidden, term,
    pair, sib, x_first, x_last, y_first, y_last, y_sum, z_in, z_out, spread, rows_out, slots_out, back, back_f, term_f,
    sib_send, sib_recv, x_send, x_recv, y_send, y_recv, z_send, z_recv, b_send, b_recv,
):
    bf16, f32 = jnp.bfloat16, jnp.float32
    nz = n_ts // NY
    nx = n_dp // 2
    me = lax.axis_index("ts")
    z, y = me // NY, lax.rem(me, NY)
    dp = lax.axis_index("dp")
    x, core = dp // 2, lax.rem(dp, 2)
    block, width = act_ref.shape
    tiles = width // LANES
    piece_rows = full.shape[2]
    cap = n_ts * piece_rows
    hid = hidden.shape[1]
    pending = []

    def node(dz, dy):
        return lax.rem(z + dz + nz, nz) * NY + lax.rem(y + dy + NY, NY)

    def chip(dx):
        return lax.rem(x + dx + nx, nx) * 2 + core

    def copy_to(sems, index, src, dst, where):
        return pltpu.make_async_remote_copy(
            src, dst, sems[0].at[index], sems[1].at[index], device_id=where, device_id_type=MESH)

    def send(sems, index, src, dst, where):
        copy = copy_to(sems, index, src, dst, where)
        copy.start()
        pending.append(copy)

    def arrive(sems, index, dst):
        copy_to(sems, index, dst, dst, {"ts": me}).wait_recv()

    right, left = {"ts": node(0, 1)}, {"ts": node(0, -1)}
    up, down = {"ts": node(1, 0)}, {"ts": node(-1, 0)}
    ahead, behind = {"dp": chip(1)}, {"dp": chip(-1)}
    sibling = {"dp": x * 2 + 1 - core}

    barrier = pltpu.get_barrier_semaphore()

    @pl.loop(1, n_ts)
    def _(step):
        pl.semaphore_signal(barrier, inc=1, device_id={"ts": lax.rem(me + step, n_ts)}, device_id_type=MESH)

    for where in (sibling, ahead, behind):
        pl.semaphore_signal(barrier, inc=1, device_id=where, device_id_type=MESH)

    weight_copies = [
        pltpu.make_async_copy(src, dst, w_sem.at[i])
        for i, (src, dst) in enumerate(((switch_hbm, switch), (expand_hbm, expand), (contract_hbm, contract)))
    ]
    for copy in weight_copies:
        copy.start()

    kept = jnp.broadcast_to(kept_row[...], (block, cap))
    position = lax.broadcasted_iota(jnp.int32, (block, cap), 0) + block * me
    rank = jnp.sum((kept < position).astype(f32), axis=1, keepdims=True)
    routed = jnp.sum((kept == position).astype(f32), axis=1, keepdims=True)
    row_class = rank - n_ts * jnp.floor(rank * (1.0 / n_ts))
    classes = lax.broadcasted_iota(jnp.int32, (block, n_ts), 1).astype(f32)
    chosen = jnp.where(classes == row_class, routed, 0.0).astype(bf16)
    own[...] = dot(chosen, act_ref[...], ROWS_BY_ROWS)
    own_cot = dot(chosen, cot_ref[...], ROWS_BY_ROWS)
    for t in range(tiles):
        slots_f[:, t, :] = own[:, t * LANES:(t + 1) * LANES]
        slots_f[:, tiles + t, :] = own_cot[:, t * LANES:(t + 1) * LANES]

    @pl.loop(0, n_ts)
    def _(c):
        slots[c] = slots_f[c].astype(bf16)

    pl.semaphore_wait(barrier, n_ts - 1 + 3)

    def p1_copy(step):
        to = lax.rem(me + step, n_ts)
        return pltpu.make_async_remote_copy(
            slots.at[to], landed.at[me], p1_send.at[step], p1_recv.at[step],
            device_id={"ts": to}, device_id_type=MESH)

    @pl.loop(1, n_ts)
    def _(step):
        p1_copy(step).start()

    landed[me] = slots[me]

    @pl.loop(1, n_ts)
    def _(step):
        source = lax.rem(me - step + n_ts, n_ts)
        pltpu.make_async_remote_copy(
            slots.at[source], landed.at[source], p1_send.at[step], p1_recv.at[step],
            device_id={"ts": source}, device_id_type=MESH).wait_recv()

    for k in range(piece_rows):
        wide[k] = landed[kept_ref[0, n_ts * k + me] // block].astype(f32)
    for t in range(2 * tiles):
        piece_f[:, t * LANES:(t + 1) * LANES] = wide[:, t, :]

    gain = gain_ref[...].astype(f32)
    scorer = scorer_ref[...].astype(f32)
    row_f = piece_f[:, :width]
    inv_rms = lax.rsqrt(jnp.sum(row_f * row_f, axis=1, keepdims=True) * (1.0 / width) + epsilon)
    weight = jax.nn.sigmoid(jnp.sum(row_f * scorer, axis=1, keepdims=True))
    full[0, me] = (row_f * inv_rms * gain).astype(bf16)
    full[1, me] = (weight * piece_f[:, width:]).astype(bf16)

    g_sems = (g_send, g_recv)
    half = width // 2

    def piece(part, n):
        return full.at[part, n]

    def piece_half(part, n, which):
        return full.at[part, n, :, pl.ds(which * half, half)]

    def group(dz):
        return full.at[1, pl.ds(lax.rem(z + dz + nz, nz) * NY, NY)]

    def group_half(dz, which):
        return full.at[1, pl.ds(lax.rem(z + dz + nz, nz) * NY + which * (NY // 2), NY // 2)]

    def share(index, ref, where):
        send(g_sems, index, ref, ref, where)

    B1, A1, B2, A2, A3 = 0, 4, 12, 20, 36
    share(B1 + 0, piece(1, me), right)
    share(B1 + 1, piece(1, me), left)
    share(A1 + 0, piece(0, me), up)
    share(A1 + 1, piece(0, me), down)

    def fan_out(j):
        dz = Z_STEPS[j]
        share(A2 + 2 * j, piece(0, node(dz, 0)), right)
        share(A2 + 2 * j + 1, piece(0, node(dz, 0)), left)

    def relay(j):
        dz = Z_STEPS[j]
        arrive(g_sems, A2 + 2 * j, piece(0, node(dz, -1)))
        share(A3 + 2 * j, piece_half(0, node(dz, -1), 0), right)
        arrive(g_sems, A2 + 2 * j + 1, piece(0, node(dz, 1)))
        share(A3 + 2 * j + 1, piece_half(0, node(dz, 1), 1), left)

    def along(s):
        if s < 4:
            arrive(g_sems, A1 + 2 * (s - 1), piece(0, node(-s, 0)))
            if s < 3:
                share(A1 + 2 * s, piece(0, node(-s, 0)), up)
            else:
                share(A1 + 6, piece_half(0, node(-3, 0), 0), up)
            arrive(g_sems, A1 + 2 * (s - 1) + 1, piece(0, node(s, 0)))
            if s < 3:
                share(A1 + 2 * s + 1, piece(0, node(s, 0)), down)
            else:
                share(A1 + 7, piece_half(0, node(3, 0), 1), down)
            fan_out(2 * s - 1)
            fan_out(2 * s)
        else:
            arrive(g_sems, A1 + 6, piece_half(0, node(-4, 0), 0))
            arrive(g_sems, A1 + 7, piece_half(0, node(4, 0), 1))
            fan_out(7)

    def groups(s):
        if s < 4:
            arrive(g_sems, B2 + 2 * (s - 1), group(-s))
            if s < 3:
                share(B2 + 2 * s, group(-s), up)
            else:
                share(B2 + 6, group_half(-3, 0), up)
            arrive(g_sems, B2 + 2 * (s - 1) + 1, group(s))
            if s < 3:
                share(B2 + 2 * s + 1, group(s), down)
            else:
                share(B2 + 7, group_half(3, 1), down)
        else:
            arrive(g_sems, B2 + 6, group_half(-4, 0))
            arrive(g_sems, B2 + 7, group_half(4, 1))

    fan_out(0)
    arrive(g_sems, B1 + 0, piece(1, node(0, -1)))
    share(B1 + 2, piece_half(1, node(0, -1), 0), right)
    arrive(g_sems, B1 + 1, piece(1, node(0, 1)))
    share(B1 + 3, piece_half(1, node(0, 1), 1), left)
    along(1)
    arrive(g_sems, B1 + 2, piece_half(1, node(0, -2), 0))
    arrive(g_sems, B1 + 3, piece_half(1, node(0, 2), 1))
    share(B2 + 0, group(0), up)
    share(B2 + 1, group(0), down)
    along(2)
    relay(0)
    along(3)
    relay(1)
    relay(2)
    groups(1)
    along(4)
    relay(3)
    relay(4)
    groups(2)
    relay(5)
    relay(6)
    relay(7)
    groups(3)
    for j in range(8):
        arrive(g_sems, A3 + 2 * j, piece_half(0, node(Z_STEPS[j], -2), 0))
        arrive(g_sems, A3 + 2 * j + 1, piece_half(0, node(Z_STEPS[j], 2), 1))

    def columns(part, start, size):
        return full[part, :, :, pl.ds(pl.multiple_of(start, LANES), size)].reshape(cap, size)

    for copy in weight_copies:
        copy.wait()
    pre_gate[...] = jnp.zeros_like(pre_gate)
    pre_up[...] = jnp.zeros_like(pre_up)
    hidden_grad[...] = jnp.zeros_like(hidden_grad)

    @pl.loop(0, width // K_TILE)
    def _(k):
        at = pl.ds(pl.multiple_of(k * K_TILE, K_TILE), K_TILE)
        normed = columns(0, k * K_TILE, K_TILE)
        pre_gate[...] += dot(normed, switch[at, :])
        pre_up[...] += dot(normed, expand[at, :])

    groups(4)

    @pl.loop(0, width // K_TILE)
    def _(k):
        at = pl.ds(pl.multiple_of(k * K_TILE, K_TILE), K_TILE)
        hidden_grad[...] += dot(columns(1, k * K_TILE, K_TILE), contract[:, at], COLS_BY_COLS)

    @pl.loop(0, nz)
    def _(i):
        n = cap // nz
        at = pl.ds(pl.multiple_of(i * n, n), n)
        gelu_out, slope_out = gelu_pair(pre_gate[at, :])
        up_value, grad = pre_up[at, :], hidden_grad[at, :]
        hidden_value = (gelu_out * up_value).astype(bf16)
        hidden[at, :] = hidden_value
        gate_value = (grad * up_value * slope_out).astype(bf16)
        up_back = (grad * gelu_out).astype(bf16)
        gate_in[at, :] = gate_value
        up_in[at, :] = up_back
        acts[at, :hid] = gate_value
        acts[at, hid:] = up_back
        router = jnp.sum(hidden_value.astype(f32) * grad, axis=1, keepdims=True)
        term[i, :, :, width:] = jnp.broadcast_to(router, (n, LANES)).astype(bf16).reshape(NY, piece_rows, LANES)

    sib_sems, x_sems, y_sems = (sib_send, sib_recv), (x_send, x_recv), (y_send, y_recv)
    z_sems = (z_send, z_recv)
    rows = sib.shape[1]
    quarter = rows // 4
    order = (2, 1, -1, 0)

    def partials(j):
        start = lax.rem(x + order[j] + nx, nx) * (2 * rows)

        @pl.loop(0, 2 * rows // LANES)
        def _(m):
            at = pl.ds(pl.multiple_of(m * LANES, LANES), LANES)
            pair[j, at, : 2 * hid] = (
                factor * dot(columns(0, start + m * LANES, LANES), acts[...], ROWS_BY_ROWS)).astype(bf16)

        both = (factor * dot(hidden[...], columns(1, start, 2 * rows), ROWS_BY_ROWS)).astype(bf16)
        pair[j, :rows, 2 * hid :] = both[:, :rows]
        pair[j, rows:, 2 * hid :] = both[:, rows:]
        for q in range(4):
            theirs = pl.ds(pl.multiple_of((1 - core) * rows + q * quarter, 16), quarter)
            send(sib_sems, 4 * j + q, pair.at[j, theirs], sib.at[j, pl.ds(q * quarter, quarter)], sibling)

    def add(j, q, others, store):
        arrive(sib_sems, 4 * j + q, sib.at[j, pl.ds(q * quarter, quarter)])

        @pl.loop(0, quarter // 16)
        def _(i):
            mine = pl.ds(pl.multiple_of(core * rows + q * quarter + i * 16, 16), 16)
            here = pl.ds(pl.multiple_of(q * quarter + i * 16, 16), 16)
            total = pair[j, mine, :].astype(f32) + sib[j, here, :].astype(f32)
            for ref, start in others:
                total += ref[pl.ds(pl.multiple_of(start + i * 16, 16), 16), :].astype(f32)
            store(here, total.astype(bf16))

    def in_place(j):
        def store(here, value):
            sib[j, here, :] = value
        return store

    def chunk(ref, q):
        return ref.at[pl.ds(q * quarter, quarter)]

    partials(0)
    partials(1)
    for q in range(4):
        add(0, q, (), in_place(0))
        way = q // 2
        send(x_sems, q, chunk(sib.at[0], q), x_first.at[way, pl.ds((q % 2) * quarter, quarter)], (ahead, behind)[way])
    partials(2)

    @pl.loop(0, width // K_TILE)
    def _(k):
        at = pl.ds(pl.multiple_of(k * K_TILE, K_TILE), K_TILE)
        value = dot(gate_in[...], switch[at, :], COLS_BY_COLS) + dot(up_in[...], expand[at, :], COLS_BY_COLS)
        term[:, :, :, at] = value.astype(bf16).reshape(nz, NY, piece_rows, K_TILE)

    zh = nz // 2

    def y_part(dy, which):
        return term.at[pl.ds(which * zh, zh), lax.rem(y + dy + NY, NY)]

    def y_half(buffer, way, which):
        return buffer.at[way, pl.ds(which * zh, zh)]

    send(y_sems, 0, y_part(2, 0), y_first.at[0], right)
    send(y_sems, 1, y_part(2, 1), y_first.at[1], left)
    send(y_sems, 2, y_part(1, 1), y_half(y_last, 0, 1), right)
    send(y_sems, 3, y_part(-1, 0), y_half(y_last, 1, 0), left)

    for q in range(2):
        add(1, 2 + q, (), in_place(1))
        send(x_sems, 4 + q, chunk(sib.at[1], 2 + q), chunk(x_last.at[0], 2 + q), ahead)
        add(2, q, (), in_place(2))
        send(x_sems, 6 + q, chunk(sib.at[2], q), chunk(x_last.at[1], q), behind)
    partials(3)

    for way, dy, to in ((0, 1, right), (1, -1, left)):
        arrive(y_sems, way, y_first.at[way])
        for k in range(zh):
            own_part = term[way * zh + k, lax.rem(y + dy + NY, NY)].astype(f32)
            y_first[way, k] = (own_part + y_first[way, k].astype(f32)).astype(bf16)
        send(y_sems, 4 + way, y_first.at[way], y_half(y_last, way, way), to)
    for way in range(2):
        arrive(y_sems, 2 + way, y_half(y_last, way, 1 - way))
        arrive(y_sems, 4 + way, y_half(y_last, way, way))

    @pl.loop(0, nz)
    def _(i):
        at = lax.rem(z + i, nz)
        total = term[at, y].astype(f32) + y_last[0, at].astype(f32)
        y_sum[i] = (total + y_last[1, at].astype(f32)).astype(bf16)

    wide_row = y_sum.shape[2]
    cut = wide_row // (2 * LANES) * LANES
    halves = (pl.ds(0, cut), pl.ds(cut, wide_row - cut))
    send(z_sems, 0, y_sum.at[4, :, halves[0]], z_in.at[0, 0, :, halves[0]], up)
    send(z_sems, 1, y_sum.at[4, :, halves[1]], z_in.at[1, 0, :, halves[1]], down)

    for q in range(2):
        arrive(x_sems, q, x_first.at[0, pl.ds(q * quarter, quarter)])
        add(1, q, ((x_first.at[0], q * quarter),), in_place(1))
        send(x_sems, 8 + q, chunk(sib.at[1], q), chunk(x_last.at[0], q), ahead)
        arrive(x_sems, 2 + q, x_first.at[1, pl.ds(q * quarter, quarter)])
        add(2, 2 + q, ((x_first.at[1], q * quarter),), in_place(2))
        send(x_sems, 10 + q, chunk(sib.at[2], 2 + q), chunk(x_last.at[1], 2 + q), behind)

    for s in range(1, 4):
        for way, to in ((0, up), (1, down)):
            mine = 4 - s if way == 0 else 4 + s
            if s == 1:
                arrive(z_sems, way, z_in.at[way, 0, :, halves[way]])
                z_out[way, s] = y_sum[mine]
                both = y_sum[mine, :, halves[way]].astype(f32) + z_in[way, 0, :, halves[way]].astype(f32)
                z_out[way, s, :, halves[way]] = both.astype(bf16)
            else:
                arrive(z_sems, 2 * (s - 1) + way, z_in.at[way, s - 1])
                z_out[way, s] = (y_sum[mine].astype(f32) + z_in[way, s - 1].astype(f32)).astype(bf16)
            send(z_sems, 2 * s + way, z_out.at[way, s], z_in.at[way, s], to)
    for way in range(2):
        arrive(z_sems, 6 + way, z_in.at[way, 3])

    spread[...] = jnp.zeros_like(spread)
    for t in range(wide_row // LANES):
        at = pl.ds(t * LANES, LANES)
        total = y_sum[0, :, at].astype(f32) + z_in[0, 3, :, at].astype(f32)
        spread[:, t, :] = total + z_in[1, 3, :, at].astype(f32)
    for k in range(piece_rows):
        rows_out[k] = spread[k].astype(bf16)

    @pl.loop(0, n_ts)
    def _(h):
        pick = 0
        for k in range(1, piece_rows):
            pick = jnp.where(kept_ref[0, n_ts * k + me] // block == h, k, pick)
        slots_out[h] = rows_out[pick]

    def back_copy(step):
        to = lax.rem(me + step, n_ts)
        return pltpu.make_async_remote_copy(
            slots_out.at[to], back.at[me], b_send.at[step], b_recv.at[step],
            device_id={"ts": to}, device_id_type=MESH)

    @pl.loop(1, n_ts)
    def _(step):
        back_copy(step).start()

    back[me] = slots_out[me]

    def store_out(here, value):
        gate_ref[here, :] = value[:, :hid]
        up_ref[here, :] = value[:, hid : 2 * hid]
        down_ref[here, :] = value[:, 2 * hid :]

    def finish(q):
        for way in range(2):
            index = (8 + q, 6 + q)[way] if q < 2 else (2 + q, 8 + q)[way]
            arrive(x_sems, index, chunk(x_last.at[way], q))
        add(3, q, ((x_last.at[0], q * quarter), (x_last.at[1], q * quarter)), store_out)

    @pl.loop(1, n_ts)
    def _(step):
        source = lax.rem(me - step + n_ts, n_ts)
        pltpu.make_async_remote_copy(
            slots_out.at[source], back.at[source], b_send.at[step], b_recv.at[step],
            device_id={"ts": source}, device_id_type=MESH).wait_recv()

    @pl.loop(0, n_ts)
    def _(c):
        back_f[c] = back[c].astype(f32)

    for t in range(tiles):
        term_f[:, t * LANES:(t + 1) * LANES] = back_f[:, t, :]
    summed_dot = back_f[:, tiles, :][:, :1]
    own_f = own[...]
    own_inv = lax.rsqrt(jnp.sum(own_f * own_f, axis=1, keepdims=True) * (1.0 / width) + epsilon)
    own_weight = jax.nn.sigmoid(jnp.sum(own_f * scorer, axis=1, keepdims=True))
    unit = own_f * own_inv
    gained = term_f[...] * gain
    mean = jnp.sum(gained * unit, axis=1, keepdims=True) * (1.0 / width)
    row_grad = own_inv * (gained - unit * mean) + ((1.0 - own_weight) * summed_dot) * scorer
    token_ref[...] = dot(chosen, row_grad.astype(bf16)).astype(bf16)

    for q in range(4):
        finish(q)

    @pl.loop(1, n_ts)
    def _(step):
        p1_copy(step).wait_send()
        back_copy(step).wait_send()

    for copy in pending:
        copy.wait_send()


def local(
    block_activity, result_cotangent, kept_locations, prenormal_scaling, scorer_matrix,
    switch_matrix, expand_matrix, contract_matrix,
):
    n_ts, n_dp = lax.axis_size("ts"), lax.axis_size("dp")
    nz = n_ts // NY
    block, width = block_activity.shape[1:]
    cap = kept_locations.shape[1]
    hid = switch_matrix.shape[1]
    rows = width // n_dp
    piece = cap // n_ts
    tiles = width // LANES
    pad = -(-(tiles + 1) // 16) * 16
    bf16, f32, dma = jnp.bfloat16, jnp.float32, pltpu.SemaphoreType.DMA
    vmem = pl.BlockSpec(memory_space=pltpu.VMEM)
    hbm = pl.BlockSpec(memory_space=pl.ANY)
    token, gate, up, down = pl.pallas_call(
        functools.partial(block_kernel, n_ts, n_dp, (n_dp * cap) ** (-0.5)),
        out_shape=(
            jax.ShapeDtypeStruct((block, width), bf16),
            jax.ShapeDtypeStruct((rows, hid), bf16),
            jax.ShapeDtypeStruct((rows, hid), bf16),
            jax.ShapeDtypeStruct((hid, rows), bf16),
        ),
        in_specs=[pl.BlockSpec(memory_space=pltpu.SMEM)] + [vmem] * 5 + [hbm] * 3,
        out_specs=(vmem,) * 4,
        scratch_shapes=[
            pltpu.VMEM((width, hid), bf16), pltpu.VMEM((width, hid), bf16), pltpu.VMEM((hid, width), bf16), dma((3,)),
            pltpu.VMEM((n_ts, width), f32),
            pltpu.VMEM((n_ts, 2 * tiles, LANES), f32),
            pltpu.VMEM((n_ts, 2 * tiles, LANES), bf16),
            pltpu.VMEM((n_ts, 2 * tiles, LANES), bf16),
            pltpu.VMEM((piece, 2 * tiles, LANES), f32),
            pltpu.VMEM((piece, 2 * width), f32),
            pltpu.VMEM((2, n_ts, piece, width), bf16),
            dma((n_ts,)), dma((n_ts,)), dma((52,)), dma((52,)),
            pltpu.VMEM((cap, hid), f32), pltpu.VMEM((cap, hid), f32), pltpu.VMEM((cap, hid), f32),
            pltpu.VMEM((cap, hid), bf16), pltpu.VMEM((cap, hid), bf16), pltpu.VMEM((cap, 2 * hid), bf16),
            pltpu.VMEM((cap, hid), bf16),
            pltpu.VMEM((nz, NY, piece, width + LANES), bf16),
            pltpu.VMEM((4, 2 * rows, 3 * hid), bf16),
            pltpu.VMEM((4, rows, 3 * hid), bf16),
            pltpu.VMEM((2, rows // 2, 3 * hid), bf16),
            pltpu.VMEM((2, rows, 3 * hid), bf16),
            pltpu.VMEM((2, nz // 2, piece, width + LANES), bf16),
            pltpu.VMEM((2, nz, piece, width + LANES), bf16),
            pltpu.VMEM((nz, piece, width + LANES), bf16),
            pltpu.VMEM((2, 4, piece, width + LANES), bf16),
            pltpu.VMEM((2, 4, piece, width + LANES), bf16),
            pltpu.VMEM((piece, pad, LANES), f32),
            pltpu.VMEM((piece, pad, LANES), bf16),
            pltpu.VMEM((n_ts, pad, LANES), bf16),
            pltpu.VMEM((n_ts, pad, LANES), bf16),
            pltpu.VMEM((n_ts, pad, LANES), f32),
            pltpu.VMEM((n_ts, width), f32),
            dma((16,)), dma((16,)), dma((12,)), dma((12,)), dma((6,)), dma((6,)),
            dma((8,)), dma((8,)), dma((n_ts,)), dma((n_ts,)),
        ],
        compiler_params=pltpu.CompilerParams(
            collective_id=0, has_side_effects=True, vmem_limit_bytes=56 * 1024 * 1024),
        name="block_backward",
    )(
        kept_locations, kept_locations, block_activity[0], result_cotangent[0],
        prenormal_scaling[None], scorer_matrix[None], switch_matrix, expand_matrix, contract_matrix,
    )
    return (token[None], gate, up, down)


def solution(mesh):
    in_specs = (
        P("dp", "ts", None), P("dp", "ts", None), P("dp", None), P(), P(),
        P(None, "ts"), P(None, "ts"), P("ts", None),
    )
    out_specs = (P("dp", "ts", None), P("dp", "ts"), P("dp", "ts"), P("ts", "dp"))
    return jax.shard_map(local, mesh=mesh, in_specs=in_specs, out_specs=out_specs, check_vma=False)
```

```python
import functools
import math

import jax
import jax.numpy as jnp
from jax import lax
from jax.experimental import pallas as pl
from jax.experimental.pallas import tpu as pltpu
from jax.sharding import PartitionSpec as P

MESH = pl.DeviceIdType.MESH
NY = 4
RS_ORDER = (
    "acts_start", "terms", ("y", 4), ("y", 3), ("y", 5), ("p", 0), ("p", 1), ("p", 2), ("p", 3), ("s", 4), "acts_relay",
    ("y", 2), ("y", 6), "x_start", ("s", 3), ("s", 5), ("e", 4), ("z", 0), ("y", 1), ("y", 7), "seen_end", "grow_own",
    ("s", 2), ("s", 6), ("e", 3), ("e", 5), ("z", 1), ("y", 0), "acts_near", ("s", 1), ("s", 7), ("e", 2), ("e", 6),
    ("z", 2), ("s", 0), "grow_near", ("e", 1), ("e", 7), ("z", 3), "acts_far", ("e", 0), "x_second", "back_start",
    "grow_far", "back_end", "x_end",
)
AG_ORDER = (
    "b1_start", "a1_start", ("f", 0), "b1_relay", ("a", 1), "b1_end", "b2_start", ("a", 2), ("r", 0), ("a", 3),
    ("r", 1), ("l", 0), ("n", 0), ("r", 2), ("g", 1), ("l", 1), ("n", 1), ("a", 4), ("r", 3), ("l", 2), ("n", 2),
    ("r", 4), ("g", 2), ("l", 3), ("n", 3), ("r", 5), ("l", 4), ("n", 4), ("r", 6), ("l", 5), ("n", 5),
    ("r", 7), ("l", 6), ("n", 6), ("g", 3), ("l", 7), ("n", 7), ("g", 4),
)
Z_STEPS = (0, -1, 1, -2, 2, -3, 3, 4)
LANES = 128
K_TILE = 512
epsilon = 1e-06
gelu_scale = math.sqrt(2.0 / math.pi)
ROWS_BY_ROWS = (((0,), (0,)), ((), ()))
COLS_BY_COLS = (((1,), (1,)), ((), ()))


def gelu_pair(pre_act):
    cubic = pre_act + 0.044715 * pre_act * pre_act * pre_act
    tanh_part = jnp.tanh(gelu_scale * cubic)
    gelu_out = 0.5 * pre_act * (1.0 + tanh_part)
    slope_out = 0.5 * (1.0 + tanh_part) + 0.5 * pre_act * (
        1.0 - tanh_part * tanh_part
    ) * gelu_scale * (1.0 + 3.0 * 0.044715 * pre_act * pre_act)
    return (gelu_out, slope_out)


def dot(a, b, dims=(((1,), (0,)), ((), ()))):
    return lax.dot_general(a, b, dims, preferred_element_type=jnp.float32)


def block_kernel(
    n_ts, n_dp, factor,
    kept_ref, kept_row, act_ref, cot_ref, vectors_ref, switch_hbm, expand_hbm, contract_hbm,
    token_ref, gate_ref, up_ref, down_ref,
    switch, expand, contract, w_sem,
    own, slots_f, slots, landed, wide, piece_f, zy, yz, scaled, p1_send, p1_recv, g_send, g_recv,
    pre_gate, pre_up, hidden_grad, gate_in, up_in, acts, hidden, term,
    pair, sib, x_first, x_last, y_first, y_last, y_sum, z_in, z_out, spread, rows_out, slots_out, back, back_f, term_f,
    sib_send, sib_recv, seen, total, n_send, n_recv, a_send, a_recv, x_send, x_recv, y_send, y_recv, z_send, z_recv, b_send, b_recv,
):
    bf16, f32 = jnp.bfloat16, jnp.float32
    nz = n_ts // NY
    nx = n_dp // 2
    me = lax.axis_index("ts")
    z, y = me // NY, lax.rem(me, NY)
    dp = lax.axis_index("dp")
    x, core = dp // 2, lax.rem(dp, 2)
    block, width = act_ref.shape
    tiles = width // LANES
    piece_rows = zy.shape[1]
    cap = n_ts * piece_rows
    hid = hidden.shape[1]
    pending = []

    def node(dz, dy):
        return lax.rem(z + dz + nz, nz) * NY + lax.rem(y + dy + NY, NY)

    def chip(dx):
        return lax.rem(x + dx + nx, nx) * 2 + core

    def copy_to(sems, index, src, dst, where):
        return pltpu.make_async_remote_copy(
            src, dst, sems[0].at[index], sems[1].at[index], device_id=where, device_id_type=MESH)

    def send(sems, index, src, dst, where):
        copy = copy_to(sems, index, src, dst, where)
        copy.start()
        pending.append(copy)

    def arrive(sems, index, dst):
        copy_to(sems, index, dst, dst, {"ts": me}).wait_recv()

    right, left = {"ts": node(0, 1)}, {"ts": node(0, -1)}
    up, down = {"ts": node(1, 0)}, {"ts": node(-1, 0)}
    ahead, behind = {"dp": chip(1)}, {"dp": chip(-1)}
    sibling = {"dp": x * 2 + 1 - core}

    barrier = pltpu.get_barrier_semaphore()

    @pl.loop(1, n_ts)
    def _(step):
        pl.semaphore_signal(barrier, inc=1, device_id={"ts": lax.rem(me + step, n_ts)}, device_id_type=MESH)

    @pl.loop(1, n_dp)
    def _(step):
        pl.semaphore_signal(barrier, inc=1, device_id={"dp": lax.rem(dp + step, n_dp)}, device_id_type=MESH)

    weight_copies = [
        pltpu.make_async_copy(src, dst, w_sem.at[i])
        for i, (src, dst) in enumerate(((switch_hbm, switch), (expand_hbm, expand), (contract_hbm, contract)))
    ]
    for copy in weight_copies:
        copy.start()

    kept = jnp.broadcast_to(kept_row[...], (block, cap))
    position = lax.broadcasted_iota(jnp.int32, (block, cap), 0) + block * me
    rank = jnp.sum((kept < position).astype(f32), axis=1, keepdims=True)
    routed = jnp.sum((kept == position).astype(f32), axis=1, keepdims=True)
    row_class = rank - n_ts * jnp.floor(rank * (1.0 / n_ts))
    classes = lax.broadcasted_iota(jnp.int32, (block, n_ts), 1).astype(f32)
    chosen = jnp.where(classes == row_class, routed, 0.0).astype(bf16)
    own[...] = dot(chosen, act_ref[...], ROWS_BY_ROWS)
    own_cot = dot(chosen, cot_ref[...], ROWS_BY_ROWS)
    for t in range(tiles):
        slots_f[:, t, :] = own[:, t * LANES:(t + 1) * LANES]
        slots_f[:, tiles + t, :] = own_cot[:, t * LANES:(t + 1) * LANES]

    @pl.loop(0, n_ts)
    def _(c):
        slots[c] = slots_f[c].astype(bf16)

    pl.semaphore_wait(barrier, n_ts - 1 + n_dp - 1)


    def p1_copy(step):
        to = lax.rem(me + step, n_ts)
        return pltpu.make_async_remote_copy(
            slots.at[to], landed.at[me], p1_send.at[step], p1_recv.at[step],
            device_id={"ts": to}, device_id_type=MESH)

    @pl.loop(1, n_ts)
    def _(step):
        p1_copy(step).start()

    landed[me] = slots[me]

    @pl.loop(1, n_ts)
    def _(step):
        source = lax.rem(me - step + n_ts, n_ts)
        pltpu.make_async_remote_copy(
            slots.at[source], landed.at[source], p1_send.at[step], p1_recv.at[step],
            device_id={"ts": source}, device_id_type=MESH).wait_recv()


    for k in range(piece_rows):
        wide[k] = landed[kept_ref[0, n_ts * k + me] // block].astype(f32)
    for t in range(2 * tiles):
        piece_f[:, t * LANES:(t + 1) * LANES] = wide[:, t, :]

    gain = vectors_ref[0:1, :].astype(f32)
    scorer = vectors_ref[1:2, :].astype(f32)
    row_f = piece_f[:, :width]
    inv_rms = lax.rsqrt(jnp.sum(row_f * row_f, axis=1, keepdims=True) * (1.0 / width) + epsilon)
    weight = jax.nn.sigmoid(jnp.sum(row_f * scorer, axis=1, keepdims=True))
    zy[me, :, :width] = (row_f * inv_rms * gain).astype(bf16)
    scaled_rows = (weight * piece_f[:, width:]).astype(bf16)
    yz[me] = scaled_rows[:, : yz.shape[2]]
    zy[me, :, width:] = scaled_rows[:, yz.shape[2] :]


    g_sems = (g_send, g_recv)

    def cut(buffer, which):
        first = -(-buffer.shape[2] // (2 * LANES)) * LANES
        return pl.ds(0, first) if which == 0 else pl.ds(first, buffer.shape[2] - first)

    def piece(buffer, n, which=None):
        return buffer.at[n] if which is None else buffer.at[n, :, cut(buffer, which)]

    def group(dz, which):
        return yz.at[pl.ds(lax.rem(z + dz + nz, nz) * NY + which * (NY // 2), NY // 2)]

    def share(index, ref, where):
        send(g_sems, index, ref, ref, where)

    B1, A1, B2, A2, A3 = 0, 4, 12, 26, 42

    def b1_start():
        share(B1 + 0, piece(yz, me), right)
        share(B1 + 1, piece(yz, me), left)

    def b1_relay():
        arrive(g_sems, B1 + 0, piece(yz, node(0, -1)))
        share(B1 + 2, piece(yz, node(0, -1), 0), right)
        arrive(g_sems, B1 + 1, piece(yz, node(0, 1)))
        share(B1 + 3, piece(yz, node(0, 1), 1), left)

    def b1_end():
        arrive(g_sems, B1 + 2, piece(yz, node(0, -2), 0))
        arrive(g_sems, B1 + 3, piece(yz, node(0, 2), 1))

    def a1_start():
        share(A1 + 0, piece(zy, me), up)
        share(A1 + 1, piece(zy, me), down)

    def fan_out(j):
        dz = Z_STEPS[j]
        share(A2 + 2 * j, piece(zy, node(dz, 0)), right)
        share(A2 + 2 * j + 1, piece(zy, node(dz, 0)), left)

    def relay(j):
        dz = Z_STEPS[j]
        arrive(g_sems, A2 + 2 * j, piece(zy, node(dz, -1)))
        share(A3 + 2 * j, piece(zy, node(dz, -1), 0), right)
        arrive(g_sems, A2 + 2 * j + 1, piece(zy, node(dz, 1)))
        share(A3 + 2 * j + 1, piece(zy, node(dz, 1), 1), left)

    def last(j):
        arrive(g_sems, A3 + 2 * j, piece(zy, node(Z_STEPS[j], -2), 0))
        arrive(g_sems, A3 + 2 * j + 1, piece(zy, node(Z_STEPS[j], 2), 1))

    def along(s):
        which = (0, 1) if s == 4 else (None, None)
        further = (0, 1) if s == 3 else (None, None)
        for way, to, sign in ((0, up, -1), (1, down, 1)):
            arrive(g_sems, A1 + 2 * (s - 1) + way, piece(zy, node(sign * s, 0), which[way]))
            if s < 4:
                share(A1 + 2 * s + way, piece(zy, node(sign * s, 0), further[way]), to)
        if s < 4:
            fan_out(2 * s - 1)
            fan_out(2 * s)
        else:
            fan_out(7)

    def b2_start():
        for which in range(2):
            share(B2 + 2 * which, group(0, which), up)
            share(B2 + 2 * which + 1, group(0, which), down)

    def groups(s):
        for which in range(2):
            for way, to, sign in ((0, up, -1), (1, down, 1)):
                if s == 4 and way != which:
                    continue
                index = B2 + 12 + way if s == 4 else B2 + 4 * (s - 1) + 2 * which + way
                arrive(g_sems, index, group(sign * s, which))
                if s < 3:
                    share(B2 + 4 * s + 2 * which + way, group(sign * s, which), to)
                elif s == 3 and way == which:
                    share(B2 + 12 + way, group(sign * s, which), to)

    window = seen.shape[3]
    pair_width = 2 * width // n_dp

    def window_at(to):
        return pl.multiple_of(to // 2 * pair_width + lax.rem(to, 2) * (pair_width - window), LANES)

    def seen_copy(j, step):
        n = pl.ds(lax.rem(z + Z_STEPS[j] + nz, nz) * NY, NY)
        to = lax.rem(dp + step, n_dp)
        index = (step - 1) * nz + j
        return pltpu.make_async_remote_copy(
            zy.at[n, :, pl.ds(window_at(to), window)], seen.at[dp, n], n_send.at[index], n_recv.at[index],
            device_id={"dp": to}, device_id_type=MESH)

    def show(j):
        @pl.loop(1, n_dp)
        def _(step):
            seen_copy(j, step).start()

    def seen_wait(j):
        n = pl.ds(lax.rem(z + Z_STEPS[j] + nz, nz) * NY, NY)

        @pl.loop(1, n_dp)
        def _(step):
            index = (step - 1) * nz + j
            source = lax.rem(dp - step + n_dp, n_dp)
            arrive((n_send, n_recv), index, seen.at[source, n])
            seen_copy(j, step).wait_send()

    steps = dict(
        b1_start=b1_start, b1_relay=b1_relay, b1_end=b1_end, a1_start=a1_start, b2_start=b2_start)
    for step in AG_ORDER:
        if isinstance(step, str):
            steps[step]()
        else:
            (fan_out, relay, last, along, groups, show)["frlagn".index(step[0])](step[1])

    def columns(buffer, start, size):
        return buffer[:, :, pl.ds(start, size)].reshape(cap, size)


    for copy in weight_copies:
        copy.wait()
    pre_gate[...] = jnp.zeros_like(pre_gate)
    pre_up[...] = jnp.zeros_like(pre_up)
    hidden_grad[...] = jnp.zeros_like(hidden_grad)

    @pl.loop(0, width // K_TILE)
    def _(k):
        at = pl.ds(pl.multiple_of(k * K_TILE, K_TILE), K_TILE)
        normed = columns(zy, pl.multiple_of(k * K_TILE, K_TILE), K_TILE)
        pre_gate[...] += dot(normed, switch[:, at], COLS_BY_COLS)
        pre_up[...] += dot(normed, expand[:, at], COLS_BY_COLS)

    for p in range(n_dp // 2):
        at = pl.ds(p * pair_width, pair_width)
        if p < n_dp // 2 - 1:
            scaled[:, at] = columns(yz, p * pair_width, pair_width)
        else:
            scaled[:, at] = columns(zy, width, pair_width)
        hidden_grad[...] += dot(scaled[:, at], contract[:, at], COLS_BY_COLS)

    @pl.loop(0, nz)
    def _(i):
        n = cap // nz
        at = pl.ds(pl.multiple_of(i * n, n), n)
        gelu_out, slope_out = gelu_pair(pre_gate[at, :])
        up_value, grad = pre_up[at, :], hidden_grad[at, :]
        hidden_value = (gelu_out * up_value).astype(bf16)
        hidden[at, :] = hidden_value
        gate_value = (grad * up_value * slope_out).astype(bf16)
        up_back = (grad * gelu_out).astype(bf16)
        gate_in[at, :] = gate_value
        up_in[at, :] = up_back
        acts[dp, at, :hid] = gate_value
        acts[dp, at, hid:] = up_back
        router = jnp.sum(hidden_value.astype(f32) * grad, axis=1, keepdims=True)
        term[i, :, :, width:] = jnp.broadcast_to(router, (n, LANES)).astype(bf16).reshape(NY, piece_rows, LANES)


    a_sems = (a_send, a_recv)
    halves = (pl.ds(0, cap // 2), pl.ds(cap // 2, cap // 2))

    def other(dx):
        return lax.rem(x + dx + nx, nx) * 2 + 1 - core

    def part(q, which):
        return acts.at[q, halves[which]]

    def pass_on(index, ref, where):
        send(a_sems, index, ref, ref, where)

    def acts_start():
        pass_on(0, part(dp, 0), ahead)
        pass_on(2, part(dp, 1), behind)
        pass_on(1, part(dp, 1), ahead)
        pass_on(3, part(dp, 0), behind)
        pass_on(6, acts.at[dp], sibling)

    def acts_relay():
        arrive(a_sems, 0, part(chip(-1), 0))
        pass_on(4, part(chip(-1), 0), ahead)
        pass_on(7, part(chip(-1), 0), sibling)
        arrive(a_sems, 2, part(chip(1), 1))
        pass_on(5, part(chip(1), 1), behind)
        pass_on(10, part(chip(1), 1), sibling)

    def acts_near():
        arrive(a_sems, 1, part(chip(-1), 1))
        pass_on(8, part(chip(-1), 1), sibling)
        arrive(a_sems, 3, part(chip(1), 0))
        pass_on(9, part(chip(1), 0), sibling)

    def acts_far():
        arrive(a_sems, 4, part(chip(2), 0))
        pass_on(11, part(chip(2), 0), sibling)
        arrive(a_sems, 5, part(chip(2), 1))
        pass_on(12, part(chip(2), 1), sibling)

    def grow(q):
        total[...] += dot(seen[q].reshape(cap, window), acts[q], ROWS_BY_ROWS)

    def grow_own():
        total[...] = dot(columns(zy, window_at(dp), window), acts[dp], ROWS_BY_ROWS)
        arrive(a_sems, 6, acts.at[other(0)])
        grow(other(0))

    def grow_near():
        for dx, index in ((-1, 7), (1, 9)):
            grow(chip(dx))
            arrive(a_sems, index, part(other(dx), 0))
            arrive(a_sems, index + 1, part(other(dx), 1))
            grow(other(dx))

    def grow_far():
        grow(chip(2))
        arrive(a_sems, 11, part(other(2), 0))
        arrive(a_sems, 12, part(other(2), 1))
        grow(other(2))
        here = pl.ds(pl.multiple_of(core * (window - rows), 8), rows)
        gate_ref[...] = (factor * total[here, :hid]).astype(bf16)
        up_ref[...] = (factor * total[here, hid:]).astype(bf16)

    sib_sems, x_sems, y_sems = (sib_send, sib_recv), (x_send, x_recv), (y_send, y_recv)
    z_sems = (z_send, z_recv)
    rows = width // n_dp
    quarter = hid // 4
    order = (2, 1, -1, 0)

    def partials(j):
        start = pl.multiple_of(lax.rem(x + order[j] + nx, nx) * pair_width, LANES)
        both = (factor * dot(hidden[...], scaled[:, pl.ds(start, pair_width)], ROWS_BY_ROWS)).astype(bf16)
        pair[j, 0] = both[:, :rows]
        pair[j, 1] = both[:, rows:]
        for q in range(4):
            at = pl.ds(q * quarter, quarter)
            send(sib_sems, 4 * j + q, pair.at[j, 1 - core, at], sib.at[j, at], sibling)

    def add(j, q, others, store):
        arrive(sib_sems, 4 * j + q, sib.at[j, pl.ds(q * quarter, quarter)])
        here = pl.ds(q * quarter, quarter)
        value = pair[j, core, here, :].astype(f32) + sib[j, here, :].astype(f32)
        for ref, start in others:
            value += ref[pl.ds(start, quarter), :].astype(f32)
        store(here, value.astype(bf16))

    def in_place(j):
        def store(here, value):
            sib[j, here, :] = value
        return store

    def chunk(ref, q):
        return ref.at[pl.ds(q * quarter, quarter)]

    def x_start():
        for q in (0, 2, 1, 3):
            add(0, q, (), in_place(0))
            way = q // 2
            send(x_sems, q, chunk(sib.at[0], q), x_first.at[way, pl.ds((q % 2) * quarter, quarter)],
                 (ahead, behind)[way])
        for q in range(2):
            add(1, 2 + q, (), in_place(1))
            send(x_sems, 4 + q, chunk(sib.at[1], 2 + q), chunk(x_last.at[0], 2 + q), ahead)
            add(2, q, (), in_place(2))
            send(x_sems, 6 + q, chunk(sib.at[2], q), chunk(x_last.at[1], q), behind)

    def x_second():
        for q in range(2):
            arrive(x_sems, q, x_first.at[0, pl.ds(q * quarter, quarter)])
            add(1, q, ((x_first.at[0], q * quarter),), in_place(1))
            send(x_sems, 8 + q, chunk(sib.at[1], q), chunk(x_last.at[0], q), ahead)
            arrive(x_sems, 2 + q, x_first.at[1, pl.ds(q * quarter, quarter)])
            add(2, 2 + q, ((x_first.at[1], q * quarter),), in_place(2))
            send(x_sems, 10 + q, chunk(sib.at[2], 2 + q), chunk(x_last.at[1], 2 + q), behind)

    def x_end():
        def store_out(here, value):
            down_ref[here, :] = value

        for q in (2, 3, 0, 1):
            for way in range(2):
                index = (8 + q, 6 + q)[way] if q < 2 else (2 + q, 8 + q)[way]
                arrive(x_sems, index, chunk(x_last.at[way], q))
            add(3, q, ((x_last.at[0], q * quarter), (x_last.at[1], q * quarter)), store_out)

    wide_row = y_sum.shape[2]
    middle = -(-wide_row // (2 * LANES)) * LANES
    cols = (pl.ds(0, middle), pl.ds(middle, wide_row - middle))

    def terms():
        @pl.loop(0, width // K_TILE)
        def _(k):
            at = pl.ds(pl.multiple_of(k * K_TILE, K_TILE), K_TILE)
            value = dot(gate_in[...], switch[:, at]) + dot(up_in[...], expand[:, at])
            term[:, :, :, at] = value.astype(bf16).reshape(nz, NY, piece_rows, K_TILE)

    def at_z(i):
        return lax.rem(z + i, nz)

    def at_y(dy):
        return lax.rem(y + dy + NY, NY)

    def y_start(i):
        opposite = term.at[at_z(i), at_y(2)]
        send(y_sems, 6 * i, opposite.at[:, cols[0]], y_first.at[i, :, cols[0]], right)
        send(y_sems, 6 * i + 1, opposite.at[:, cols[1]], y_first.at[i, :, cols[1]], left)
        send(y_sems, 6 * i + 2, term.at[at_z(i), at_y(1), :, cols[1]], y_last.at[0, i, :, cols[1]], right)
        send(y_sems, 6 * i + 3, term.at[at_z(i), at_y(-1), :, cols[0]], y_last.at[1, i, :, cols[0]], left)

    def y_second(i):
        for way, dy, to in ((0, 1, right), (1, -1, left)):
            arrive(y_sems, 6 * i + way, y_first.at[i, :, cols[way]])
            value = term[at_z(i), at_y(dy), :, cols[way]].astype(f32) + y_first[i, :, cols[way]].astype(f32)
            y_first[i, :, cols[way]] = value.astype(bf16)
            send(y_sems, 6 * i + 4 + way, y_first.at[i, :, cols[way]], y_last.at[way, i, :, cols[way]], to)

    def y_end(i):
        for way in range(2):
            arrive(y_sems, 6 * i + 2 + way, y_last.at[way, i, :, cols[1 - way]])
            arrive(y_sems, 6 * i + 4 + way, y_last.at[way, i, :, cols[way]])
        value = term[at_z(i), y].astype(f32) + y_last[0, i].astype(f32)
        y_sum[i] = (value + y_last[1, i].astype(f32)).astype(bf16)

    def z_step(s):
        for way, to in ((0, up), (1, down)):
            mine = 4 - s if way == 0 else 4 + s
            if s == 0:
                send(z_sems, way, y_sum.at[4, :, cols[way]], z_in.at[way, 0, :, cols[way]], to)
                continue
            if s == 1:
                arrive(z_sems, way, z_in.at[way, 0, :, cols[way]])
                z_out[way, s] = y_sum[mine]
                both = y_sum[mine, :, cols[way]].astype(f32) + z_in[way, 0, :, cols[way]].astype(f32)
                z_out[way, s, :, cols[way]] = both.astype(bf16)
            else:
                arrive(z_sems, 2 * (s - 1) + way, z_in.at[way, s - 1])
                z_out[way, s] = (y_sum[mine].astype(f32) + z_in[way, s - 1].astype(f32)).astype(bf16)
            send(z_sems, 2 * s + way, z_out.at[way, s], z_in.at[way, s], to)

    def back_copy(step):
        to = lax.rem(me + step, n_ts)
        return pltpu.make_async_remote_copy(
            slots_out.at[to], back.at[me], b_send.at[step], b_recv.at[step],
            device_id={"ts": to}, device_id_type=MESH)

    def back_start():
        for way in range(2):
            arrive(z_sems, 6 + way, z_in.at[way, 3])
        spread[...] = jnp.zeros_like(spread)
        for t in range(wide_row // LANES):
            at = pl.ds(t * LANES, LANES)
            value = y_sum[0, :, at].astype(f32) + z_in[0, 3, :, at].astype(f32)
            spread[:, t, :] = value + z_in[1, 3, :, at].astype(f32)
        for k in range(piece_rows):
            rows_out[k] = spread[k].astype(bf16)

        @pl.loop(0, n_ts)
        def _(h):
            pick = 0
            for k in range(1, piece_rows):
                pick = jnp.where(kept_ref[0, n_ts * k + me] // block == h, k, pick)
            slots_out[h] = rows_out[pick]

        @pl.loop(1, n_ts)
        def _(step):
            back_copy(step).start()

        back[me] = slots_out[me]

    def back_end():
        @pl.loop(1, n_ts)
        def _(step):
            source = lax.rem(me - step + n_ts, n_ts)
            pltpu.make_async_remote_copy(
                slots_out.at[source], back.at[source], b_send.at[step], b_recv.at[step],
                device_id={"ts": source}, device_id_type=MESH).wait_recv()

        @pl.loop(0, n_ts)
        def _(c):
            back_f[c] = back[c].astype(f32)

        for t in range(tiles):
            term_f[:, t * LANES:(t + 1) * LANES] = back_f[:, t, :]
        summed_dot = back_f[:, tiles, :][:, :1]
        own_f = own[...]
        own_inv = lax.rsqrt(jnp.sum(own_f * own_f, axis=1, keepdims=True) * (1.0 / width) + epsilon)
        own_weight = jax.nn.sigmoid(jnp.sum(own_f * scorer, axis=1, keepdims=True))
        unit = own_f * own_inv
        gained = term_f[...] * gain
        mean = jnp.sum(gained * unit, axis=1, keepdims=True) * (1.0 / width)
        row_grad = own_inv * (gained - unit * mean) + ((1.0 - own_weight) * summed_dot) * scorer
        token_ref[...] = dot(chosen, row_grad.astype(bf16)).astype(bf16)

    def seen_end():
        for j in range(nz):
            seen_wait(j)

    jobs = dict(
        acts_start=acts_start, acts_relay=acts_relay, acts_near=acts_near, acts_far=acts_far, grow_own=grow_own,
        grow_near=grow_near, grow_far=grow_far, x_start=x_start, x_second=x_second, x_end=x_end, terms=terms,
        back_start=back_start, back_end=back_end, seen_end=seen_end)
    for job in RS_ORDER:
        if isinstance(job, str):
            jobs[job]()
        else:
            (partials, y_start, y_second, y_end, z_step)["pysez".index(job[0])](job[1])

    @pl.loop(1, n_ts)
    def _(step):
        p1_copy(step).wait_send()
        back_copy(step).wait_send()

    for copy in pending:
        copy.wait_send()


def store_kernel(*refs):
    sems = refs[-1]
    count = (len(refs) - 1) // 2
    copies = [pltpu.make_async_copy(refs[i], refs[count + i], sems.at[i]) for i in range(count)]
    for copy in copies:
        copy.start()
    for copy in copies:
        copy.wait()


def store_results(*results):
    hbm = pl.BlockSpec(memory_space=pl.ANY)
    return pl.pallas_call(
        store_kernel,
        out_shape=tuple(jax.ShapeDtypeStruct(r.shape, r.dtype) for r in results),
        in_specs=[hbm] * len(results),
        out_specs=(hbm,) * len(results),
        scratch_shapes=[pltpu.SemaphoreType.DMA((len(results),))],
        name="store_results",
    )(*results)


def local(
    block_activity, result_cotangent, kept_locations, prenormal_scaling, scorer_matrix,
    switch_matrix, expand_matrix, contract_matrix,
):
    n_ts, n_dp = lax.axis_size("ts"), lax.axis_size("dp")
    nz = n_ts // NY
    block, width = block_activity.shape[1:]
    cap = kept_locations.shape[1]
    hid = switch_matrix.shape[1]
    rows = width // n_dp
    piece = cap // n_ts
    tiles = width // LANES
    window = -(-rows // LANES) * LANES
    pad = -(-(tiles + 1) // 16) * 16
    bf16, f32, dma = jnp.bfloat16, jnp.float32, pltpu.SemaphoreType.DMA
    vmem = pl.BlockSpec(memory_space=pltpu.VMEM)
    hbm = pl.BlockSpec(memory_space=pl.ANY)
    token, gate, up, down = pl.pallas_call(
        functools.partial(block_kernel, n_ts, n_dp, (n_dp * cap) ** (-0.5)),
        out_shape=(
            jax.ShapeDtypeStruct((block, width), bf16),
            jax.ShapeDtypeStruct((rows, hid), bf16),
            jax.ShapeDtypeStruct((rows, hid), bf16),
            jax.ShapeDtypeStruct((hid, rows), bf16),
        ),
        in_specs=[pl.BlockSpec(memory_space=pltpu.SMEM)] + [vmem] * 4 + [hbm] * 3,
        out_specs=(vmem,) * 4,
        scratch_shapes=[
            pltpu.VMEM((hid, width), bf16), pltpu.VMEM((hid, width), bf16), pltpu.VMEM((hid, width), bf16), dma((3,)),
            pltpu.VMEM((n_ts, width), f32),
            pltpu.VMEM((n_ts, 2 * tiles, LANES), f32),
            pltpu.VMEM((n_ts, 2 * tiles, LANES), bf16),
            pltpu.VMEM((n_ts, 2 * tiles, LANES), bf16),
            pltpu.VMEM((piece, 2 * tiles, LANES), f32),
            pltpu.VMEM((piece, 2 * width), f32),
            pltpu.VMEM((n_ts, piece, width + 2 * rows), bf16),
            pltpu.VMEM((n_ts, piece, width - 2 * rows), bf16),
            pltpu.VMEM((cap, width), bf16),
            dma((n_ts,)), dma((n_ts,)), dma((58,)), dma((58,)),
            pltpu.VMEM((cap, hid), f32), pltpu.VMEM((cap, hid), f32), pltpu.VMEM((cap, hid), f32),
            pltpu.VMEM((cap, hid), bf16), pltpu.VMEM((cap, hid), bf16), pltpu.VMEM((n_dp, cap, 2 * hid), bf16),
            pltpu.VMEM((cap, hid), bf16),
            pltpu.VMEM((nz, NY, piece, width + LANES), bf16),
            pltpu.VMEM((4, 2, hid, rows), bf16),
            pltpu.VMEM((4, hid, rows), bf16),
            pltpu.VMEM((2, hid // 2, rows), bf16),
            pltpu.VMEM((2, hid, rows), bf16),
            pltpu.VMEM((nz, piece, width + LANES), bf16),
            pltpu.VMEM((2, nz, piece, width + LANES), bf16),
            pltpu.VMEM((nz, piece, width + LANES), bf16),
            pltpu.VMEM((2, 4, piece, width + LANES), bf16),
            pltpu.VMEM((2, 4, piece, width + LANES), bf16),
            pltpu.VMEM((piece, pad, LANES), f32),
            pltpu.VMEM((piece, pad, LANES), bf16),
            pltpu.VMEM((n_ts, pad, LANES), bf16),
            pltpu.VMEM((n_ts, pad, LANES), bf16),
            pltpu.VMEM((n_ts, pad, LANES), f32),
            pltpu.VMEM((n_ts, width), f32),
            dma((16,)), dma((16,)),
            pltpu.VMEM((n_dp, n_ts, piece, window), bf16),
            pltpu.VMEM((window, 2 * hid), f32),
            dma((n_dp * nz,)), dma((n_dp * nz,)), dma((13,)), dma((13,)),
            dma((12,)), dma((12,)), dma((6 * nz,)), dma((6 * nz,)),
            dma((8,)), dma((8,)), dma((n_ts,)), dma((n_ts,)),
        ],
        compiler_params=pltpu.CompilerParams(
            collective_id=0, has_side_effects=True, vmem_limit_bytes=56 * 1024 * 1024),
        name="block_backward",
    )(
        kept_locations, kept_locations, block_activity[0], result_cotangent[0],
        jnp.stack([prenormal_scaling, scorer_matrix]), switch_matrix.T, expand_matrix.T, contract_matrix,
    )
    return store_results(token[None], gate, up, down)


def solution(mesh):
    in_specs = (
        P("dp", "ts", None), P("dp", "ts", None), P("dp", None), P(), P(),
        P(None, "ts"), P(None, "ts"), P("ts", None),
    )
    out_specs = (P("dp", "ts", None), P("dp", "ts"), P("dp", "ts"), P("ts", "dp"))
    return jax.shard_map(local, mesh=mesh, in_specs=in_specs, out_specs=out_specs, check_vma=False)
```

```python
import functools
import math

import jax
import jax.numpy as jnp
from jax import lax
from jax.experimental import pallas as pl
from jax.experimental.pallas import tpu as pltpu
from jax.sharding import PartitionSpec as P

MESH = pl.DeviceIdType.MESH
NY = 4
RS_ORDER = (
    "acts_start", "terms", ("y", 4), ("y", 3), ("y", 5), ("p", 0), ("p", 1), ("p", 2), ("p", 3), ("s", 4),
    ("y", 2), ("y", 6), "x_start", ("s", 3), ("s", 5), "acts_relay", ("e", 4), ("z", 0), ("y", 1), ("y", 7), ("y", 0),
    ("s", 2), ("s", 6), ("e", 3), ("e", 5), ("z", 1), ("s", 1), ("s", 7), ("e", 2), ("e", 6), ("z", 2), "seen_end",
    "grow_own", ("s", 0), ("e", 1), ("e", 7), ("z", 3), ("e", 0), "grow_near", "x_second", "back_start",
    "grow_far", "back_end", "grow_end", "x_end",
)
AG_ORDER = (
    "b1_start", "a1_start", ("f", 0), "b1_relay", ("a", 1), "b1_end", "b2_start", ("a", 2), ("r", 0), ("a", 3),
    ("r", 1), ("l", 0), ("r", 2), ("g", 1), ("l", 1), ("a", 4), ("r", 3), ("l", 2),
    ("r", 4), ("g", 2), ("l", 3), ("r", 5), ("l", 4), ("r", 6), ("l", 5),
    ("r", 7), ("l", 6), ("g", 3), ("l", 7), "pre", ("g", 4),
)
Z_STEPS = (0, -1, 1, -2, 2, -3, 3, 4)
LANES = 128
K_TILE = 512
epsilon = 1e-06
gelu_scale = math.sqrt(2.0 / math.pi)
ROWS_BY_ROWS = (((0,), (0,)), ((), ()))
COLS_BY_COLS = (((1,), (1,)), ((), ()))


def gelu_pair(pre_act):
    cubic = pre_act + 0.044715 * pre_act * pre_act * pre_act
    tanh_part = jnp.tanh(gelu_scale * cubic)
    gelu_out = 0.5 * pre_act * (1.0 + tanh_part)
    slope_out = 0.5 * (1.0 + tanh_part) + 0.5 * pre_act * (
        1.0 - tanh_part * tanh_part
    ) * gelu_scale * (1.0 + 3.0 * 0.044715 * pre_act * pre_act)
    return (gelu_out, slope_out)


def dot(a, b, dims=(((1,), (0,)), ((), ()))):
    return lax.dot_general(a, b, dims, preferred_element_type=jnp.float32)


def block_kernel(
    n_ts, n_dp, factor,
    kept_ref, kept_row, act_ref, cot_ref, vectors_ref, switch_hbm, expand_hbm, contract_hbm,
    token_ref, gate_ref, up_ref, down_ref,
    switch, expand, contract, w_sem,
    picks, own, slots_f, slots, landed, wide, piece_f, zy, yz, scaled, p1_send, p1_recv, g_send, g_recv,
    pre_gate, pre_up, hidden_grad, gate_in, up_in, acts, hidden, term,
    pair, sib, x_first, x_last, y_first, y_last, y_sum, z_in, z_out, spread, rows_out, slots_out, back, back_f, term_f,
    sib_send, sib_recv, seen, total, half_out, half_in, n_send, n_recv, a_send, a_recv, x_send, x_recv, y_send, y_recv, z_send, z_recv, b_send, b_recv,
):
    bf16, f32 = jnp.bfloat16, jnp.float32
    nz = n_ts // NY
    nx = n_dp // 2
    me = lax.axis_index("ts")
    z, y = me // NY, lax.rem(me, NY)
    dp = lax.axis_index("dp")
    x, core = dp // 2, lax.rem(dp, 2)
    block, width = act_ref.shape
    tiles = width // LANES
    piece_rows = zy.shape[1]
    cap = n_ts * piece_rows
    hid = hidden.shape[1]
    pending = []

    def node(dz, dy):
        return lax.rem(z + dz + nz, nz) * NY + lax.rem(y + dy + NY, NY)

    def chip(dx):
        return lax.rem(x + dx + nx, nx) * 2 + core

    def copy_to(sems, index, src, dst, where):
        return pltpu.make_async_remote_copy(
            src, dst, sems[0].at[index], sems[1].at[index], device_id=where, device_id_type=MESH)

    def send(sems, index, src, dst, where):
        copy = copy_to(sems, index, src, dst, where)
        copy.start()
        pending.append(copy)

    def arrive(sems, index, dst):
        copy_to(sems, index, dst, dst, {"ts": me}).wait_recv()

    right, left = {"ts": node(0, 1)}, {"ts": node(0, -1)}
    up, down = {"ts": node(1, 0)}, {"ts": node(-1, 0)}
    ahead, behind = {"dp": chip(1)}, {"dp": chip(-1)}
    sibling = {"dp": x * 2 + 1 - core}

    barrier = pltpu.get_barrier_semaphore()

    @pl.loop(1, n_ts)
    def _(step):
        pl.semaphore_signal(barrier, inc=1, device_id={"ts": lax.rem(me + step, n_ts)}, device_id_type=MESH)

    for where in (sibling, ahead, behind, {"dp": chip(2)}):
        pl.semaphore_signal(barrier, inc=1, device_id=where, device_id_type=MESH)

    weight_copies = [
        pltpu.make_async_copy(src, dst, w_sem.at[i])
        for i, (src, dst) in enumerate(((switch_hbm, switch), (expand_hbm, expand), (contract_hbm, contract)))
    ]
    for copy in weight_copies:
        copy.start()

    kept = jnp.broadcast_to(kept_row[...], (block, cap))
    position = lax.broadcasted_iota(jnp.int32, (block, cap), 0) + block * me
    rank = jnp.sum((kept < position).astype(f32), axis=1, keepdims=True)
    routed = jnp.sum((kept == position).astype(f32), axis=1, keepdims=True)
    row_class = rank - n_ts * jnp.floor(rank * (1.0 / n_ts))
    classes = lax.broadcasted_iota(jnp.int32, (block, n_ts), 1).astype(f32)
    chosen = jnp.where(classes == row_class, routed, 0.0).astype(bf16)
    own[...] = dot(chosen, act_ref[...], ROWS_BY_ROWS)
    own_cot = dot(chosen, cot_ref[...], ROWS_BY_ROWS)
    for t in range(tiles):
        slots_f[:, t, :] = own[:, t * LANES:(t + 1) * LANES]
        slots_f[:, tiles + t, :] = own_cot[:, t * LANES:(t + 1) * LANES]

    @pl.loop(0, n_ts)
    def _(c):
        slots[c] = slots_f[c].astype(bf16)

    pl.semaphore_wait(barrier, n_ts - 1 + 4)


    def p1_copy(step):
        to = lax.rem(me + step, n_ts)
        return pltpu.make_async_remote_copy(
            slots.at[to], landed.at[me], p1_send.at[step], p1_recv.at[step],
            device_id={"ts": to}, device_id_type=MESH)

    @pl.loop(1, n_ts)
    def _(step):
        p1_copy(step).start()

    landed[me] = slots[me]

    @pl.loop(0, n_ts)
    def _(h):
        pick = 0
        for k in range(1, piece_rows):
            pick = jnp.where(kept_ref[0, n_ts * k + me] // block == h, k, pick)
        picks[h] = pick

    @pl.loop(1, n_ts)
    def _(step):
        source = lax.rem(me - step + n_ts, n_ts)
        pltpu.make_async_remote_copy(
            slots.at[source], landed.at[source], p1_send.at[step], p1_recv.at[step],
            device_id={"ts": source}, device_id_type=MESH).wait_recv()


    for k in range(piece_rows):
        wide[k] = landed[kept_ref[0, n_ts * k + me] // block].astype(f32)
    for t in range(2 * tiles):
        piece_f[:, t * LANES:(t + 1) * LANES] = wide[:, t, :]

    gain = vectors_ref[0:1, :].astype(f32)
    scorer = vectors_ref[1:2, :].astype(f32)
    row_f = piece_f[:, :width]
    inv_rms = lax.rsqrt(jnp.sum(row_f * row_f, axis=1, keepdims=True) * (1.0 / width) + epsilon)
    weight = jax.nn.sigmoid(jnp.sum(row_f * scorer, axis=1, keepdims=True))
    zy[me, :, :width] = (row_f * inv_rms * gain).astype(bf16)
    scaled_rows = (weight * piece_f[:, width:]).astype(bf16)
    yz[me] = scaled_rows[:, : yz.shape[2]]
    zy[me, :, width:] = scaled_rows[:, yz.shape[2] :]


    g_sems = (g_send, g_recv)

    def cut(buffer, which):
        first = -(-buffer.shape[2] // (2 * LANES)) * LANES
        return pl.ds(0, first) if which == 0 else pl.ds(first, buffer.shape[2] - first)

    def piece(buffer, n, which=None):
        return buffer.at[n] if which is None else buffer.at[n, :, cut(buffer, which)]

    def group(dz, which):
        return yz.at[pl.ds(lax.rem(z + dz + nz, nz) * NY + which * (NY // 2), NY // 2)]

    def share(index, ref, where):
        send(g_sems, index, ref, ref, where)

    B1, A1, B2, A2, A3 = 0, 4, 12, 26, 42

    def b1_start():
        share(B1 + 0, piece(yz, me), right)
        share(B1 + 1, piece(yz, me), left)

    def b1_relay():
        arrive(g_sems, B1 + 0, piece(yz, node(0, -1)))
        share(B1 + 2, piece(yz, node(0, -1), 0), right)
        arrive(g_sems, B1 + 1, piece(yz, node(0, 1)))
        share(B1 + 3, piece(yz, node(0, 1), 1), left)

    def b1_end():
        arrive(g_sems, B1 + 2, piece(yz, node(0, -2), 0))
        arrive(g_sems, B1 + 3, piece(yz, node(0, 2), 1))

    def a1_start():
        share(A1 + 0, piece(zy, me), up)
        share(A1 + 1, piece(zy, me), down)
        show(0, 0)

    def fan_out(j):
        dz = Z_STEPS[j]
        share(A2 + 2 * j, piece(zy, node(dz, 0)), right)
        share(A2 + 2 * j + 1, piece(zy, node(dz, 0)), left)

    def relay(j):
        dz = Z_STEPS[j]
        arrive(g_sems, A2 + 2 * j, piece(zy, node(dz, -1)))
        share(A3 + 2 * j, piece(zy, node(dz, -1), 0), right)
        arrive(g_sems, A2 + 2 * j + 1, piece(zy, node(dz, 1)))
        share(A3 + 2 * j + 1, piece(zy, node(dz, 1), 1), left)
        show(dz, -1)
        show(dz, 1)

    def last(j):
        arrive(g_sems, A3 + 2 * j, piece(zy, node(Z_STEPS[j], -2), 0))
        arrive(g_sems, A3 + 2 * j + 1, piece(zy, node(Z_STEPS[j], 2), 1))
        show(Z_STEPS[j], 2)

    def along(s):
        which = (0, 1) if s == 4 else (None, None)
        further = (0, 1) if s == 3 else (None, None)
        for way, to, sign in ((0, up, -1), (1, down, 1)):
            arrive(g_sems, A1 + 2 * (s - 1) + way, piece(zy, node(sign * s, 0), which[way]))
            if s < 4:
                share(A1 + 2 * s + way, piece(zy, node(sign * s, 0), further[way]), to)
        if s < 4:
            fan_out(2 * s - 1)
            fan_out(2 * s)
            show(-s, 0)
            show(s, 0)
        else:
            fan_out(7)
            show(4, 0)

    def b2_start():
        for which in range(2):
            share(B2 + 2 * which, group(0, which), up)
            share(B2 + 2 * which + 1, group(0, which), down)

    def groups(s):
        for which in range(2):
            for way, to, sign in ((0, up, -1), (1, down, 1)):
                if s == 4 and way != which:
                    continue
                index = B2 + 12 + way if s == 4 else B2 + 4 * (s - 1) + 2 * which + way
                arrive(g_sems, index, group(sign * s, which))
                if s < 3:
                    share(B2 + 4 * s + 2 * which + way, group(sign * s, which), to)
                elif s == 3 and way == which:
                    share(B2 + 12 + way, group(sign * s, which), to)

    pair_width = 2 * width // n_dp
    far = (1, -1, 2)

    def seen_copy(rel, index):
        n = node(rel // NY, lax.rem(rel, NY))
        at = pl.ds(pl.multiple_of(lax.rem(x + far[index] + nx, nx) * pair_width, LANES), pair_width)
        return pltpu.make_async_remote_copy(
            zy.at[n, :, at], seen.at[x, n], n_send.at[index * n_ts + rel], n_recv.at[index * n_ts + rel],
            device_id={"dp": chip(far[index])}, device_id_type=MESH)

    def show(dz, dy):
        for index in range(3):
            seen_copy(dz % nz * NY + dy % NY, index).start()

    def seen_end():
        @pl.loop(0, n_ts)
        def _(rel):
            n = node(rel // NY, lax.rem(rel, NY))
            for index in range(3):
                arrive((n_send, n_recv), index * n_ts + rel, seen.at[lax.rem(x - far[index] + nx, nx), n])
                seen_copy(rel, index).wait_send()

    def columns(buffer, start, size):
        return buffer[:, :, pl.ds(start, size)].reshape(cap, size)

    def pre():
        for copy in weight_copies:
            copy.wait()
        pre_gate[...] = jnp.zeros_like(pre_gate)
        pre_up[...] = jnp.zeros_like(pre_up)

        @pl.loop(0, width // K_TILE)
        def _(k):
            at = pl.ds(pl.multiple_of(k * K_TILE, K_TILE), K_TILE)
            normed = columns(zy, pl.multiple_of(k * K_TILE, K_TILE), K_TILE)
            pre_gate[...] += dot(normed, switch[:, at], COLS_BY_COLS)
            pre_up[...] += dot(normed, expand[:, at], COLS_BY_COLS)

    steps = dict(
        pre=pre,        b1_start=b1_start, b1_relay=b1_relay, b1_end=b1_end, a1_start=a1_start, b2_start=b2_start)
    for step in AG_ORDER:
        if isinstance(step, str):
            steps[step]()
        else:
            (fan_out, relay, last, along, groups)["frlag".index(step[0])](step[1])

    hidden_grad[...] = jnp.zeros_like(hidden_grad)
    for p in range(n_dp // 2):
        at = pl.ds(p * pair_width, pair_width)
        if p < n_dp // 2 - 1:
            scaled[:, at] = columns(yz, p * pair_width, pair_width)
        else:
            scaled[:, at] = columns(zy, width, pair_width)
        hidden_grad[...] += dot(scaled[:, at], contract[:, at], COLS_BY_COLS)

    @pl.loop(0, nz)
    def _(i):
        n = cap // nz
        at = pl.ds(pl.multiple_of(i * n, n), n)
        gelu_out, slope_out = gelu_pair(pre_gate[at, :])
        up_value, grad = pre_up[at, :], hidden_grad[at, :]
        hidden_value = (gelu_out * up_value).astype(bf16)
        hidden[at, :] = hidden_value
        gate_value = (grad * up_value * slope_out).astype(bf16)
        up_back = (grad * gelu_out).astype(bf16)
        gate_in[at, :] = gate_value
        up_in[at, :] = up_back
        acts[x, at, :hid] = gate_value
        acts[x, at, hid:] = up_back
        router = jnp.sum(hidden_value.astype(f32) * grad, axis=1, keepdims=True)
        term[i, :, :, width:] = jnp.broadcast_to(router, (n, LANES)).astype(bf16).reshape(NY, piece_rows, LANES)


    a_sems = (a_send, a_recv)
    halves = (pl.ds(0, cap // 2), pl.ds(cap // 2, cap // 2))
    rows = width // n_dp

    def part(dx, which):
        return acts.at[lax.rem(x + dx + nx, nx), halves[which]]

    def pass_on(index, ref, where):
        send(a_sems, index, ref, ref, where)

    def acts_start():
        pass_on(0, part(0, 0), ahead)
        pass_on(2, part(0, 1), behind)
        pass_on(1, part(0, 1), ahead)
        pass_on(3, part(0, 0), behind)

    def acts_relay():
        arrive(a_sems, 0, part(-1, 0))
        pass_on(4, part(-1, 0), ahead)
        arrive(a_sems, 2, part(1, 1))
        pass_on(5, part(1, 1), behind)

    def grow(dx):
        at = lax.rem(x + dx + nx, nx)
        total[...] += dot(seen[at].reshape(cap, pair_width), acts[at], ROWS_BY_ROWS)

    def grow_own():
        start = pl.multiple_of(x * pair_width, LANES)
        total[...] = dot(columns(zy, start, pair_width), acts[x], ROWS_BY_ROWS)

    def grow_near():
        arrive(a_sems, 1, part(-1, 1))
        grow(-1)
        arrive(a_sems, 3, part(1, 0))
        grow(1)

    def grow_far():
        arrive(a_sems, 4, part(2, 0))
        arrive(a_sems, 5, part(2, 1))
        grow(2)
        theirs = pl.ds(pl.multiple_of((1 - core) * rows, 16), rows)
        half_out[...] = (factor * total[theirs, :]).astype(bf16)
        send(a_sems, 6, half_out, half_in, sibling)

    def grow_end():
        arrive(a_sems, 6, half_in)
        here = pl.ds(pl.multiple_of(core * rows, 16), rows)
        value = factor * total[here, :] + half_in[...].astype(f32)
        gate_ref[...] = value[:, :hid].astype(bf16)
        up_ref[...] = value[:, hid:].astype(bf16)

    sib_sems, x_sems, y_sems = (sib_send, sib_recv), (x_send, x_recv), (y_send, y_recv)
    z_sems = (z_send, z_recv)
    quarter = hid // 4
    order = (2, 1, -1, 0)

    def partials(j):
        start = pl.multiple_of(lax.rem(x + order[j] + nx, nx) * pair_width, LANES)
        both = (factor * dot(hidden[...], scaled[:, pl.ds(start, pair_width)], ROWS_BY_ROWS)).astype(bf16)
        pair[j, 0] = both[:, :rows]
        pair[j, 1] = both[:, rows:]
        for q in range(4):
            at = pl.ds(q * quarter, quarter)
            send(sib_sems, 4 * j + q, pair.at[j, 1 - core, at], sib.at[j, at], sibling)

    def add(j, q, others, store):
        arrive(sib_sems, 4 * j + q, sib.at[j, pl.ds(q * quarter, quarter)])
        here = pl.ds(q * quarter, quarter)
        value = pair[j, core, here, :].astype(f32) + sib[j, here, :].astype(f32)
        for ref, start in others:
            value += ref[pl.ds(start, quarter), :].astype(f32)
        store(here, value.astype(bf16))

    def in_place(j):
        def store(here, value):
            sib[j, here, :] = value
        return store

    def chunk(ref, q):
        return ref.at[pl.ds(q * quarter, quarter)]

    def x_start():
        for q in (0, 2, 1, 3):
            add(0, q, (), in_place(0))
            way = q // 2
            send(x_sems, q, chunk(sib.at[0], q), x_first.at[way, pl.ds((q % 2) * quarter, quarter)],
                 (ahead, behind)[way])
        for q in range(2):
            add(1, 2 + q, (), in_place(1))
            send(x_sems, 4 + q, chunk(sib.at[1], 2 + q), chunk(x_last.at[0], 2 + q), ahead)
            add(2, q, (), in_place(2))
            send(x_sems, 6 + q, chunk(sib.at[2], q), chunk(x_last.at[1], q), behind)

    def x_second():
        for q in range(2):
            arrive(x_sems, q, x_first.at[0, pl.ds(q * quarter, quarter)])
            add(1, q, ((x_first.at[0], q * quarter),), in_place(1))
            send(x_sems, 8 + q, chunk(sib.at[1], q), chunk(x_last.at[0], q), ahead)
            arrive(x_sems, 2 + q, x_first.at[1, pl.ds(q * quarter, quarter)])
            add(2, 2 + q, ((x_first.at[1], q * quarter),), in_place(2))
            send(x_sems, 10 + q, chunk(sib.at[2], 2 + q), chunk(x_last.at[1], 2 + q), behind)

    def x_end():
        def store_out(here, value):
            down_ref[here, :] = value

        for q in (2, 3, 0, 1):
            for way in range(2):
                index = (8 + q, 6 + q)[way] if q < 2 else (2 + q, 8 + q)[way]
                arrive(x_sems, index, chunk(x_last.at[way], q))
            add(3, q, ((x_last.at[0], q * quarter), (x_last.at[1], q * quarter)), store_out)

    wide_row = y_sum.shape[2]
    middle = -(-wide_row // (2 * LANES)) * LANES
    cols = (pl.ds(0, middle), pl.ds(middle, wide_row - middle))

    def terms():
        @pl.loop(0, width // K_TILE)
        def _(k):
            at = pl.ds(pl.multiple_of(k * K_TILE, K_TILE), K_TILE)
            value = dot(gate_in[...], switch[:, at]) + dot(up_in[...], expand[:, at])
            term[:, :, :, at] = value.astype(bf16).reshape(nz, NY, piece_rows, K_TILE)

    def at_z(i):
        return lax.rem(z + i, nz)

    def at_y(dy):
        return lax.rem(y + dy + NY, NY)

    def y_start(i):
        opposite = term.at[at_z(i), at_y(2)]
        send(y_sems, 6 * i, opposite.at[:, cols[0]], y_first.at[i, :, cols[0]], right)
        send(y_sems, 6 * i + 1, opposite.at[:, cols[1]], y_first.at[i, :, cols[1]], left)
        send(y_sems, 6 * i + 2, term.at[at_z(i), at_y(1), :, cols[1]], y_last.at[0, i, :, cols[1]], right)
        send(y_sems, 6 * i + 3, term.at[at_z(i), at_y(-1), :, cols[0]], y_last.at[1, i, :, cols[0]], left)

    def y_second(i):
        for way, dy, to in ((0, 1, right), (1, -1, left)):
            arrive(y_sems, 6 * i + way, y_first.at[i, :, cols[way]])
            value = term[at_z(i), at_y(dy), :, cols[way]].astype(f32) + y_first[i, :, cols[way]].astype(f32)
            y_first[i, :, cols[way]] = value.astype(bf16)
            send(y_sems, 6 * i + 4 + way, y_first.at[i, :, cols[way]], y_last.at[way, i, :, cols[way]], to)

    def y_end(i):
        for way in range(2):
            arrive(y_sems, 6 * i + 2 + way, y_last.at[way, i, :, cols[1 - way]])
            arrive(y_sems, 6 * i + 4 + way, y_last.at[way, i, :, cols[way]])
        value = term[at_z(i), y].astype(f32) + y_last[0, i].astype(f32)
        y_sum[i] = (value + y_last[1, i].astype(f32)).astype(bf16)

    def z_step(s):
        for way, to in ((0, up), (1, down)):
            mine = 4 - s if way == 0 else 4 + s
            if s == 0:
                send(z_sems, way, y_sum.at[4, :, cols[way]], z_in.at[way, 0, :, cols[way]], to)
                continue
            if s == 1:
                arrive(z_sems, way, z_in.at[way, 0, :, cols[way]])
                z_out[way, s] = y_sum[mine]
                both = y_sum[mine, :, cols[way]].astype(f32) + z_in[way, 0, :, cols[way]].astype(f32)
                z_out[way, s, :, cols[way]] = both.astype(bf16)
            else:
                arrive(z_sems, 2 * (s - 1) + way, z_in.at[way, s - 1])
                z_out[way, s] = (y_sum[mine].astype(f32) + z_in[way, s - 1].astype(f32)).astype(bf16)
            send(z_sems, 2 * s + way, z_out.at[way, s], z_in.at[way, s], to)

    def back_copy(step):
        to = lax.rem(me + step, n_ts)
        return pltpu.make_async_remote_copy(
            slots_out.at[to], back.at[me], b_send.at[step], b_recv.at[step],
            device_id={"ts": to}, device_id_type=MESH)

    def z_end():
        for way in range(2):
            arrive(z_sems, 6 + way, z_in.at[way, 3])

    def back_start():
        z_end()
        spread[...] = jnp.zeros_like(spread)
        for t in range(wide_row // LANES):
            at = pl.ds(t * LANES, LANES)
            value = y_sum[0, :, at].astype(f32) + z_in[0, 3, :, at].astype(f32)
            spread[:, t, :] = value + z_in[1, 3, :, at].astype(f32)
        for k in range(piece_rows):
            rows_out[k] = spread[k].astype(bf16)

        @pl.loop(0, n_ts)
        def _(h):
            slots_out[h] = rows_out[picks[h]]

        @pl.loop(1, n_ts)
        def _(step):
            back_copy(step).start()

        back[me] = slots_out[me]

    def back_end():
        @pl.loop(1, n_ts)
        def _(step):
            source = lax.rem(me - step + n_ts, n_ts)
            pltpu.make_async_remote_copy(
                slots_out.at[source], back.at[source], b_send.at[step], b_recv.at[step],
                device_id={"ts": source}, device_id_type=MESH).wait_recv()
            back_copy(step).wait_send()

        @pl.loop(0, n_ts)
        def _(c):
            back_f[c] = back[c].astype(f32)

        for t in range(tiles):
            term_f[:, t * LANES:(t + 1) * LANES] = back_f[:, t, :]
        summed_dot = back_f[:, tiles, :][:, :1]
        own_f = own[...]
        own_inv = lax.rsqrt(jnp.sum(own_f * own_f, axis=1, keepdims=True) * (1.0 / width) + epsilon)
        own_weight = jax.nn.sigmoid(jnp.sum(own_f * scorer, axis=1, keepdims=True))
        unit = own_f * own_inv
        gained = term_f[...] * gain
        mean = jnp.sum(gained * unit, axis=1, keepdims=True) * (1.0 / width)
        row_grad = own_inv * (gained - unit * mean) + ((1.0 - own_weight) * summed_dot) * scorer
        token_ref[...] = dot(chosen, row_grad.astype(bf16)).astype(bf16)

    jobs = dict(
        acts_start=acts_start, acts_relay=acts_relay, grow_own=grow_own, grow_near=grow_near, grow_far=grow_far,
        grow_end=grow_end, x_start=x_start, x_second=x_second, x_end=x_end, terms=terms, z_end=z_end, back_start=back_start, back_end=back_end, seen_end=seen_end)
    for job in RS_ORDER:
        if isinstance(job, str):
            jobs[job]()
        else:
            (partials, y_start, y_second, y_end, z_step)["pysez".index(job[0])](job[1])

    @pl.loop(1, n_ts)
    def _(step):
        p1_copy(step).wait_send()

    for copy in pending:
        copy.wait_send()


def store_kernel(*refs):
    count = (len(refs) - 2) // 3
    sems = refs[-2:]
    inward = [pltpu.make_async_copy(refs[i], refs[2 * count + i], sems[0].at[i]) for i in range(count)]
    outward = [pltpu.make_async_copy(refs[2 * count + i], refs[count + i], sems[1].at[i]) for i in range(count)]
    for copy in inward:
        copy.start()
    for first, second in zip(inward, outward):
        first.wait()
        second.start()
    for copy in outward:
        copy.wait()


def store_results(*results):
    hbm = pl.BlockSpec(memory_space=pl.ANY)
    return pl.pallas_call(
        store_kernel,
        out_shape=tuple(jax.ShapeDtypeStruct(r.shape, r.dtype) for r in results),
        in_specs=[hbm] * len(results),
        out_specs=(hbm,) * len(results),
        scratch_shapes=[pltpu.VMEM(r.shape, r.dtype) for r in results]
        + [pltpu.SemaphoreType.DMA((len(results),))] * 2,
        name="store_results",
    )(*results)


def local(
    block_activity, result_cotangent, kept_locations, prenormal_scaling, scorer_matrix,
    switch_matrix, expand_matrix, contract_matrix,
):
    n_ts, n_dp = lax.axis_size("ts"), lax.axis_size("dp")
    nz = n_ts // NY
    block, width = block_activity.shape[1:]
    cap = kept_locations.shape[1]
    hid = switch_matrix.shape[1]
    rows = width // n_dp
    piece = cap // n_ts
    tiles = width // LANES
    pad = -(-(tiles + 1) // 16) * 16
    bf16, f32, dma = jnp.bfloat16, jnp.float32, pltpu.SemaphoreType.DMA
    vmem = pl.BlockSpec(memory_space=pltpu.VMEM)
    hbm = pl.BlockSpec(memory_space=pl.ANY)
    token, gate, up, down = pl.pallas_call(
        functools.partial(block_kernel, n_ts, n_dp, (n_dp * cap) ** (-0.5)),
        out_shape=(
            jax.ShapeDtypeStruct((block, width), bf16),
            jax.ShapeDtypeStruct((rows, hid), bf16),
            jax.ShapeDtypeStruct((rows, hid), bf16),
            jax.ShapeDtypeStruct((hid, rows), bf16),
        ),
        in_specs=[pl.BlockSpec(memory_space=pltpu.SMEM)] + [vmem] * 4 + [hbm] * 3,
        out_specs=(vmem,) * 4,
        scratch_shapes=[
            pltpu.VMEM((hid, width), bf16), pltpu.VMEM((hid, width), bf16), pltpu.VMEM((hid, width), bf16), dma((3,)),
            pltpu.SMEM((n_ts,), jnp.int32),
            pltpu.VMEM((n_ts, width), f32),
            pltpu.VMEM((n_ts, 2 * tiles, LANES), f32),
            pltpu.VMEM((n_ts, 2 * tiles, LANES), bf16),
            pltpu.VMEM((n_ts, 2 * tiles, LANES), bf16),
            pltpu.VMEM((piece, 2 * tiles, LANES), f32),
            pltpu.VMEM((piece, 2 * width), f32),
            pltpu.VMEM((n_ts, piece, width + 2 * rows), bf16),
            pltpu.VMEM((n_ts, piece, width - 2 * rows), bf16),
            pltpu.VMEM((cap, width), bf16),
            dma((n_ts,)), dma((n_ts,)), dma((58,)), dma((58,)),
            pltpu.VMEM((cap, hid), f32), pltpu.VMEM((cap, hid), f32), pltpu.VMEM((cap, hid), f32),
            pltpu.VMEM((cap, hid), bf16), pltpu.VMEM((cap, hid), bf16), pltpu.VMEM((n_dp // 2, cap, 2 * hid), bf16),
            pltpu.VMEM((cap, hid), bf16),
            pltpu.VMEM((nz, NY, piece, width + LANES), bf16),
            pltpu.VMEM((4, 2, hid, rows), bf16),
            pltpu.VMEM((4, hid, rows), bf16),
            pltpu.VMEM((2, hid // 2, rows), bf16),
            pltpu.VMEM((2, hid, rows), bf16),
            pltpu.VMEM((nz, piece, width + LANES), bf16),
            pltpu.VMEM((2, nz, piece, width + LANES), bf16),
            pltpu.VMEM((nz, piece, width + LANES), bf16),
            pltpu.VMEM((2, 4, piece, width + LANES), bf16),
            pltpu.VMEM((2, 4, piece, width + LANES), bf16),
            pltpu.VMEM((piece, pad, LANES), f32),
            pltpu.VMEM((piece, pad, LANES), bf16),
            pltpu.VMEM((n_ts, pad, LANES), bf16),
            pltpu.VMEM((n_ts, pad, LANES), bf16),
            pltpu.VMEM((n_ts, pad, LANES), f32),
            pltpu.VMEM((n_ts, width), f32),
            dma((16,)), dma((16,)),
            pltpu.VMEM((n_dp // 2, n_ts, piece, 2 * rows), bf16),
            pltpu.VMEM((2 * rows, 2 * hid), f32),
            pltpu.VMEM((rows, 2 * hid), bf16),
            pltpu.VMEM((rows, 2 * hid), bf16),
            dma((3 * n_ts,)), dma((3 * n_ts,)), dma((7,)), dma((7,)),
            dma((12,)), dma((12,)), dma((6 * nz,)), dma((6 * nz,)),
            dma((8,)), dma((8,)), dma((n_ts,)), dma((n_ts,)),
        ],
        compiler_params=pltpu.CompilerParams(
            collective_id=0, has_side_effects=True, vmem_limit_bytes=56 * 1024 * 1024),
        name="block_backward",
    )(
        kept_locations, kept_locations, block_activity[0], result_cotangent[0],
        jnp.stack([prenormal_scaling, scorer_matrix]), switch_matrix.T, expand_matrix.T, contract_matrix,
    )
    return store_results(token[None], gate, up, down)


def solution(mesh):
    in_specs = (
        P("dp", "ts", None), P("dp", "ts", None), P("dp", None), P(), P(),
        P(None, "ts"), P(None, "ts"), P("ts", None),
    )
    out_specs = (P("dp", "ts", None), P("dp", "ts"), P("dp", "ts"), P("ts", "dp"))
    return jax.shard_map(local, mesh=mesh, in_specs=in_specs, out_specs=out_specs, check_vma=False)
```

```python
import functools
import math

import jax
import jax.numpy as jnp
from jax import lax
from jax.experimental import pallas as pl
from jax.experimental.pallas import tpu as pltpu
from jax.sharding import PartitionSpec as P

MESH = pl.DeviceIdType.MESH
NY = 4
RS_ORDER = (
    "acts_start", "terms", ("y", 4), ("y", 3), ("y", 5), ("p", 0), ("p", 1), ("p", 2), ("p", 3), ("s", 4),
    ("y", 2), ("y", 6), "x_start", ("s", 3), ("s", 5), "acts_relay", ("y", 1), ("y", 7), ("y", 0),
    ("s", 2), ("s", 6), ("e", 4), ("e", 3), ("e", 5), "z_first", ("s", 1), ("s", 7), ("e", 2), ("e", 6), "z_second",
    ("s", 0), "seen_end", "grow_own", ("e", 1), ("e", 7), "z_third", ("e", 0), "grow_near", "x_second", "back_start",
    "grow_far", "back_end", "grow_end", "x_end",
)
B_STEPS = (0, -1, 1, 2)
AG_ORDER = (
    "b1_start", "a1_start", ("f", 0), ("c", 0, 0), "b1_relay", ("c", 1, 0), ("c", 2, 0), ("a", 1), ("c", 0, 1), ("r", 0),
    "b1_end", ("c", 3, 0), ("a", 2), ("c", 1, 1), ("c", 2, 1), ("c", 0, 2), ("r", 1), ("l", 0), ("r", 2), ("c", 3, 1),
    ("a", 3), ("c", 1, 2), ("c", 2, 2), ("l", 1), ("c", 0, 3), ("r", 3), ("l", 2), ("a", 4), ("r", 4), ("c", 3, 2),
    ("c", 1, 3), ("c", 2, 3), ("l", 3), ("r", 5), ("l", 4), ("c", 0, 4), ("r", 6), ("l", 5), ("c", 3, 3), ("r", 7),
    ("c", 1, 4), ("c", 2, 4), ("l", 6), ("l", 7), "pre", ("c", 3, 4),
)
Z_STEPS = (0, -1, 1, -2, 2, -3, 3, 4)
LANES = 128
K_TILE = 512
epsilon = 1e-06
gelu_scale = math.sqrt(2.0 / math.pi)
ROWS_BY_ROWS = (((0,), (0,)), ((), ()))
COLS_BY_COLS = (((1,), (1,)), ((), ()))


def gelu_pair(pre_act):
    cubic = pre_act + 0.044715 * pre_act * pre_act * pre_act
    tanh_part = jnp.tanh(gelu_scale * cubic)
    gelu_out = 0.5 * pre_act * (1.0 + tanh_part)
    slope_out = 0.5 * (1.0 + tanh_part) + 0.5 * pre_act * (
        1.0 - tanh_part * tanh_part
    ) * gelu_scale * (1.0 + 3.0 * 0.044715 * pre_act * pre_act)
    return (gelu_out, slope_out)


def dot(a, b, dims=(((1,), (0,)), ((), ()))):
    return lax.dot_general(a, b, dims, preferred_element_type=jnp.float32)


def block_kernel(
    n_ts, n_dp, factor,
    kept_ref, kept_row, act_ref, cot_ref, vectors_ref, switch_hbm, expand_hbm, contract_hbm,
    token_ref, gate_ref, up_ref, down_ref,
    switch, expand, contract, w_sem,
    picks, own, slots_f, slots, landed, wide, piece_f, zy, yz, scaled, p1_send, p1_recv, g_send, g_recv,
    pre_gate, pre_up, hidden_grad, gate_in, up_in, acts, hidden, term,
    pair, sib, x_first, x_last, y_first, y_last, y_sum, z_in, z_out, spread, rows_out, slots_out, back, back_f, term_f,
    sib_send, sib_recv, seen, total, half_out, half_in, n_send, n_recv, a_send, a_recv, x_send, x_recv, y_send, y_recv, z_send, z_recv, b_send, b_recv,
):
    bf16, f32 = jnp.bfloat16, jnp.float32
    nz = n_ts // NY
    nx = n_dp // 2
    me = lax.axis_index("ts")
    z, y = me // NY, lax.rem(me, NY)
    dp = lax.axis_index("dp")
    x, core = dp // 2, lax.rem(dp, 2)
    block, width = act_ref.shape
    tiles = width // LANES
    piece_rows = zy.shape[1]
    cap = n_ts * piece_rows
    hid = hidden.shape[1]
    pending = []

    def node(dz, dy):
        return lax.rem(z + dz + nz, nz) * NY + lax.rem(y + dy + NY, NY)

    def chip(dx):
        return lax.rem(x + dx + nx, nx) * 2 + core

    def copy_to(sems, index, src, dst, where):
        return pltpu.make_async_remote_copy(
            src, dst, sems[0].at[index], sems[1].at[index], device_id=where, device_id_type=MESH)

    def send(sems, index, src, dst, where):
        copy = copy_to(sems, index, src, dst, where)
        copy.start()
        pending.append(copy)

    def arrive(sems, index, dst):
        copy_to(sems, index, dst, dst, {"ts": me}).wait_recv()

    right, left = {"ts": node(0, 1)}, {"ts": node(0, -1)}
    up, down = {"ts": node(1, 0)}, {"ts": node(-1, 0)}
    ahead, behind = {"dp": chip(1)}, {"dp": chip(-1)}
    sibling = {"dp": x * 2 + 1 - core}

    barrier = pltpu.get_barrier_semaphore()

    @pl.loop(1, n_ts)
    def _(step):
        pl.semaphore_signal(barrier, inc=1, device_id={"ts": lax.rem(me + step, n_ts)}, device_id_type=MESH)

    for where in (sibling, ahead, behind, {"dp": chip(2)}):
        pl.semaphore_signal(barrier, inc=1, device_id=where, device_id_type=MESH)

    weight_copies = [
        pltpu.make_async_copy(src, dst, w_sem.at[i])
        for i, (src, dst) in enumerate(((switch_hbm, switch), (expand_hbm, expand), (contract_hbm, contract)))
    ]
    for copy in weight_copies:
        copy.start()

    kept = jnp.broadcast_to(kept_row[...], (block, cap))
    position = lax.broadcasted_iota(jnp.int32, (block, cap), 0) + block * me
    rank = jnp.sum((kept < position).astype(f32), axis=1, keepdims=True)
    routed = jnp.sum((kept == position).astype(f32), axis=1, keepdims=True)
    row_class = rank - n_ts * jnp.floor(rank * (1.0 / n_ts))
    classes = lax.broadcasted_iota(jnp.int32, (block, n_ts), 1).astype(f32)
    chosen = jnp.where(classes == row_class, routed, 0.0).astype(bf16)
    own[...] = dot(chosen, act_ref[...], ROWS_BY_ROWS)
    own_cot = dot(chosen, cot_ref[...], ROWS_BY_ROWS)
    for t in range(tiles):
        slots_f[:, t, :] = own[:, t * LANES:(t + 1) * LANES]
        slots_f[:, tiles + t, :] = own_cot[:, t * LANES:(t + 1) * LANES]

    @pl.loop(0, n_ts)
    def _(c):
        slots[c] = slots_f[c].astype(bf16)

    pl.semaphore_wait(barrier, n_ts - 1 + 4)


    def p1_copy(step):
        to = lax.rem(me + step, n_ts)
        return pltpu.make_async_remote_copy(
            slots.at[to], landed.at[me], p1_send.at[step], p1_recv.at[step],
            device_id={"ts": to}, device_id_type=MESH)

    @pl.loop(1, n_ts)
    def _(step):
        p1_copy(step).start()

    landed[me] = slots[me]

    @pl.loop(0, n_ts)
    def _(h):
        pick = 0
        for k in range(1, piece_rows):
            pick = jnp.where(kept_ref[0, n_ts * k + me] // block == h, k, pick)
        picks[h] = pick

    @pl.loop(1, n_ts)
    def _(step):
        source = lax.rem(me - step + n_ts, n_ts)
        pltpu.make_async_remote_copy(
            slots.at[source], landed.at[source], p1_send.at[step], p1_recv.at[step],
            device_id={"ts": source}, device_id_type=MESH).wait_recv()


    for k in range(piece_rows):
        wide[k] = landed[kept_ref[0, n_ts * k + me] // block].astype(f32)
    for t in range(2 * tiles):
        piece_f[:, t * LANES:(t + 1) * LANES] = wide[:, t, :]

    gain = vectors_ref[0:1, :].astype(f32)
    scorer = vectors_ref[1:2, :].astype(f32)
    row_f = piece_f[:, :width]
    inv_rms = lax.rsqrt(jnp.sum(row_f * row_f, axis=1, keepdims=True) * (1.0 / width) + epsilon)
    weight = jax.nn.sigmoid(jnp.sum(row_f * scorer, axis=1, keepdims=True))
    zy[me, :, :width] = (row_f * inv_rms * gain).astype(bf16)
    scaled_rows = (weight * piece_f[:, width:]).astype(bf16)
    yz[me] = scaled_rows[:, : yz.shape[2]]
    zy[me, :, width:] = scaled_rows[:, yz.shape[2] :]


    g_sems = (g_send, g_recv)

    def cut(buffer, which):
        first = -(-buffer.shape[2] // (2 * LANES)) * LANES
        return pl.ds(0, first) if which == 0 else pl.ds(first, buffer.shape[2] - first)

    def piece(buffer, n, which=None):
        return buffer.at[n] if which is None else buffer.at[n, :, cut(buffer, which)]

    def share(index, ref, where):
        send(g_sems, index, ref, ref, where)

    B1, A1, A2, A3, B2 = 0, 4, 12, 28, 44

    def b1_start():
        share(B1 + 0, piece(yz, me), right)
        share(B1 + 1, piece(yz, me), left)

    def b1_relay():
        arrive(g_sems, B1 + 0, piece(yz, node(0, -1)))
        share(B1 + 2, piece(yz, node(0, -1), 0), right)
        arrive(g_sems, B1 + 1, piece(yz, node(0, 1)))
        share(B1 + 3, piece(yz, node(0, 1), 1), left)

    def b1_end():
        arrive(g_sems, B1 + 2, piece(yz, node(0, -2), 0))
        arrive(g_sems, B1 + 3, piece(yz, node(0, 2), 1))

    def a1_start():
        share(A1 + 0, piece(zy, me), up)
        share(A1 + 1, piece(zy, me), down)
        show(0, 0)

    def fan_out(j):
        dz = Z_STEPS[j]
        share(A2 + 2 * j, piece(zy, node(dz, 0)), right)
        share(A2 + 2 * j + 1, piece(zy, node(dz, 0)), left)

    def relay(j):
        dz = Z_STEPS[j]
        arrive(g_sems, A2 + 2 * j, piece(zy, node(dz, -1)))
        share(A3 + 2 * j, piece(zy, node(dz, -1), 0), right)
        arrive(g_sems, A2 + 2 * j + 1, piece(zy, node(dz, 1)))
        share(A3 + 2 * j + 1, piece(zy, node(dz, 1), 1), left)
        show(dz, -1)
        show(dz, 1)

    def last(j):
        arrive(g_sems, A3 + 2 * j, piece(zy, node(Z_STEPS[j], -2), 0))
        arrive(g_sems, A3 + 2 * j + 1, piece(zy, node(Z_STEPS[j], 2), 1))
        show(Z_STEPS[j], 2)

    def along(s):
        which = (0, 1) if s == 4 else (None, None)
        further = (0, 1) if s == 3 else (None, None)
        for way, to, sign in ((0, up, -1), (1, down, 1)):
            arrive(g_sems, A1 + 2 * (s - 1) + way, piece(zy, node(sign * s, 0), which[way]))
            if s < 4:
                share(A1 + 2 * s + way, piece(zy, node(sign * s, 0), further[way]), to)
        if s < 4:
            fan_out(2 * s - 1)
            fan_out(2 * s)
            show(-s, 0)
            show(s, 0)
        else:
            fan_out(7)
            show(4, 0)

    def chain(k, s):
        dy, one_way = B_STEPS[k], k // 2
        for way, to, sign in ((0, up, -1), (1, down, 1)):
            if s == 4 and way != one_way:
                continue
            ref = piece(yz, node(sign * s, dy))
            if s > 0:
                arrive(g_sems, B2 + 8 * k + 2 * (s - 1) + way, ref)
            if s < 3 or (s == 3 and way == one_way):
                share(B2 + 8 * k + 2 * s + way, ref, to)

    pair_width = 2 * width // n_dp
    far = (1, -1, 2)

    def seen_copy(rel, index):
        n = node(rel // NY, lax.rem(rel, NY))
        at = pl.ds(pl.multiple_of(lax.rem(x + far[index] + nx, nx) * pair_width, LANES), pair_width)
        return pltpu.make_async_remote_copy(
            zy.at[n, :, at], seen.at[x, n], n_send.at[index * n_ts + rel], n_recv.at[index * n_ts + rel],
            device_id={"dp": chip(far[index])}, device_id_type=MESH)

    def show(dz, dy):
        for index in range(3):
            seen_copy(dz % nz * NY + dy % NY, index).start()

    def seen_end():
        @pl.loop(0, n_ts)
        def _(rel):
            n = node(rel // NY, lax.rem(rel, NY))
            for index in range(3):
                arrive((n_send, n_recv), index * n_ts + rel, seen.at[lax.rem(x - far[index] + nx, nx), n])
                seen_copy(rel, index).wait_send()

    def columns(buffer, start, size):
        return buffer[:, :, pl.ds(start, size)].reshape(cap, size)

    def pre():
        for copy in weight_copies:
            copy.wait()
        pre_gate[...] = jnp.zeros_like(pre_gate)
        pre_up[...] = jnp.zeros_like(pre_up)

        @pl.loop(0, width // K_TILE)
        def _(k):
            at = pl.ds(pl.multiple_of(k * K_TILE, K_TILE), K_TILE)
            normed = columns(zy, pl.multiple_of(k * K_TILE, K_TILE), K_TILE)
            pre_gate[...] += dot(normed, switch[:, at], COLS_BY_COLS)
            pre_up[...] += dot(normed, expand[:, at], COLS_BY_COLS)

    steps = dict(
        pre=pre,        b1_start=b1_start, b1_relay=b1_relay, b1_end=b1_end, a1_start=a1_start)
    for step in AG_ORDER:
        if isinstance(step, str):
            steps[step]()
        else:
            (fan_out, relay, last, along, chain)["frlac".index(step[0])](*step[1:])

    hidden_grad[...] = jnp.zeros_like(hidden_grad)
    for p in range(n_dp // 2):
        at = pl.ds(p * pair_width, pair_width)
        if p < n_dp // 2 - 1:
            scaled[:, at] = columns(yz, p * pair_width, pair_width)
        else:
            scaled[:, at] = columns(zy, width, pair_width)
        hidden_grad[...] += dot(scaled[:, at], contract[:, at], COLS_BY_COLS)

    @pl.loop(0, nz)
    def _(i):
        n = cap // nz
        at = pl.ds(pl.multiple_of(i * n, n), n)
        gelu_out, slope_out = gelu_pair(pre_gate[at, :])
        up_value, grad = pre_up[at, :], hidden_grad[at, :]
        hidden_value = (gelu_out * up_value).astype(bf16)
        hidden[at, :] = hidden_value
        gate_value = (grad * up_value * slope_out).astype(bf16)
        up_back = (grad * gelu_out).astype(bf16)
        gate_in[at, :] = gate_value
        up_in[at, :] = up_back
        acts[x, at, :hid] = gate_value
        acts[x, at, hid:] = up_back
        router = jnp.sum(hidden_value.astype(f32) * grad, axis=1, keepdims=True)
        term[i, :, :, width:] = jnp.broadcast_to(router, (n, LANES)).astype(bf16).reshape(NY, piece_rows, LANES)


    a_sems = (a_send, a_recv)
    halves = (pl.ds(0, cap // 2), pl.ds(cap // 2, cap // 2))
    rows = width // n_dp

    def part(dx, which):
        return acts.at[lax.rem(x + dx + nx, nx), halves[which]]

    def pass_on(index, ref, where):
        send(a_sems, index, ref, ref, where)

    def acts_start():
        pass_on(0, part(0, 0), ahead)
        pass_on(2, part(0, 1), behind)
        pass_on(1, part(0, 1), ahead)
        pass_on(3, part(0, 0), behind)

    def acts_relay():
        arrive(a_sems, 0, part(-1, 0))
        pass_on(4, part(-1, 0), ahead)
        arrive(a_sems, 2, part(1, 1))
        pass_on(5, part(1, 1), behind)

    def grow(dx):
        at = lax.rem(x + dx + nx, nx)
        total[...] += dot(seen[at].reshape(cap, pair_width), acts[at], ROWS_BY_ROWS)

    def grow_own():
        start = pl.multiple_of(x * pair_width, LANES)
        total[...] = dot(columns(zy, start, pair_width), acts[x], ROWS_BY_ROWS)

    def grow_near():
        arrive(a_sems, 1, part(-1, 1))
        grow(-1)
        arrive(a_sems, 3, part(1, 0))
        grow(1)

    def grow_far():
        arrive(a_sems, 4, part(2, 0))
        arrive(a_sems, 5, part(2, 1))
        grow(2)
        theirs = pl.ds(pl.multiple_of((1 - core) * rows, 16), rows)
        half_out[...] = (factor * total[theirs, :]).astype(bf16)
        send(a_sems, 6, half_out, half_in, sibling)

    def grow_end():
        arrive(a_sems, 6, half_in)
        here = pl.ds(pl.multiple_of(core * rows, 16), rows)
        value = factor * total[here, :] + half_in[...].astype(f32)
        gate_ref[...] = value[:, :hid].astype(bf16)
        up_ref[...] = value[:, hid:].astype(bf16)

    sib_sems, x_sems, y_sems = (sib_send, sib_recv), (x_send, x_recv), (y_send, y_recv)
    z_sems = (z_send, z_recv)
    quarter = hid // 4
    order = (2, 1, -1, 0)

    def partials(j):
        start = pl.multiple_of(lax.rem(x + order[j] + nx, nx) * pair_width, LANES)
        both = (factor * dot(hidden[...], scaled[:, pl.ds(start, pair_width)], ROWS_BY_ROWS)).astype(bf16)
        pair[j, 0] = both[:, :rows]
        pair[j, 1] = both[:, rows:]
        for q in range(4):
            at = pl.ds(q * quarter, quarter)
            send(sib_sems, 4 * j + q, pair.at[j, 1 - core, at], sib.at[j, at], sibling)

    def add(j, q, others, store):
        arrive(sib_sems, 4 * j + q, sib.at[j, pl.ds(q * quarter, quarter)])
        here = pl.ds(q * quarter, quarter)
        value = pair[j, core, here, :].astype(f32) + sib[j, here, :].astype(f32)
        for ref, start in others:
            value += ref[pl.ds(start, quarter), :].astype(f32)
        store(here, value.astype(bf16))

    def in_place(j):
        def store(here, value):
            sib[j, here, :] = value
        return store

    def chunk(ref, q):
        return ref.at[pl.ds(q * quarter, quarter)]

    def x_start():
        for q in (0, 2, 1, 3):
            add(0, q, (), in_place(0))
            way = q // 2
            send(x_sems, q, chunk(sib.at[0], q), x_first.at[way, pl.ds((q % 2) * quarter, quarter)],
                 (ahead, behind)[way])
        for q in range(2):
            add(1, 2 + q, (), in_place(1))
            send(x_sems, 4 + q, chunk(sib.at[1], 2 + q), chunk(x_last.at[0], 2 + q), ahead)
            add(2, q, (), in_place(2))
            send(x_sems, 6 + q, chunk(sib.at[2], q), chunk(x_last.at[1], q), behind)

    def x_second():
        for q in range(2):
            arrive(x_sems, q, x_first.at[0, pl.ds(q * quarter, quarter)])
            add(1, q, ((x_first.at[0], q * quarter),), in_place(1))
            send(x_sems, 8 + q, chunk(sib.at[1], q), chunk(x_last.at[0], q), ahead)
            arrive(x_sems, 2 + q, x_first.at[1, pl.ds(q * quarter, quarter)])
            add(2, 2 + q, ((x_first.at[1], q * quarter),), in_place(2))
            send(x_sems, 10 + q, chunk(sib.at[2], 2 + q), chunk(x_last.at[1], 2 + q), behind)

    def x_end():
        def store_out(here, value):
            down_ref[here, :] = value

        for q in (2, 3, 0, 1):
            for way in range(2):
                index = (8 + q, 6 + q)[way] if q < 2 else (2 + q, 8 + q)[way]
                arrive(x_sems, index, chunk(x_last.at[way], q))
            add(3, q, ((x_last.at[0], q * quarter), (x_last.at[1], q * quarter)), store_out)

    wide_row = y_sum.shape[2]
    middle = -(-wide_row // (2 * LANES)) * LANES
    cols = (pl.ds(0, middle), pl.ds(middle, wide_row - middle))

    def terms():
        @pl.loop(0, width // K_TILE)
        def _(k):
            at = pl.ds(pl.multiple_of(k * K_TILE, K_TILE), K_TILE)
            value = dot(gate_in[...], switch[:, at]) + dot(up_in[...], expand[:, at])
            term[:, :, :, at] = value.astype(bf16).reshape(nz, NY, piece_rows, K_TILE)

    def at_z(i):
        return lax.rem(z + i, nz)

    def at_y(dy):
        return lax.rem(y + dy + NY, NY)

    def y_start(i):
        opposite = term.at[at_z(i), at_y(2)]
        send(y_sems, 6 * i, opposite.at[:, cols[0]], y_first.at[i, :, cols[0]], right)
        send(y_sems, 6 * i + 1, opposite.at[:, cols[1]], y_first.at[i, :, cols[1]], left)
        send(y_sems, 6 * i + 2, term.at[at_z(i), at_y(1), :, cols[1]], y_last.at[0, i, :, cols[1]], right)
        send(y_sems, 6 * i + 3, term.at[at_z(i), at_y(-1), :, cols[0]], y_last.at[1, i, :, cols[0]], left)

    def y_second(i):
        for way, dy, to in ((0, 1, right), (1, -1, left)):
            arrive(y_sems, 6 * i + way, y_first.at[i, :, cols[way]])
            value = term[at_z(i), at_y(dy), :, cols[way]].astype(f32) + y_first[i, :, cols[way]].astype(f32)
            y_first[i, :, cols[way]] = value.astype(bf16)
            send(y_sems, 6 * i + 4 + way, y_first.at[i, :, cols[way]], y_last.at[way, i, :, cols[way]], to)

    def y_end(i):
        for way in range(2):
            arrive(y_sems, 6 * i + 2 + way, y_last.at[way, i, :, cols[1 - way]])
            arrive(y_sems, 6 * i + 4 + way, y_last.at[way, i, :, cols[way]])
        value = term[at_z(i), y].astype(f32) + y_last[0, i].astype(f32)
        y_sum[i] = (value + y_last[1, i].astype(f32)).astype(bf16)

    def z_first():
        for way, sign in ((0, 1), (1, -1)):
            send(z_sems, 4 * way, y_sum.at[4, :, cols[way]], z_in.at[way, 0, :, cols[way]], {"ts": node(2 * sign, 0)})
            send(z_sems, 4 * way + 1, y_sum.at[3 if way == 0 else 5], z_in.at[way, 1], {"ts": node(sign, 0)})

    def z_second():
        for way, sign in ((0, 1), (1, -1)):
            arrive(z_sems, 4 * way + 1, z_in.at[way, 1])
            arrive(z_sems, 4 * way, z_in.at[way, 0, :, cols[way]])
            mine = 2 if way == 0 else 6
            rest = cols[1 - way]
            z_out[way, :, rest] = (
                y_sum[mine, :, rest].astype(f32) + z_in[way, 1, :, rest].astype(f32)).astype(bf16)
            value = y_sum[mine, :, cols[way]].astype(f32) + z_in[way, 1, :, cols[way]].astype(f32)
            z_out[way, :, cols[way]] = (value + z_in[way, 0, :, cols[way]].astype(f32)).astype(bf16)
            send(z_sems, 4 * way + 2, z_out.at[way], z_in.at[way, 2], {"ts": node(2 * sign, 0)})

    def z_third():
        for way, sign in ((0, 1), (1, -1)):
            send(z_sems, 4 * way + 3, y_sum.at[1 if way == 0 else 7], z_in.at[way, 3], {"ts": node(sign, 0)})

    def back_copy(step):
        to = lax.rem(me + step, n_ts)
        return pltpu.make_async_remote_copy(
            slots_out.at[to], back.at[me], b_send.at[step], b_recv.at[step],
            device_id={"ts": to}, device_id_type=MESH)

    def z_end():
        for way in range(2):
            arrive(z_sems, 4 * way + 2, z_in.at[way, 2])
            arrive(z_sems, 4 * way + 3, z_in.at[way, 3])

    def back_start():
        z_end()
        spread[...] = jnp.zeros_like(spread)
        for t in range(wide_row // LANES):
            at = pl.ds(t * LANES, LANES)
            value = y_sum[0, :, at].astype(f32)
            for way in range(2):
                value += z_in[way, 2, :, at].astype(f32) + z_in[way, 3, :, at].astype(f32)
            spread[:, t, :] = value
        for k in range(piece_rows):
            rows_out[k] = spread[k].astype(bf16)

        @pl.loop(0, n_ts)
        def _(h):
            slots_out[h] = rows_out[picks[h]]

        @pl.loop(1, n_ts)
        def _(step):
            back_copy(step).start()

        back[me] = slots_out[me]

    def back_end():
        @pl.loop(1, n_ts)
        def _(step):
            source = lax.rem(me - step + n_ts, n_ts)
            pltpu.make_async_remote_copy(
                slots_out.at[source], back.at[source], b_send.at[step], b_recv.at[step],
                device_id={"ts": source}, device_id_type=MESH).wait_recv()
            back_copy(step).wait_send()

        @pl.loop(0, n_ts)
        def _(c):
            back_f[c] = back[c].astype(f32)

        for t in range(tiles):
            term_f[:, t * LANES:(t + 1) * LANES] = back_f[:, t, :]
        summed_dot = back_f[:, tiles, :][:, :1]
        own_f = own[...]
        own_inv = lax.rsqrt(jnp.sum(own_f * own_f, axis=1, keepdims=True) * (1.0 / width) + epsilon)
        own_weight = jax.nn.sigmoid(jnp.sum(own_f * scorer, axis=1, keepdims=True))
        unit = own_f * own_inv
        gained = term_f[...] * gain
        mean = jnp.sum(gained * unit, axis=1, keepdims=True) * (1.0 / width)
        row_grad = own_inv * (gained - unit * mean) + ((1.0 - own_weight) * summed_dot) * scorer
        token_ref[...] = dot(chosen, row_grad.astype(bf16)).astype(bf16)

    jobs = dict(
        acts_start=acts_start, acts_relay=acts_relay, grow_own=grow_own, grow_near=grow_near, grow_far=grow_far,
        grow_end=grow_end, x_start=x_start, x_second=x_second, x_end=x_end, terms=terms, z_first=z_first, z_second=z_second, z_third=z_third, z_end=z_end, back_start=back_start, back_end=back_end, seen_end=seen_end)
    for job in RS_ORDER:
        if isinstance(job, str):
            jobs[job]()
        else:
            (partials, y_start, y_second, y_end)["pyse".index(job[0])](job[1])

    @pl.loop(1, n_ts)
    def _(step):
        p1_copy(step).wait_send()

    for copy in pending:
        copy.wait_send()


def store_kernel(*refs):
    count = (len(refs) - 2) // 3
    sems = refs[-2:]
    inward = [pltpu.make_async_copy(refs[i], refs[2 * count + i], sems[0].at[i]) for i in range(count)]
    outward = [pltpu.make_async_copy(refs[2 * count + i], refs[count + i], sems[1].at[i]) for i in range(count)]
    for copy in inward:
        copy.start()
    for first, second in zip(inward, outward):
        first.wait()
        second.start()
    for copy in outward:
        copy.wait()


def store_results(*results):
    hbm = pl.BlockSpec(memory_space=pl.ANY)
    return pl.pallas_call(
        store_kernel,
        out_shape=tuple(jax.ShapeDtypeStruct(r.shape, r.dtype) for r in results),
        in_specs=[hbm] * len(results),
        out_specs=(hbm,) * len(results),
        scratch_shapes=[pltpu.VMEM(r.shape, r.dtype) for r in results]
        + [pltpu.SemaphoreType.DMA((len(results),))] * 2,
        name="store_results",
    )(*results)


def local(
    block_activity, result_cotangent, kept_locations, prenormal_scaling, scorer_matrix,
    switch_matrix, expand_matrix, contract_matrix,
):
    n_ts, n_dp = lax.axis_size("ts"), lax.axis_size("dp")
    nz = n_ts // NY
    block, width = block_activity.shape[1:]
    cap = kept_locations.shape[1]
    hid = switch_matrix.shape[1]
    rows = width // n_dp
    piece = cap // n_ts
    tiles = width // LANES
    pad = -(-(tiles + 1) // 16) * 16
    bf16, f32, dma = jnp.bfloat16, jnp.float32, pltpu.SemaphoreType.DMA
    vmem = pl.BlockSpec(memory_space=pltpu.VMEM)
    hbm = pl.BlockSpec(memory_space=pl.ANY)
    token, gate, up, down = pl.pallas_call(
        functools.partial(block_kernel, n_ts, n_dp, (n_dp * cap) ** (-0.5)),
        out_shape=(
            jax.ShapeDtypeStruct((block, width), bf16),
            jax.ShapeDtypeStruct((rows, hid), bf16),
            jax.ShapeDtypeStruct((rows, hid), bf16),
            jax.ShapeDtypeStruct((hid, rows), bf16),
        ),
        in_specs=[pl.BlockSpec(memory_space=pltpu.SMEM)] + [vmem] * 4 + [hbm] * 3,
        out_specs=(vmem,) * 4,
        scratch_shapes=[
            pltpu.VMEM((hid, width), bf16), pltpu.VMEM((hid, width), bf16), pltpu.VMEM((hid, width), bf16), dma((3,)),
            pltpu.SMEM((n_ts,), jnp.int32),
            pltpu.VMEM((n_ts, width), f32),
            pltpu.VMEM((n_ts, 2 * tiles, LANES), f32),
            pltpu.VMEM((n_ts, 2 * tiles, LANES), bf16),
            pltpu.VMEM((n_ts, 2 * tiles, LANES), bf16),
            pltpu.VMEM((piece, 2 * tiles, LANES), f32),
            pltpu.VMEM((piece, 2 * width), f32),
            pltpu.VMEM((n_ts, piece, width + 2 * rows), bf16),
            pltpu.VMEM((n_ts, piece, width - 2 * rows), bf16),
            pltpu.VMEM((cap, width), bf16),
            dma((n_ts,)), dma((n_ts,)), dma((76,)), dma((76,)),
            pltpu.VMEM((cap, hid), f32), pltpu.VMEM((cap, hid), f32), pltpu.VMEM((cap, hid), f32),
            pltpu.VMEM((cap, hid), bf16), pltpu.VMEM((cap, hid), bf16), pltpu.VMEM((n_dp // 2, cap, 2 * hid), bf16),
            pltpu.VMEM((cap, hid), bf16),
            pltpu.VMEM((nz, NY, piece, width + LANES), bf16),
            pltpu.VMEM((4, 2, hid, rows), bf16),
            pltpu.VMEM((4, hid, rows), bf16),
            pltpu.VMEM((2, hid // 2, rows), bf16),
            pltpu.VMEM((2, hid, rows), bf16),
            pltpu.VMEM((nz, piece, width + LANES), bf16),
            pltpu.VMEM((2, nz, piece, width + LANES), bf16),
            pltpu.VMEM((nz, piece, width + LANES), bf16),
            pltpu.VMEM((2, 4, piece, width + LANES), bf16),
            pltpu.VMEM((2, piece, width + LANES), bf16),
            pltpu.VMEM((piece, pad, LANES), f32),
            pltpu.VMEM((piece, pad, LANES), bf16),
            pltpu.VMEM((n_ts, pad, LANES), bf16),
            pltpu.VMEM((n_ts, pad, LANES), bf16),
            pltpu.VMEM((n_ts, pad, LANES), f32),
            pltpu.VMEM((n_ts, width), f32),
            dma((16,)), dma((16,)),
            pltpu.VMEM((n_dp // 2, n_ts, piece, 2 * rows), bf16),
            pltpu.VMEM((2 * rows, 2 * hid), f32),
            pltpu.VMEM((rows, 2 * hid), bf16),
            pltpu.VMEM((rows, 2 * hid), bf16),
            dma((3 * n_ts,)), dma((3 * n_ts,)), dma((7,)), dma((7,)),
            dma((12,)), dma((12,)), dma((6 * nz,)), dma((6 * nz,)),
            dma((8,)), dma((8,)), dma((n_ts,)), dma((n_ts,)),
        ],
        compiler_params=pltpu.CompilerParams(
            collective_id=0, has_side_effects=True, vmem_limit_bytes=56 * 1024 * 1024),
        name="block_backward",
    )(
        kept_locations, kept_locations, block_activity[0], result_cotangent[0],
        jnp.stack([prenormal_scaling, scorer_matrix]), switch_matrix.T, expand_matrix.T, contract_matrix,
    )
    return store_results(token[None], gate, up, down)


def solution(mesh):
    in_specs = (
        P("dp", "ts", None), P("dp", "ts", None), P("dp", None), P(), P(),
        P(None, "ts"), P(None, "ts"), P("ts", None),
    )
    out_specs = (P("dp", "ts", None), P("dp", "ts"), P("dp", "ts"), P("ts", "dp"))
    return jax.shard_map(local, mesh=mesh, in_specs=in_specs, out_specs=out_specs, check_vma=False)
```

```python
import functools
import math

import jax
import jax.numpy as jnp
from jax import lax
from jax.experimental import pallas as pl
from jax.experimental.pallas import tpu as pltpu
from jax.sharding import PartitionSpec as P

MESH = pl.DeviceIdType.MESH
NY = 4
RS_ORDER = (
    "acts_start", "terms", ("y", 4), ("y", 3), ("y", 5), ("p", 0), ("p", 1), ("p", 2), ("p", 3), ("s", 4),
    ("y", 2), ("y", 6), "x_start", ("s", 3), ("s", 5), "acts_relay", ("y", 1), ("y", 7), ("y", 0),
    ("s", 2), ("s", 6), ("e", 4), ("e", 3), ("e", 5), "z_first", ("s", 1), ("s", 7), ("e", 2), ("e", 6), "z_second",
    ("s", 0), "seen_end", "grow_own", ("e", 1), ("e", 7), "z_third", ("e", 0), "grow_near", "x_second", "back_start",
    "grow_far", "back_end", "grow_end", "x_end",
)
B_STEPS = (0, -1, 1, 2)
AG_ORDER = (
    "b1_start", "a1_start", ("f", 0), ("c", 0, 0), "b1_relay", ("c", 1, 0), ("c", 2, 0), ("a", 1), ("c", 0, 1), ("r", 0),
    "b1_end", ("c", 3, 0), ("a", 2), ("c", 1, 1), ("c", 2, 1), ("c", 0, 2), ("r", 1), ("l", 0), ("r", 2), ("c", 3, 1),
    ("a", 3), ("c", 1, 2), ("c", 2, 2), ("l", 1), ("c", 0, 3), ("r", 3), ("l", 2), ("a", 4), ("r", 4), ("c", 3, 2),
    ("c", 1, 3), ("c", 2, 3), ("l", 3), ("r", 5), ("l", 4), ("c", 0, 4), ("r", 6), ("l", 5), ("c", 3, 3), ("r", 7),
    ("c", 1, 4), ("c", 2, 4), ("l", 6), ("l", 7), "pre", ("c", 3, 4),
)
Z_STEPS = (0, -1, 1, -2, 2, -3, 3, 4)
LANES = 128
K_TILE = 512
epsilon = 1e-06
gelu_scale = math.sqrt(2.0 / math.pi)
ROWS_BY_ROWS = (((0,), (0,)), ((), ()))
COLS_BY_COLS = (((1,), (1,)), ((), ()))


def gelu_pair(pre_act):
    cubic = pre_act + 0.044715 * pre_act * pre_act * pre_act
    tanh_part = jnp.tanh(gelu_scale * cubic)
    gelu_out = 0.5 * pre_act * (1.0 + tanh_part)
    slope_out = 0.5 * (1.0 + tanh_part) + 0.5 * pre_act * (
        1.0 - tanh_part * tanh_part
    ) * gelu_scale * (1.0 + 3.0 * 0.044715 * pre_act * pre_act)
    return (gelu_out, slope_out)


def dot(a, b, dims=(((1,), (0,)), ((), ()))):
    return lax.dot_general(a, b, dims, preferred_element_type=jnp.float32)


def block_kernel(
    n_ts, n_dp, factor,
    kept_ref, kept_row, act_ref, cot_ref, gain_ref, scorer_ref, switch_hbm, expand_hbm, contract_hbm,
    token_ref, gate_ref, up_ref, down_ref,
    switch, expand, contract, w_sem,
    picks, own, slots_f, slots, landed, wide, piece_f, zy, yz, scaled, p1_send, p1_recv, g_send, g_recv,
    pre_gate, pre_up, hidden_grad, gate_in, up_in, acts, hidden, term,
    pair, sib, x_first, x_last, y_first, y_last, y_sum, z_in, z_out, spread, rows_out, slots_out, back, back_f, term_f,
    sib_send, sib_recv, seen, total, half_out, half_in, n_send, n_recv, a_send, a_recv, x_send, x_recv, y_send, y_recv, z_send, z_recv, b_send, b_recv,
):
    bf16, f32 = jnp.bfloat16, jnp.float32
    nz = n_ts // NY
    nx = n_dp // 2
    me = lax.axis_index("ts")
    z, y = me // NY, lax.rem(me, NY)
    dp = lax.axis_index("dp")
    x, core = dp // 2, lax.rem(dp, 2)
    block, width = act_ref.shape
    tiles = width // LANES
    piece_rows = zy.shape[1]
    cap = n_ts * piece_rows
    hid = hidden.shape[1]
    pending = []

    def node(dz, dy):
        return lax.rem(z + dz + nz, nz) * NY + lax.rem(y + dy + NY, NY)

    def chip(dx):
        return lax.rem(x + dx + nx, nx) * 2 + core

    def copy_to(sems, index, src, dst, where):
        return pltpu.make_async_remote_copy(
            src, dst, sems[0].at[index], sems[1].at[index], device_id=where, device_id_type=MESH)

    def send(sems, index, src, dst, where):
        copy = copy_to(sems, index, src, dst, where)
        copy.start()
        pending.append(copy)

    def arrive(sems, index, dst):
        copy_to(sems, index, dst, dst, {"ts": me}).wait_recv()

    right, left = {"ts": node(0, 1)}, {"ts": node(0, -1)}
    up, down = {"ts": node(1, 0)}, {"ts": node(-1, 0)}
    ahead, behind = {"dp": chip(1)}, {"dp": chip(-1)}
    sibling = {"dp": x * 2 + 1 - core}

    barrier = pltpu.get_barrier_semaphore()

    @pl.loop(1, n_ts)
    def _(step):
        pl.semaphore_signal(barrier, inc=1, device_id={"ts": lax.rem(me + step, n_ts)}, device_id_type=MESH)

    for where in (sibling, ahead, behind, {"dp": chip(2)}):
        pl.semaphore_signal(barrier, inc=1, device_id=where, device_id_type=MESH)

    weight_copies = [
        pltpu.make_async_copy(src, dst, w_sem.at[i])
        for i, (src, dst) in enumerate(((switch_hbm, switch), (expand_hbm, expand), (contract_hbm, contract)))
    ]
    for copy in weight_copies:
        copy.start()

    kept = jnp.broadcast_to(kept_row[...], (block, cap))
    position = lax.broadcasted_iota(jnp.int32, (block, cap), 0) + block * me
    rank = jnp.sum((kept < position).astype(f32), axis=1, keepdims=True)
    routed = jnp.sum((kept == position).astype(f32), axis=1, keepdims=True)
    row_class = rank - n_ts * jnp.floor(rank * (1.0 / n_ts))
    classes = lax.broadcasted_iota(jnp.int32, (block, n_ts), 1).astype(f32)
    chosen = jnp.where(classes == row_class, routed, 0.0).astype(bf16)
    own[...] = dot(chosen, act_ref[...], ROWS_BY_ROWS)
    own_cot = dot(chosen, cot_ref[...], ROWS_BY_ROWS)
    for t in range(tiles):
        slots_f[:, t, :] = own[:, t * LANES:(t + 1) * LANES]
        slots_f[:, tiles + t, :] = own_cot[:, t * LANES:(t + 1) * LANES]

    @pl.loop(0, n_ts)
    def _(c):
        slots[c] = slots_f[c].astype(bf16)

    pl.semaphore_wait(barrier, n_ts - 1 + 4)


    def p1_copy(step):
        to = lax.rem(me + step, n_ts)
        return pltpu.make_async_remote_copy(
            slots.at[to], landed.at[me], p1_send.at[step], p1_recv.at[step],
            device_id={"ts": to}, device_id_type=MESH)

    @pl.loop(1, n_ts)
    def _(step):
        p1_copy(step).start()

    landed[me] = slots[me]

    gain = gain_ref[...].astype(f32).reshape(1, width)
    scorer = scorer_ref[...].astype(f32).reshape(1, width)
    own_f = own[...]
    own_inv = lax.rsqrt(jnp.sum(own_f * own_f, axis=1, keepdims=True) * (1.0 / width) + epsilon)
    own_weight = jax.nn.sigmoid(jnp.sum(own_f * scorer, axis=1, keepdims=True))
    own[...] = own_f * own_inv

    @pl.loop(0, n_ts)
    def _(h):
        pick = 0
        for k in range(1, piece_rows):
            pick = jnp.where(kept_ref[0, n_ts * k + me] // block == h, k, pick)
        picks[h] = pick

    @pl.loop(1, n_ts)
    def _(step):
        source = lax.rem(me - step + n_ts, n_ts)
        pltpu.make_async_remote_copy(
            slots.at[source], landed.at[source], p1_send.at[step], p1_recv.at[step],
            device_id={"ts": source}, device_id_type=MESH).wait_recv()


    for k in range(piece_rows):
        wide[k] = landed[kept_ref[0, n_ts * k + me] // block].astype(f32)
    for t in range(2 * tiles):
        piece_f[:, t * LANES:(t + 1) * LANES] = wide[:, t, :]

    row_f = piece_f[:, :width]
    inv_rms = lax.rsqrt(jnp.sum(row_f * row_f, axis=1, keepdims=True) * (1.0 / width) + epsilon)
    weight = jax.nn.sigmoid(jnp.sum(row_f * scorer, axis=1, keepdims=True))
    zy[me, :, :width] = (row_f * inv_rms * gain).astype(bf16)
    scaled_rows = (weight * piece_f[:, width:]).astype(bf16)
    yz[me] = scaled_rows[:, : yz.shape[2]]
    zy[me, :, width:] = scaled_rows[:, yz.shape[2] :]


    g_sems = (g_send, g_recv)

    def cut(buffer, which):
        first = -(-buffer.shape[2] // (2 * LANES)) * LANES
        return pl.ds(0, first) if which == 0 else pl.ds(first, buffer.shape[2] - first)

    def piece(buffer, n, which=None):
        return buffer.at[n] if which is None else buffer.at[n, :, cut(buffer, which)]

    def share(index, ref, where):
        send(g_sems, index, ref, ref, where)

    B1, A1, A2, A3, B2 = 0, 4, 12, 28, 44

    def b1_start():
        share(B1 + 0, piece(yz, me), right)
        share(B1 + 1, piece(yz, me), left)

    def b1_relay():
        arrive(g_sems, B1 + 0, piece(yz, node(0, -1)))
        share(B1 + 2, piece(yz, node(0, -1), 0), right)
        arrive(g_sems, B1 + 1, piece(yz, node(0, 1)))
        share(B1 + 3, piece(yz, node(0, 1), 1), left)

    def b1_end():
        arrive(g_sems, B1 + 2, piece(yz, node(0, -2), 0))
        arrive(g_sems, B1 + 3, piece(yz, node(0, 2), 1))

    def a1_start():
        share(A1 + 0, piece(zy, me), up)
        share(A1 + 1, piece(zy, me), down)
        show(0, 0)

    def fan_out(j):
        dz = Z_STEPS[j]
        share(A2 + 2 * j, piece(zy, node(dz, 0)), right)
        share(A2 + 2 * j + 1, piece(zy, node(dz, 0)), left)

    def relay(j):
        dz = Z_STEPS[j]
        arrive(g_sems, A2 + 2 * j, piece(zy, node(dz, -1)))
        share(A3 + 2 * j, piece(zy, node(dz, -1), 0), right)
        arrive(g_sems, A2 + 2 * j + 1, piece(zy, node(dz, 1)))
        share(A3 + 2 * j + 1, piece(zy, node(dz, 1), 1), left)
        show(dz, -1)
        show(dz, 1)

    def last(j):
        arrive(g_sems, A3 + 2 * j, piece(zy, node(Z_STEPS[j], -2), 0))
        arrive(g_sems, A3 + 2 * j + 1, piece(zy, node(Z_STEPS[j], 2), 1))
        show(Z_STEPS[j], 2)

    def along(s):
        which = (0, 1) if s == 4 else (None, None)
        further = (0, 1) if s == 3 else (None, None)
        for way, to, sign in ((0, up, -1), (1, down, 1)):
            arrive(g_sems, A1 + 2 * (s - 1) + way, piece(zy, node(sign * s, 0), which[way]))
            if s < 4:
                share(A1 + 2 * s + way, piece(zy, node(sign * s, 0), further[way]), to)
        if s < 4:
            fan_out(2 * s - 1)
            fan_out(2 * s)
            show(-s, 0)
            show(s, 0)
        else:
            fan_out(7)
            show(4, 0)

    def chain(k, s):
        dy, one_way = B_STEPS[k], k // 2
        for way, to, sign in ((0, up, -1), (1, down, 1)):
            if s == 4 and way != one_way:
                continue
            ref = piece(yz, node(sign * s, dy))
            if s > 0:
                arrive(g_sems, B2 + 8 * k + 2 * (s - 1) + way, ref)
            if s < 3 or (s == 3 and way == one_way):
                share(B2 + 8 * k + 2 * s + way, ref, to)

    pair_width = 2 * width // n_dp
    far = (1, -1, 2)

    def seen_copy(rel, index):
        n = node(rel // NY, lax.rem(rel, NY))
        at = pl.ds(pl.multiple_of(lax.rem(x + far[index] + nx, nx) * pair_width, LANES), pair_width)
        return pltpu.make_async_remote_copy(
            zy.at[n, :, at], seen.at[x, n], n_send.at[index * n_ts + rel], n_recv.at[index * n_ts + rel],
            device_id={"dp": chip(far[index])}, device_id_type=MESH)

    def show(dz, dy):
        for index in range(3):
            seen_copy(dz % nz * NY + dy % NY, index).start()

    def seen_end():
        @pl.loop(0, n_ts)
        def _(rel):
            n = node(rel // NY, lax.rem(rel, NY))
            for index in range(3):
                arrive((n_send, n_recv), index * n_ts + rel, seen.at[lax.rem(x - far[index] + nx, nx), n])
                seen_copy(rel, index).wait_send()

    def columns(buffer, start, size):
        return buffer[:, :, pl.ds(start, size)].reshape(cap, size)

    def pre():
        for copy in weight_copies:
            copy.wait()
        pre_gate[...] = jnp.zeros_like(pre_gate)
        pre_up[...] = jnp.zeros_like(pre_up)

        @pl.loop(0, width // K_TILE)
        def _(k):
            at = pl.ds(pl.multiple_of(k * K_TILE, K_TILE), K_TILE)
            normed = columns(zy, pl.multiple_of(k * K_TILE, K_TILE), K_TILE)
            pre_gate[...] += dot(normed, switch[:, at], COLS_BY_COLS)
            pre_up[...] += dot(normed, expand[:, at], COLS_BY_COLS)

    steps = dict(
        pre=pre,        b1_start=b1_start, b1_relay=b1_relay, b1_end=b1_end, a1_start=a1_start)
    for step in AG_ORDER:
        if isinstance(step, str):
            steps[step]()
        else:
            (fan_out, relay, last, along, chain)["frlac".index(step[0])](*step[1:])

    hidden_grad[...] = jnp.zeros_like(hidden_grad)
    for p in range(n_dp // 2):
        at = pl.ds(p * pair_width, pair_width)
        if p < n_dp // 2 - 1:
            scaled[:, at] = columns(yz, p * pair_width, pair_width)
        else:
            scaled[:, at] = columns(zy, width, pair_width)
        hidden_grad[...] += dot(scaled[:, at], contract[:, at], COLS_BY_COLS)

    @pl.loop(0, nz)
    def _(i):
        n = cap // nz
        at = pl.ds(pl.multiple_of(i * n, n), n)
        gelu_out, slope_out = gelu_pair(pre_gate[at, :])
        up_value, grad = pre_up[at, :], hidden_grad[at, :]
        hidden_value = (gelu_out * up_value).astype(bf16)
        hidden[at, :] = hidden_value
        gate_value = (grad * up_value * slope_out).astype(bf16)
        up_back = (grad * gelu_out).astype(bf16)
        gate_in[at, :] = gate_value
        up_in[at, :] = up_back
        acts[x, at, :hid] = gate_value
        acts[x, at, hid:] = up_back
        router = jnp.sum(hidden_value.astype(f32) * grad, axis=1, keepdims=True)
        term[i, :, :, width:] = jnp.broadcast_to(router, (n, LANES)).astype(bf16).reshape(NY, piece_rows, LANES)


    a_sems = (a_send, a_recv)
    halves = (pl.ds(0, cap // 2), pl.ds(cap // 2, cap // 2))
    rows = width // n_dp

    def part(dx, which):
        return acts.at[lax.rem(x + dx + nx, nx), halves[which]]

    def pass_on(index, ref, where):
        send(a_sems, index, ref, ref, where)

    def acts_start():
        pass_on(0, part(0, 0), ahead)
        pass_on(2, part(0, 1), behind)
        pass_on(1, part(0, 1), ahead)
        pass_on(3, part(0, 0), behind)

    def acts_relay():
        arrive(a_sems, 0, part(-1, 0))
        pass_on(4, part(-1, 0), ahead)
        arrive(a_sems, 2, part(1, 1))
        pass_on(5, part(1, 1), behind)

    def grow(dx):
        at = lax.rem(x + dx + nx, nx)
        total[...] += dot(seen[at].reshape(cap, pair_width), acts[at], ROWS_BY_ROWS)

    def grow_own():
        start = pl.multiple_of(x * pair_width, LANES)
        total[...] = dot(columns(zy, start, pair_width), acts[x], ROWS_BY_ROWS)

    def grow_near():
        arrive(a_sems, 1, part(-1, 1))
        grow(-1)
        arrive(a_sems, 3, part(1, 0))
        grow(1)

    def grow_far():
        arrive(a_sems, 4, part(2, 0))
        arrive(a_sems, 5, part(2, 1))
        grow(2)
        theirs = pl.ds(pl.multiple_of((1 - core) * rows, 16), rows)
        half_out[...] = (factor * total[theirs, :]).astype(bf16)
        send(a_sems, 6, half_out, half_in, sibling)

    def grow_end():
        arrive(a_sems, 6, half_in)
        here = pl.ds(pl.multiple_of(core * rows, 16), rows)
        value = factor * total[here, :] + half_in[...].astype(f32)
        gate_ref[...] = value[:, :hid].astype(bf16)
        up_ref[...] = value[:, hid:].astype(bf16)

    sib_sems, x_sems, y_sems = (sib_send, sib_recv), (x_send, x_recv), (y_send, y_recv)
    z_sems = (z_send, z_recv)
    quarter = hid // 4
    order = (2, 1, -1, 0)

    def partials(j):
        start = pl.multiple_of(lax.rem(x + order[j] + nx, nx) * pair_width, LANES)
        both = (factor * dot(hidden[...], scaled[:, pl.ds(start, pair_width)], ROWS_BY_ROWS)).astype(bf16)
        pair[j, 0] = both[:, :rows]
        pair[j, 1] = both[:, rows:]
        for q in range(4):
            at = pl.ds(q * quarter, quarter)
            send(sib_sems, 4 * j + q, pair.at[j, 1 - core, at], sib.at[j, at], sibling)

    def add(j, q, others, store):
        arrive(sib_sems, 4 * j + q, sib.at[j, pl.ds(q * quarter, quarter)])
        here = pl.ds(q * quarter, quarter)
        value = pair[j, core, here, :].astype(f32) + sib[j, here, :].astype(f32)
        for ref, start in others:
            value += ref[pl.ds(start, quarter), :].astype(f32)
        store(here, value.astype(bf16))

    def in_place(j):
        def store(here, value):
            sib[j, here, :] = value
        return store

    def chunk(ref, q):
        return ref.at[pl.ds(q * quarter, quarter)]

    def x_start():
        for q in (0, 2, 1, 3):
            add(0, q, (), in_place(0))
            way = q // 2
            send(x_sems, q, chunk(sib.at[0], q), x_first.at[way, pl.ds((q % 2) * quarter, quarter)],
                 (ahead, behind)[way])
        for q in range(2):
            add(1, 2 + q, (), in_place(1))
            send(x_sems, 4 + q, chunk(sib.at[1], 2 + q), chunk(x_last.at[0], 2 + q), ahead)
            add(2, q, (), in_place(2))
            send(x_sems, 6 + q, chunk(sib.at[2], q), chunk(x_last.at[1], q), behind)

    def x_second():
        for q in range(2):
            arrive(x_sems, q, x_first.at[0, pl.ds(q * quarter, quarter)])
            add(1, q, ((x_first.at[0], q * quarter),), in_place(1))
            send(x_sems, 8 + q, chunk(sib.at[1], q), chunk(x_last.at[0], q), ahead)
            arrive(x_sems, 2 + q, x_first.at[1, pl.ds(q * quarter, quarter)])
            add(2, 2 + q, ((x_first.at[1], q * quarter),), in_place(2))
            send(x_sems, 10 + q, chunk(sib.at[2], 2 + q), chunk(x_last.at[1], 2 + q), behind)

    def x_end():
        def store_out(here, value):
            down_ref[here, :] = value

        for q in (2, 3, 0, 1):
            for way in range(2):
                index = (8 + q, 6 + q)[way] if q < 2 else (2 + q, 8 + q)[way]
                arrive(x_sems, index, chunk(x_last.at[way], q))
            add(3, q, ((x_last.at[0], q * quarter), (x_last.at[1], q * quarter)), store_out)

    wide_row = y_sum.shape[2]
    middle = -(-wide_row // (2 * LANES)) * LANES
    cols = (pl.ds(0, middle), pl.ds(middle, wide_row - middle))

    def terms():
        @pl.loop(0, width // K_TILE)
        def _(k):
            at = pl.ds(pl.multiple_of(k * K_TILE, K_TILE), K_TILE)
            value = dot(gate_in[...], switch[:, at]) + dot(up_in[...], expand[:, at])
            term[:, :, :, at] = value.astype(bf16).reshape(nz, NY, piece_rows, K_TILE)

    def at_z(i):
        return lax.rem(z + i, nz)

    def at_y(dy):
        return lax.rem(y + dy + NY, NY)

    def y_start(i):
        opposite = term.at[at_z(i), at_y(2)]
        send(y_sems, 6 * i, opposite.at[:, cols[0]], y_first.at[i, :, cols[0]], right)
        send(y_sems, 6 * i + 1, opposite.at[:, cols[1]], y_first.at[i, :, cols[1]], left)
        send(y_sems, 6 * i + 2, term.at[at_z(i), at_y(1), :, cols[1]], y_last.at[0, i, :, cols[1]], right)
        send(y_sems, 6 * i + 3, term.at[at_z(i), at_y(-1), :, cols[0]], y_last.at[1, i, :, cols[0]], left)

    def y_second(i):
        for way, dy, to in ((0, 1, right), (1, -1, left)):
            arrive(y_sems, 6 * i + way, y_first.at[i, :, cols[way]])
            value = term[at_z(i), at_y(dy), :, cols[way]].astype(f32) + y_first[i, :, cols[way]].astype(f32)
            y_first[i, :, cols[way]] = value.astype(bf16)
            send(y_sems, 6 * i + 4 + way, y_first.at[i, :, cols[way]], y_last.at[way, i, :, cols[way]], to)

    def y_end(i):
        for way in range(2):
            arrive(y_sems, 6 * i + 2 + way, y_last.at[way, i, :, cols[1 - way]])
            arrive(y_sems, 6 * i + 4 + way, y_last.at[way, i, :, cols[way]])
        value = term[at_z(i), y].astype(f32) + y_last[0, i].astype(f32)
        y_sum[i] = (value + y_last[1, i].astype(f32)).astype(bf16)

    def z_first():
        for way, sign in ((0, 1), (1, -1)):
            send(z_sems, 4 * way, y_sum.at[4, :, cols[way]], z_in.at[way, 0, :, cols[way]], {"ts": node(2 * sign, 0)})
            send(z_sems, 4 * way + 1, y_sum.at[3 if way == 0 else 5], z_in.at[way, 1], {"ts": node(sign, 0)})

    def z_second():
        for way, sign in ((0, 1), (1, -1)):
            arrive(z_sems, 4 * way + 1, z_in.at[way, 1])
            arrive(z_sems, 4 * way, z_in.at[way, 0, :, cols[way]])
            mine = 2 if way == 0 else 6
            rest = cols[1 - way]
            z_out[way, :, rest] = (
                y_sum[mine, :, rest].astype(f32) + z_in[way, 1, :, rest].astype(f32)).astype(bf16)
            value = y_sum[mine, :, cols[way]].astype(f32) + z_in[way, 1, :, cols[way]].astype(f32)
            z_out[way, :, cols[way]] = (value + z_in[way, 0, :, cols[way]].astype(f32)).astype(bf16)
            send(z_sems, 4 * way + 2, z_out.at[way], z_in.at[way, 2], {"ts": node(2 * sign, 0)})

    def z_third():
        for way, sign in ((0, 1), (1, -1)):
            send(z_sems, 4 * way + 3, y_sum.at[1 if way == 0 else 7], z_in.at[way, 3], {"ts": node(sign, 0)})

    def back_copy(step):
        to = lax.rem(me + step, n_ts)
        return pltpu.make_async_remote_copy(
            slots_out.at[to], back.at[me], b_send.at[step], b_recv.at[step],
            device_id={"ts": to}, device_id_type=MESH)

    def z_end():
        for way in range(2):
            arrive(z_sems, 4 * way + 2, z_in.at[way, 2])
            arrive(z_sems, 4 * way + 3, z_in.at[way, 3])

    def back_start():
        z_end()
        spread[...] = jnp.zeros_like(spread)
        for t in range(wide_row // LANES):
            at = pl.ds(t * LANES, LANES)
            value = y_sum[0, :, at].astype(f32)
            for way in range(2):
                value += z_in[way, 2, :, at].astype(f32) + z_in[way, 3, :, at].astype(f32)
            spread[:, t, :] = value
        for k in range(piece_rows):
            rows_out[k] = spread[k].astype(bf16)

        @pl.loop(0, n_ts)
        def _(h):
            slots_out[h] = rows_out[picks[h]]

        @pl.loop(1, n_ts)
        def _(step):
            back_copy(step).start()

        back[me] = slots_out[me]

    def back_end():
        @pl.loop(1, n_ts)
        def _(step):
            source = lax.rem(me - step + n_ts, n_ts)
            pltpu.make_async_remote_copy(
                slots_out.at[source], back.at[source], b_send.at[step], b_recv.at[step],
                device_id={"ts": source}, device_id_type=MESH).wait_recv()
            back_copy(step).wait_send()

        @pl.loop(0, n_ts)
        def _(c):
            back_f[c] = back[c].astype(f32)

        for t in range(tiles):
            term_f[:, t * LANES:(t + 1) * LANES] = back_f[:, t, :]
        summed_dot = back_f[:, tiles, :][:, :1]
        unit = own[...]
        gained = term_f[...] * gain
        mean = jnp.sum(gained * unit, axis=1, keepdims=True) * (1.0 / width)
        row_grad = own_inv * (gained - unit * mean) + ((1.0 - own_weight) * summed_dot) * scorer
        token_ref[...] = dot(chosen, row_grad.astype(bf16)).astype(bf16)

    jobs = dict(
        acts_start=acts_start, acts_relay=acts_relay, grow_own=grow_own, grow_near=grow_near, grow_far=grow_far,
        grow_end=grow_end, x_start=x_start, x_second=x_second, x_end=x_end, terms=terms, z_first=z_first, z_second=z_second, z_third=z_third, z_end=z_end, back_start=back_start, back_end=back_end, seen_end=seen_end)
    for job in RS_ORDER:
        if isinstance(job, str):
            jobs[job]()
        else:
            (partials, y_start, y_second, y_end)["pyse".index(job[0])](job[1])

    @pl.loop(1, n_ts)
    def _(step):
        p1_copy(step).wait_send()

    for copy in pending:
        copy.wait_send()


def store_kernel(*refs):
    count = (len(refs) - 2) // 3
    sems = refs[-2:]
    inward = [pltpu.make_async_copy(refs[i], refs[2 * count + i], sems[0].at[i]) for i in range(count)]
    outward = [pltpu.make_async_copy(refs[2 * count + i], refs[count + i], sems[1].at[i]) for i in range(count)]
    for copy in inward:
        copy.start()
    for first, second in zip(inward, outward):
        first.wait()
        second.start()
    for copy in outward:
        copy.wait()


def store_results(*results):
    hbm = pl.BlockSpec(memory_space=pl.ANY)
    return pl.pallas_call(
        store_kernel,
        out_shape=tuple(jax.ShapeDtypeStruct(r.shape, r.dtype) for r in results),
        in_specs=[hbm] * len(results),
        out_specs=(hbm,) * len(results),
        scratch_shapes=[pltpu.VMEM(r.shape, r.dtype) for r in results]
        + [pltpu.SemaphoreType.DMA((len(results),))] * 2,
        name="store_results",
    )(*results)


def local(
    block_activity, result_cotangent, kept_locations, prenormal_scaling, scorer_matrix,
    switch_matrix, expand_matrix, contract_matrix,
):
    n_ts, n_dp = lax.axis_size("ts"), lax.axis_size("dp")
    nz = n_ts // NY
    block, width = block_activity.shape[1:]
    cap = kept_locations.shape[1]
    hid = switch_matrix.shape[1]
    rows = width // n_dp
    piece = cap // n_ts
    tiles = width // LANES
    pad = -(-(tiles + 1) // 16) * 16
    bf16, f32, dma = jnp.bfloat16, jnp.float32, pltpu.SemaphoreType.DMA
    vmem = pl.BlockSpec(memory_space=pltpu.VMEM)
    hbm = pl.BlockSpec(memory_space=pl.ANY)
    token, gate, up, down = pl.pallas_call(
        functools.partial(block_kernel, n_ts, n_dp, (n_dp * cap) ** (-0.5)),
        out_shape=(
            jax.ShapeDtypeStruct((block, width), bf16),
            jax.ShapeDtypeStruct((rows, hid), bf16),
            jax.ShapeDtypeStruct((rows, hid), bf16),
            jax.ShapeDtypeStruct((hid, rows), bf16),
        ),
        in_specs=[pl.BlockSpec(memory_space=pltpu.SMEM)] + [vmem] * 5 + [hbm] * 3,
        out_specs=(vmem,) * 4,
        scratch_shapes=[
            pltpu.VMEM((hid, width), bf16), pltpu.VMEM((hid, width), bf16), pltpu.VMEM((hid, width), bf16), dma((3,)),
            pltpu.SMEM((n_ts,), jnp.int32),
            pltpu.VMEM((n_ts, width), f32),
            pltpu.VMEM((n_ts, 2 * tiles, LANES), f32),
            pltpu.VMEM((n_ts, 2 * tiles, LANES), bf16),
            pltpu.VMEM((n_ts, 2 * tiles, LANES), bf16),
            pltpu.VMEM((piece, 2 * tiles, LANES), f32),
            pltpu.VMEM((piece, 2 * width), f32),
            pltpu.VMEM((n_ts, piece, width + 2 * rows), bf16),
            pltpu.VMEM((n_ts, piece, width - 2 * rows), bf16),
            pltpu.VMEM((cap, width), bf16),
            dma((n_ts,)), dma((n_ts,)), dma((76,)), dma((76,)),
            pltpu.VMEM((cap, hid), f32), pltpu.VMEM((cap, hid), f32), pltpu.VMEM((cap, hid), f32),
            pltpu.VMEM((cap, hid), bf16), pltpu.VMEM((cap, hid), bf16), pltpu.VMEM((n_dp // 2, cap, 2 * hid), bf16),
            pltpu.VMEM((cap, hid), bf16),
            pltpu.VMEM((nz, NY, piece, width + LANES), bf16),
            pltpu.VMEM((4, 2, hid, rows), bf16),
            pltpu.VMEM((4, hid, rows), bf16),
            pltpu.VMEM((2, hid // 2, rows), bf16),
            pltpu.VMEM((2, hid, rows), bf16),
            pltpu.VMEM((nz, piece, width + LANES), bf16),
            pltpu.VMEM((2, nz, piece, width + LANES), bf16),
            pltpu.VMEM((nz, piece, width + LANES), bf16),
            pltpu.VMEM((2, 4, piece, width + LANES), bf16),
            pltpu.VMEM((2, piece, width + LANES), bf16),
            pltpu.VMEM((piece, pad, LANES), f32),
            pltpu.VMEM((piece, pad, LANES), bf16),
            pltpu.VMEM((n_ts, pad, LANES), bf16),
            pltpu.VMEM((n_ts, pad, LANES), bf16),
            pltpu.VMEM((n_ts, pad, LANES), f32),
            pltpu.VMEM((n_ts, width), f32),
            dma((16,)), dma((16,)),
            pltpu.VMEM((n_dp // 2, n_ts, piece, 2 * rows), bf16),
            pltpu.VMEM((2 * rows, 2 * hid), f32),
            pltpu.VMEM((rows, 2 * hid), bf16),
            pltpu.VMEM((rows, 2 * hid), bf16),
            dma((3 * n_ts,)), dma((3 * n_ts,)), dma((7,)), dma((7,)),
            dma((12,)), dma((12,)), dma((6 * nz,)), dma((6 * nz,)),
            dma((8,)), dma((8,)), dma((n_ts,)), dma((n_ts,)),
        ],
        compiler_params=pltpu.CompilerParams(
            collective_id=0, has_side_effects=True, vmem_limit_bytes=56 * 1024 * 1024),
        name="block_backward",
    )(
        kept_locations, kept_locations, block_activity[0], result_cotangent[0],
        prenormal_scaling, scorer_matrix, switch_matrix.T, expand_matrix.T, contract_matrix,
    )
    return store_results(token[None], gate, up, down)


def solution(mesh):
    in_specs = (
        P("dp", "ts", None), P("dp", "ts", None), P("dp", None), P(), P(),
        P(None, "ts"), P(None, "ts"), P("ts", None),
    )
    out_specs = (P("dp", "ts", None), P("dp", "ts"), P("dp", "ts"), P("ts", "dp"))
    return jax.shard_map(local, mesh=mesh, in_specs=in_specs, out_specs=out_specs, check_vma=False)
```

```python
import functools
import math

import jax
import jax.numpy as jnp
from jax import lax
from jax.experimental import pallas as pl
from jax.experimental.pallas import tpu as pltpu
from jax.sharding import PartitionSpec as P

MESH = pl.DeviceIdType.MESH
NY = 4
RS_ORDER = (
    "acts_start", "terms", ("y", 4), ("y", 3), ("y", 5), ("p", 0), ("p", 1), ("p", 2), ("p", 3), ("s", 4),
    ("y", 2), ("y", 6), "x_start", ("s", 3), ("s", 5), "acts_relay", ("y", 1), ("y", 7), ("y", 0),
    ("s", 2), ("s", 6), ("e", 4), ("e", 3), ("e", 5), "z_first", ("s", 1), ("s", 7), ("e", 2), ("e", 6), "z_second",
    ("s", 0), "seen_end", "grow_own", ("e", 1), ("e", 7), "z_third", ("e", 0), "grow_near", "x_second", "back_start",
    "grow_far", "back_end", "grow_end", "x_end",
)
B_STEPS = (0, -1, 1, 2)
AG_ORDER = (
    "b1_start", "a1_start", ("f", 0), ("c", 0, 0), "b1_relay", ("c", 1, 0), ("c", 2, 0), ("a", 1), ("c", 0, 1), ("r", 0),
    "b1_end", ("c", 3, 0), ("a", 2), ("c", 1, 1), ("c", 2, 1), ("c", 0, 2), ("r", 1), ("l", 0), ("r", 2), ("c", 3, 1),
    ("a", 3), ("c", 1, 2), ("c", 2, 2), ("l", 1), ("c", 0, 3), ("r", 3), ("l", 2), ("a", 4), ("r", 4), ("c", 3, 2),
    ("c", 1, 3), ("c", 2, 3), ("l", 3), ("r", 5), ("l", 4), ("c", 0, 4), ("r", 6), ("l", 5), ("c", 3, 3), ("r", 7),
    ("c", 1, 4), ("c", 2, 4), ("l", 6), ("l", 7), "pre", ("c", 3, 4),
)
Z_STEPS = (0, -1, 1, -2, 2, -3, 3, 4)
LANES = 128
K_TILE = 512
epsilon = 1e-06
gelu_scale = math.sqrt(2.0 / math.pi)
ROWS_BY_ROWS = (((0,), (0,)), ((), ()))
COLS_BY_COLS = (((1,), (1,)), ((), ()))


def gelu_pair(pre_act):
    cubic = pre_act + 0.044715 * pre_act * pre_act * pre_act
    tanh_part = jnp.tanh(gelu_scale * cubic)
    gelu_out = 0.5 * pre_act * (1.0 + tanh_part)
    slope_out = 0.5 * (1.0 + tanh_part) + 0.5 * pre_act * (
        1.0 - tanh_part * tanh_part
    ) * gelu_scale * (1.0 + 3.0 * 0.044715 * pre_act * pre_act)
    return (gelu_out, slope_out)


def dot(a, b, dims=(((1,), (0,)), ((), ()))):
    return lax.dot_general(a, b, dims, preferred_element_type=jnp.float32)


def block_kernel(
    n_ts, n_dp, factor,
    kept_ref, kept_row, act_ref, cot_ref, gain_ref, scorer_ref, switch_hbm, expand_hbm, contract_hbm,
    token_ref, gate_ref, up_ref, down_ref,
    switch, expand, contract, w_sem,
    picks, own, slots_f, slots, landed, wide, piece_f, zy, yz, scaled, p1_send, p1_recv, g_send, g_recv,
    pre_gate, pre_up, hidden_grad, gate_in, up_in, acts, hidden, term,
    pair, sib, x_first, x_last, y_first, y_last, y_sum, z_in, z_out, spread, rows_out, slots_out, back, back_f, term_f,
    sib_send, sib_recv, seen, total, half_out, half_in, n_send, n_recv, a_send, a_recv, x_send, x_recv, y_send, y_recv, z_send, z_recv, b_send, b_recv,
):
    bf16, f32 = jnp.bfloat16, jnp.float32
    nz = n_ts // NY
    nx = n_dp // 2
    me = lax.axis_index("ts")
    z, y = me // NY, lax.rem(me, NY)
    dp = lax.axis_index("dp")
    x, core = dp // 2, lax.rem(dp, 2)
    block, width = act_ref.shape
    tiles = width // LANES
    piece_rows = zy.shape[1]
    cap = n_ts * piece_rows
    hid = hidden.shape[1]
    pending = []

    def node(dz, dy):
        return lax.rem(z + dz + nz, nz) * NY + lax.rem(y + dy + NY, NY)

    def chip(dx):
        return lax.rem(x + dx + nx, nx) * 2 + core

    def copy_to(sems, index, src, dst, where):
        return pltpu.make_async_remote_copy(
            src, dst, sems[0].at[index], sems[1].at[index], device_id=where, device_id_type=MESH)

    def send(sems, index, src, dst, where):
        copy = copy_to(sems, index, src, dst, where)
        copy.start()
        pending.append(copy)

    def arrive(sems, index, dst):
        copy_to(sems, index, dst, dst, {"ts": me}).wait_recv()

    right, left = {"ts": node(0, 1)}, {"ts": node(0, -1)}
    up, down = {"ts": node(1, 0)}, {"ts": node(-1, 0)}
    ahead, behind = {"dp": chip(1)}, {"dp": chip(-1)}
    sibling = {"dp": x * 2 + 1 - core}

    barrier = pltpu.get_barrier_semaphore()

    @pl.loop(1, n_ts)
    def _(step):
        pl.semaphore_signal(barrier, inc=1, device_id={"ts": lax.rem(me + step, n_ts)}, device_id_type=MESH)

    for where in (sibling, ahead, behind, {"dp": chip(2)}):
        pl.semaphore_signal(barrier, inc=1, device_id=where, device_id_type=MESH)

    weight_copies = [
        pltpu.make_async_copy(src, dst, w_sem.at[i])
        for i, (src, dst) in enumerate(((switch_hbm, switch), (expand_hbm, expand), (contract_hbm, contract)))
    ]
    for copy in weight_copies:
        copy.start()

    kept = jnp.broadcast_to(kept_row[...], (block, cap))
    position = lax.broadcasted_iota(jnp.int32, (block, cap), 0) + block * me
    rank = jnp.sum((kept < position).astype(f32), axis=1, keepdims=True)
    routed = jnp.sum((kept == position).astype(f32), axis=1, keepdims=True)
    row_class = rank - n_ts * jnp.floor(rank * (1.0 / n_ts))
    classes = lax.broadcasted_iota(jnp.int32, (block, n_ts), 1).astype(f32)
    chosen = jnp.where(classes == row_class, routed, 0.0).astype(bf16)
    own[...] = dot(chosen, act_ref[...], ROWS_BY_ROWS)
    own_cot = dot(chosen, cot_ref[...], ROWS_BY_ROWS)
    for t in range(tiles):
        slots_f[:, t, :] = own[:, t * LANES:(t + 1) * LANES]
        slots_f[:, tiles + t, :] = own_cot[:, t * LANES:(t + 1) * LANES]

    @pl.loop(0, n_ts)
    def _(c):
        slots[c] = slots_f[c].astype(bf16)

    pl.semaphore_wait(barrier, n_ts - 1 + 4)


    def p1_copy(step):
        to = lax.rem(me + step, n_ts)
        return pltpu.make_async_remote_copy(
            slots.at[to], landed.at[me], p1_send.at[step], p1_recv.at[step],
            device_id={"ts": to}, device_id_type=MESH)

    @pl.loop(1, n_ts)
    def _(step):
        p1_copy(lax.rem(step + n_ts // 2 - 2, n_ts - 1) + 1).start()

    landed[me] = slots[me]

    gain = gain_ref[...].astype(f32).reshape(1, width)
    scorer = scorer_ref[...].astype(f32).reshape(1, width)
    own_f = own[...]
    own_inv = lax.rsqrt(jnp.sum(own_f * own_f, axis=1, keepdims=True) * (1.0 / width) + epsilon)
    own_weight = jax.nn.sigmoid(jnp.sum(own_f * scorer, axis=1, keepdims=True))
    own[...] = own_f * own_inv

    @pl.loop(0, n_ts)
    def _(h):
        pick = 0
        for k in range(1, piece_rows):
            pick = jnp.where(kept_ref[0, n_ts * k + me] // block == h, k, pick)
        picks[h] = pick

    @pl.loop(1, n_ts)
    def _(step):
        source = lax.rem(me - step + n_ts, n_ts)
        pltpu.make_async_remote_copy(
            slots.at[source], landed.at[source], p1_send.at[step], p1_recv.at[step],
            device_id={"ts": source}, device_id_type=MESH).wait_recv()


    for k in range(piece_rows):
        wide[k] = landed[kept_ref[0, n_ts * k + me] // block].astype(f32)
    for t in range(2 * tiles):
        piece_f[:, t * LANES:(t + 1) * LANES] = wide[:, t, :]

    row_f = piece_f[:, :width]
    inv_rms = lax.rsqrt(jnp.sum(row_f * row_f, axis=1, keepdims=True) * (1.0 / width) + epsilon)
    weight = jax.nn.sigmoid(jnp.sum(row_f * scorer, axis=1, keepdims=True))
    zy[me, :, :width] = (row_f * inv_rms * gain).astype(bf16)
    scaled_rows = (weight * piece_f[:, width:]).astype(bf16)
    yz[me] = scaled_rows[:, : yz.shape[2]]
    zy[me, :, width:] = scaled_rows[:, yz.shape[2] :]


    g_sems = (g_send, g_recv)

    def cut(buffer, which):
        first = -(-buffer.shape[2] // (2 * LANES)) * LANES
        return pl.ds(0, first) if which == 0 else pl.ds(first, buffer.shape[2] - first)

    def piece(buffer, n, which=None):
        return buffer.at[n] if which is None else buffer.at[n, :, cut(buffer, which)]

    def share(index, ref, where):
        send(g_sems, index, ref, ref, where)

    B1, A1, A2, A3, B2 = 0, 4, 12, 28, 44

    def b1_start():
        share(B1 + 0, piece(yz, me), right)
        share(B1 + 1, piece(yz, me), left)

    def b1_relay():
        arrive(g_sems, B1 + 0, piece(yz, node(0, -1)))
        share(B1 + 2, piece(yz, node(0, -1), 0), right)
        arrive(g_sems, B1 + 1, piece(yz, node(0, 1)))
        share(B1 + 3, piece(yz, node(0, 1), 1), left)

    def b1_end():
        arrive(g_sems, B1 + 2, piece(yz, node(0, -2), 0))
        arrive(g_sems, B1 + 3, piece(yz, node(0, 2), 1))

    def a1_start():
        share(A1 + 0, piece(zy, me), up)
        share(A1 + 1, piece(zy, me), down)
        show(0, 0)

    def fan_out(j):
        dz = Z_STEPS[j]
        share(A2 + 2 * j, piece(zy, node(dz, 0)), right)
        share(A2 + 2 * j + 1, piece(zy, node(dz, 0)), left)

    def relay(j):
        dz = Z_STEPS[j]
        arrive(g_sems, A2 + 2 * j, piece(zy, node(dz, -1)))
        share(A3 + 2 * j, piece(zy, node(dz, -1), 0), right)
        arrive(g_sems, A2 + 2 * j + 1, piece(zy, node(dz, 1)))
        share(A3 + 2 * j + 1, piece(zy, node(dz, 1), 1), left)
        show(dz, -1)
        show(dz, 1)

    def last(j):
        arrive(g_sems, A3 + 2 * j, piece(zy, node(Z_STEPS[j], -2), 0))
        arrive(g_sems, A3 + 2 * j + 1, piece(zy, node(Z_STEPS[j], 2), 1))
        show(Z_STEPS[j], 2)

    def along(s):
        which = (0, 1) if s == 4 else (None, None)
        further = (0, 1) if s == 3 else (None, None)
        for way, to, sign in ((0, up, -1), (1, down, 1)):
            arrive(g_sems, A1 + 2 * (s - 1) + way, piece(zy, node(sign * s, 0), which[way]))
            if s < 4:
                share(A1 + 2 * s + way, piece(zy, node(sign * s, 0), further[way]), to)
        if s < 4:
            fan_out(2 * s - 1)
            fan_out(2 * s)
            show(-s, 0)
            show(s, 0)
        else:
            fan_out(7)
            show(4, 0)

    def chain(k, s):
        dy, one_way = B_STEPS[k], k // 2
        for way, to, sign in ((0, up, -1), (1, down, 1)):
            if s == 4 and way != one_way:
                continue
            ref = piece(yz, node(sign * s, dy))
            if s > 0:
                arrive(g_sems, B2 + 8 * k + 2 * (s - 1) + way, ref)
            if s < 3 or (s == 3 and way == one_way):
                share(B2 + 8 * k + 2 * s + way, ref, to)

    pair_width = 2 * width // n_dp
    far = (1, -1, 2)

    def seen_copy(rel, index):
        n = node(rel // NY, lax.rem(rel, NY))
        at = pl.ds(pl.multiple_of(lax.rem(x + far[index] + nx, nx) * pair_width, LANES), pair_width)
        return pltpu.make_async_remote_copy(
            zy.at[n, :, at], seen.at[x, n], n_send.at[index * n_ts + rel], n_recv.at[index * n_ts + rel],
            device_id={"dp": chip(far[index])}, device_id_type=MESH)

    def show(dz, dy):
        for index in range(3):
            seen_copy(dz % nz * NY + dy % NY, index).start()

    def seen_end():
        @pl.loop(0, n_ts)
        def _(rel):
            n = node(rel // NY, lax.rem(rel, NY))
            for index in range(3):
                arrive((n_send, n_recv), index * n_ts + rel, seen.at[lax.rem(x - far[index] + nx, nx), n])
                seen_copy(rel, index).wait_send()

    def columns(buffer, start, size):
        return buffer[:, :, pl.ds(start, size)].reshape(cap, size)

    def pre():
        for copy in weight_copies:
            copy.wait()
        pre_gate[...] = jnp.zeros_like(pre_gate)
        pre_up[...] = jnp.zeros_like(pre_up)

        @pl.loop(0, width // K_TILE)
        def _(k):
            at = pl.ds(pl.multiple_of(k * K_TILE, K_TILE), K_TILE)
            normed = columns(zy, pl.multiple_of(k * K_TILE, K_TILE), K_TILE)
            pre_gate[...] += dot(normed, switch[:, at], COLS_BY_COLS)
            pre_up[...] += dot(normed, expand[:, at], COLS_BY_COLS)

    steps = dict(
        pre=pre,        b1_start=b1_start, b1_relay=b1_relay, b1_end=b1_end, a1_start=a1_start)
    for step in AG_ORDER:
        if isinstance(step, str):
            steps[step]()
        else:
            (fan_out, relay, last, along, chain)["frlac".index(step[0])](*step[1:])

    hidden_grad[...] = jnp.zeros_like(hidden_grad)
    for p in range(n_dp // 2):
        at = pl.ds(p * pair_width, pair_width)
        if p < n_dp // 2 - 1:
            scaled[:, at] = columns(yz, p * pair_width, pair_width)
        else:
            scaled[:, at] = columns(zy, width, pair_width)
        hidden_grad[...] += dot(scaled[:, at], contract[:, at], COLS_BY_COLS)

    @pl.loop(0, nz)
    def _(i):
        n = cap // nz
        at = pl.ds(pl.multiple_of(i * n, n), n)
        gelu_out, slope_out = gelu_pair(pre_gate[at, :])
        up_value, grad = pre_up[at, :], hidden_grad[at, :]
        hidden_value = (gelu_out * up_value).astype(bf16)
        hidden[at, :] = hidden_value
        gate_value = (grad * up_value * slope_out).astype(bf16)
        up_back = (grad * gelu_out).astype(bf16)
        gate_in[at, :] = gate_value
        up_in[at, :] = up_back
        acts[x, at, :hid] = gate_value
        acts[x, at, hid:] = up_back
        router = jnp.sum(hidden_value.astype(f32) * grad, axis=1, keepdims=True)
        term[i, :, :, width:] = jnp.broadcast_to(router, (n, LANES)).astype(bf16).reshape(NY, piece_rows, LANES)


    a_sems = (a_send, a_recv)
    halves = (pl.ds(0, cap // 2), pl.ds(cap // 2, cap // 2))
    rows = width // n_dp

    def part(dx, which):
        return acts.at[lax.rem(x + dx + nx, nx), halves[which]]

    def pass_on(index, ref, where):
        send(a_sems, index, ref, ref, where)

    def acts_start():
        pass_on(0, part(0, 0), ahead)
        pass_on(2, part(0, 1), behind)
        pass_on(1, part(0, 1), ahead)
        pass_on(3, part(0, 0), behind)

    def acts_relay():
        arrive(a_sems, 0, part(-1, 0))
        pass_on(4, part(-1, 0), ahead)
        arrive(a_sems, 2, part(1, 1))
        pass_on(5, part(1, 1), behind)

    def grow(dx):
        at = lax.rem(x + dx + nx, nx)
        total[...] += dot(seen[at].reshape(cap, pair_width), acts[at], ROWS_BY_ROWS)

    def grow_own():
        start = pl.multiple_of(x * pair_width, LANES)
        total[...] = dot(columns(zy, start, pair_width), acts[x], ROWS_BY_ROWS)

    def grow_near():
        arrive(a_sems, 1, part(-1, 1))
        grow(-1)
        arrive(a_sems, 3, part(1, 0))
        grow(1)

    def grow_far():
        arrive(a_sems, 4, part(2, 0))
        arrive(a_sems, 5, part(2, 1))
        grow(2)
        theirs = pl.ds(pl.multiple_of((1 - core) * rows, 16), rows)
        half_out[...] = (factor * total[theirs, :]).astype(bf16)
        send(a_sems, 6, half_out, half_in, sibling)

    def grow_end():
        arrive(a_sems, 6, half_in)
        here = pl.ds(pl.multiple_of(core * rows, 16), rows)
        value = factor * total[here, :] + half_in[...].astype(f32)
        gate_ref[...] = value[:, :hid].astype(bf16)
        up_ref[...] = value[:, hid:].astype(bf16)

    sib_sems, x_sems, y_sems = (sib_send, sib_recv), (x_send, x_recv), (y_send, y_recv)
    z_sems = (z_send, z_recv)
    quarter = hid // 4
    order = (2, 1, -1, 0)

    def partials(j):
        start = pl.multiple_of(lax.rem(x + order[j] + nx, nx) * pair_width, LANES)
        both = (factor * dot(hidden[...], scaled[:, pl.ds(start, pair_width)], ROWS_BY_ROWS)).astype(bf16)
        pair[j, 0] = both[:, :rows]
        pair[j, 1] = both[:, rows:]
        for q in range(4):
            at = pl.ds(q * quarter, quarter)
            send(sib_sems, 4 * j + q, pair.at[j, 1 - core, at], sib.at[j, at], sibling)

    def add(j, q, others, store):
        arrive(sib_sems, 4 * j + q, sib.at[j, pl.ds(q * quarter, quarter)])
        here = pl.ds(q * quarter, quarter)
        value = pair[j, core, here, :].astype(f32) + sib[j, here, :].astype(f32)
        for ref, start in others:
            value += ref[pl.ds(start, quarter), :].astype(f32)
        store(here, value.astype(bf16))

    def in_place(j):
        def store(here, value):
            sib[j, here, :] = value
        return store

    def chunk(ref, q):
        return ref.at[pl.ds(q * quarter, quarter)]

    def x_start():
        for q in (0, 2, 1, 3):
            add(0, q, (), in_place(0))
            way = q // 2
            send(x_sems, q, chunk(sib.at[0], q), x_first.at[way, pl.ds((q % 2) * quarter, quarter)],
                 (ahead, behind)[way])
        for q in range(2):
            add(1, 2 + q, (), in_place(1))
            send(x_sems, 4 + q, chunk(sib.at[1], 2 + q), chunk(x_last.at[0], 2 + q), ahead)
            add(2, q, (), in_place(2))
            send(x_sems, 6 + q, chunk(sib.at[2], q), chunk(x_last.at[1], q), behind)

    def x_second():
        for q in range(2):
            arrive(x_sems, q, x_first.at[0, pl.ds(q * quarter, quarter)])
            add(1, q, ((x_first.at[0], q * quarter),), in_place(1))
            send(x_sems, 8 + q, chunk(sib.at[1], q), chunk(x_last.at[0], q), ahead)
            arrive(x_sems, 2 + q, x_first.at[1, pl.ds(q * quarter, quarter)])
            add(2, 2 + q, ((x_first.at[1], q * quarter),), in_place(2))
            send(x_sems, 10 + q, chunk(sib.at[2], 2 + q), chunk(x_last.at[1], 2 + q), behind)

    def x_end():
        def store_out(here, value):
            down_ref[here, :] = value

        for q in (2, 3, 0, 1):
            for way in range(2):
                index = (8 + q, 6 + q)[way] if q < 2 else (2 + q, 8 + q)[way]
                arrive(x_sems, index, chunk(x_last.at[way], q))
            add(3, q, ((x_last.at[0], q * quarter), (x_last.at[1], q * quarter)), store_out)

    wide_row = y_sum.shape[2]
    middle = -(-wide_row // (2 * LANES)) * LANES
    cols = (pl.ds(0, middle), pl.ds(middle, wide_row - middle))

    def terms():
        @pl.loop(0, width // K_TILE)
        def _(k):
            at = pl.ds(pl.multiple_of(k * K_TILE, K_TILE), K_TILE)
            value = dot(gate_in[...], switch[:, at]) + dot(up_in[...], expand[:, at])
            term[:, :, :, at] = value.astype(bf16).reshape(nz, NY, piece_rows, K_TILE)

    def at_z(i):
        return lax.rem(z + i, nz)

    def at_y(dy):
        return lax.rem(y + dy + NY, NY)

    def y_start(i):
        opposite = term.at[at_z(i), at_y(2)]
        send(y_sems, 6 * i, opposite.at[:, cols[0]], y_first.at[i, :, cols[0]], right)
        send(y_sems, 6 * i + 1, opposite.at[:, cols[1]], y_first.at[i, :, cols[1]], left)
        send(y_sems, 6 * i + 2, term.at[at_z(i), at_y(1), :, cols[1]], y_last.at[0, i, :, cols[1]], right)
        send(y_sems, 6 * i + 3, term.at[at_z(i), at_y(-1), :, cols[0]], y_last.at[1, i, :, cols[0]], left)

    def y_second(i):
        for way, dy, to in ((0, 1, right), (1, -1, left)):
            arrive(y_sems, 6 * i + way, y_first.at[i, :, cols[way]])
            value = term[at_z(i), at_y(dy), :, cols[way]].astype(f32) + y_first[i, :, cols[way]].astype(f32)
            y_first[i, :, cols[way]] = value.astype(bf16)
            send(y_sems, 6 * i + 4 + way, y_first.at[i, :, cols[way]], y_last.at[way, i, :, cols[way]], to)

    def y_end(i):
        for way in range(2):
            arrive(y_sems, 6 * i + 2 + way, y_last.at[way, i, :, cols[1 - way]])
            arrive(y_sems, 6 * i + 4 + way, y_last.at[way, i, :, cols[way]])
        value = term[at_z(i), y].astype(f32) + y_last[0, i].astype(f32)
        y_sum[i] = (value + y_last[1, i].astype(f32)).astype(bf16)

    def z_first():
        for way, sign in ((0, 1), (1, -1)):
            send(z_sems, 4 * way, y_sum.at[4, :, cols[way]], z_in.at[way, 0, :, cols[way]], {"ts": node(2 * sign, 0)})
            send(z_sems, 4 * way + 1, y_sum.at[3 if way == 0 else 5], z_in.at[way, 1], {"ts": node(sign, 0)})

    def z_second():
        for way, sign in ((0, 1), (1, -1)):
            arrive(z_sems, 4 * way + 1, z_in.at[way, 1])
            arrive(z_sems, 4 * way, z_in.at[way, 0, :, cols[way]])
            mine = 2 if way == 0 else 6
            rest = cols[1 - way]
            z_out[way, :, rest] = (
                y_sum[mine, :, rest].astype(f32) + z_in[way, 1, :, rest].astype(f32)).astype(bf16)
            value = y_sum[mine, :, cols[way]].astype(f32) + z_in[way, 1, :, cols[way]].astype(f32)
            z_out[way, :, cols[way]] = (value + z_in[way, 0, :, cols[way]].astype(f32)).astype(bf16)
            send(z_sems, 4 * way + 2, z_out.at[way], z_in.at[way, 2], {"ts": node(2 * sign, 0)})

    def z_third():
        for way, sign in ((0, 1), (1, -1)):
            send(z_sems, 4 * way + 3, y_sum.at[1 if way == 0 else 7], z_in.at[way, 3], {"ts": node(sign, 0)})

    def back_copy(step):
        to = lax.rem(me + step, n_ts)
        return pltpu.make_async_remote_copy(
            slots_out.at[to], back.at[me], b_send.at[step], b_recv.at[step],
            device_id={"ts": to}, device_id_type=MESH)

    def z_end():
        for way in range(2):
            arrive(z_sems, 4 * way + 2, z_in.at[way, 2])
            arrive(z_sems, 4 * way + 3, z_in.at[way, 3])

    def back_start():
        z_end()
        spread[...] = jnp.zeros_like(spread)
        for t in range(wide_row // LANES):
            at = pl.ds(t * LANES, LANES)
            value = y_sum[0, :, at].astype(f32)
            for way in range(2):
                value += z_in[way, 2, :, at].astype(f32) + z_in[way, 3, :, at].astype(f32)
            spread[:, t, :] = value
        for k in range(piece_rows):
            rows_out[k] = spread[k].astype(bf16)

        @pl.loop(0, n_ts)
        def _(h):
            slots_out[h] = rows_out[picks[h]]

        @pl.loop(1, n_ts)
        def _(step):
            back_copy(lax.rem(step + n_ts // 2 - 2, n_ts - 1) + 1).start()

        back[me] = slots_out[me]

    def back_end():
        @pl.loop(1, n_ts)
        def _(step):
            source = lax.rem(me - step + n_ts, n_ts)
            pltpu.make_async_remote_copy(
                slots_out.at[source], back.at[source], b_send.at[step], b_recv.at[step],
                device_id={"ts": source}, device_id_type=MESH).wait_recv()
            back_copy(step).wait_send()

        @pl.loop(0, n_ts)
        def _(c):
            back_f[c] = back[c].astype(f32)

        for t in range(tiles):
            term_f[:, t * LANES:(t + 1) * LANES] = back_f[:, t, :]
        summed_dot = back_f[:, tiles, :][:, :1]
        unit = own[...]
        gained = term_f[...] * gain
        mean = jnp.sum(gained * unit, axis=1, keepdims=True) * (1.0 / width)
        row_grad = own_inv * (gained - unit * mean) + ((1.0 - own_weight) * summed_dot) * scorer
        token_ref[...] = dot(chosen, row_grad.astype(bf16)).astype(bf16)

    jobs = dict(
        acts_start=acts_start, acts_relay=acts_relay, grow_own=grow_own, grow_near=grow_near, grow_far=grow_far,
        grow_end=grow_end, x_start=x_start, x_second=x_second, x_end=x_end, terms=terms, z_first=z_first, z_second=z_second, z_third=z_third, z_end=z_end, back_start=back_start, back_end=back_end, seen_end=seen_end)
    for job in RS_ORDER:
        if isinstance(job, str):
            jobs[job]()
        else:
            (partials, y_start, y_second, y_end)["pyse".index(job[0])](job[1])

    @pl.loop(1, n_ts)
    def _(step):
        p1_copy(step).wait_send()

    for copy in pending:
        copy.wait_send()


def store_kernel(*refs):
    count = (len(refs) - 2) // 3
    sems = refs[-2:]
    inward = [pltpu.make_async_copy(refs[i], refs[2 * count + i], sems[0].at[i]) for i in range(count)]
    outward = [pltpu.make_async_copy(refs[2 * count + i], refs[count + i], sems[1].at[i]) for i in range(count)]
    for copy in inward:
        copy.start()
    for first, second in zip(inward, outward):
        first.wait()
        second.start()
    for copy in outward:
        copy.wait()


def store_results(*results):
    hbm = pl.BlockSpec(memory_space=pl.ANY)
    return pl.pallas_call(
        store_kernel,
        out_shape=tuple(jax.ShapeDtypeStruct(r.shape, r.dtype) for r in results),
        in_specs=[hbm] * len(results),
        out_specs=(hbm,) * len(results),
        scratch_shapes=[pltpu.VMEM(r.shape, r.dtype) for r in results]
        + [pltpu.SemaphoreType.DMA((len(results),))] * 2,
        name="store_results",
    )(*results)


def local(
    block_activity, result_cotangent, kept_locations, prenormal_scaling, scorer_matrix,
    switch_matrix, expand_matrix, contract_matrix,
):
    n_ts, n_dp = lax.axis_size("ts"), lax.axis_size("dp")
    nz = n_ts // NY
    block, width = block_activity.shape[1:]
    cap = kept_locations.shape[1]
    hid = switch_matrix.shape[1]
    rows = width // n_dp
    piece = cap // n_ts
    tiles = width // LANES
    pad = -(-(tiles + 1) // 16) * 16
    bf16, f32, dma = jnp.bfloat16, jnp.float32, pltpu.SemaphoreType.DMA
    vmem = pl.BlockSpec(memory_space=pltpu.VMEM)
    hbm = pl.BlockSpec(memory_space=pl.ANY)
    token, gate, up, down = pl.pallas_call(
        functools.partial(block_kernel, n_ts, n_dp, (n_dp * cap) ** (-0.5)),
        out_shape=(
            jax.ShapeDtypeStruct((block, width), bf16),
            jax.ShapeDtypeStruct((rows, hid), bf16),
            jax.ShapeDtypeStruct((rows, hid), bf16),
            jax.ShapeDtypeStruct((hid, rows), bf16),
        ),
        in_specs=[pl.BlockSpec(memory_space=pltpu.SMEM)] + [vmem] * 5 + [hbm] * 3,
        out_specs=(vmem,) * 4,
        scratch_shapes=[
            pltpu.VMEM((hid, width), bf16), pltpu.VMEM((hid, width), bf16), pltpu.VMEM((hid, width), bf16), dma((3,)),
            pltpu.SMEM((n_ts,), jnp.int32),
            pltpu.VMEM((n_ts, width), f32),
            pltpu.VMEM((n_ts, 2 * tiles, LANES), f32),
            pltpu.VMEM((n_ts, 2 * tiles, LANES), bf16),
            pltpu.VMEM((n_ts, 2 * tiles, LANES), bf16),
            pltpu.VMEM((piece, 2 * tiles, LANES), f32),
            pltpu.VMEM((piece, 2 * width), f32),
            pltpu.VMEM((n_ts, piece, width + 2 * rows), bf16),
            pltpu.VMEM((n_ts, piece, width - 2 * rows), bf16),
            pltpu.VMEM((cap, width), bf16),
            dma((n_ts,)), dma((n_ts,)), dma((76,)), dma((76,)),
            pltpu.VMEM((cap, hid), f32), pltpu.VMEM((cap, hid), f32), pltpu.VMEM((cap, hid), f32),
            pltpu.VMEM((cap, hid), bf16), pltpu.VMEM((cap, hid), bf16), pltpu.VMEM((n_dp // 2, cap, 2 * hid), bf16),
            pltpu.VMEM((cap, hid), bf16),
            pltpu.VMEM((nz, NY, piece, width + LANES), bf16),
            pltpu.VMEM((4, 2, hid, rows), bf16),
            pltpu.VMEM((4, hid, rows), bf16),
            pltpu.VMEM((2, hid // 2, rows), bf16),
            pltpu.VMEM((2, hid, rows), bf16),
            pltpu.VMEM((nz, piece, width + LANES), bf16),
            pltpu.VMEM((2, nz, piece, width + LANES), bf16),
            pltpu.VMEM((nz, piece, width + LANES), bf16),
            pltpu.VMEM((2, 4, piece, width + LANES), bf16),
            pltpu.VMEM((2, piece, width + LANES), bf16),
            pltpu.VMEM((piece, pad, LANES), f32),
            pltpu.VMEM((piece, pad, LANES), bf16),
            pltpu.VMEM((n_ts, pad, LANES), bf16),
            pltpu.VMEM((n_ts, pad, LANES), bf16),
            pltpu.VMEM((n_ts, pad, LANES), f32),
            pltpu.VMEM((n_ts, width), f32),
            dma((16,)), dma((16,)),
            pltpu.VMEM((n_dp // 2, n_ts, piece, 2 * rows), bf16),
            pltpu.VMEM((2 * rows, 2 * hid), f32),
            pltpu.VMEM((rows, 2 * hid), bf16),
            pltpu.VMEM((rows, 2 * hid), bf16),
            dma((3 * n_ts,)), dma((3 * n_ts,)), dma((7,)), dma((7,)),
            dma((12,)), dma((12,)), dma((6 * nz,)), dma((6 * nz,)),
            dma((8,)), dma((8,)), dma((n_ts,)), dma((n_ts,)),
        ],
        compiler_params=pltpu.CompilerParams(
            collective_id=0, has_side_effects=True, vmem_limit_bytes=56 * 1024 * 1024),
        name="block_backward",
    )(
        kept_locations, kept_locations, block_activity[0], result_cotangent[0],
        prenormal_scaling, scorer_matrix, switch_matrix.T, expand_matrix.T, contract_matrix,
    )
    return store_results(token[None], gate, up, down)


def solution(mesh):
    in_specs = (
        P("dp", "ts", None), P("dp", "ts", None), P("dp", None), P(), P(),
        P(None, "ts"), P(None, "ts"), P("ts", None),
    )
    out_specs = (P("dp", "ts", None), P("dp", "ts"), P("dp", "ts"), P("ts", "dp"))
    return jax.shard_map(local, mesh=mesh, in_specs=in_specs, out_specs=out_specs, check_vma=False)
```
